32 devices in a mesh: rad: 8 (over z, x), az: 4 (over y, core).
Axes of the slice: x: 2, y: 2, z: 4, core: 2. Of those that a mesh axis runs over, the one named last changes fastest.
Arguments:
- state: float32 [6, 2, 256, 4096], P(None, None, 'rad', 'az'), may hold values from -4 to 4, as said below
- offsets: int32 [256], P('rad'), may hold values from 0 to 4095
- viscosity: float32 [2, 256, 4096], P(None, 'rad', 'az'), may hold values from 0.02 to 0.2
- absorb: float32 [2, 256, 4096], P(None, 'rad', 'az'), may hold values from 0.5 to 8
Outputs:
- new_state: float32 [6, 2, 256, 4096], P(None, None, 'rad', 'az')
- depth: float32 [2, 256, 4096], P(None, 'rad', 'az')
The draws below stay inside these ranges and needn't reach their ends.
Inputs may be any that keep to these rules, and one draw needn't show every extreme that they name: state[0] lies in 0.5 to 2, state[1], state[2], state[3] in -4 to 4, state[4] in 1 to 3, state[5] in 0.1 to 1.
All inputs are finite; a program needn't handle non-finite values.
Results may differ from the reference program's by a relative error of at most 0.00002.
Values sent between devices are 32-bit elements; how exact they have to be, the bound alone decides.
A program may use at most 128 MiB of HBM per device.

```python
import math
import jax
import jax.numpy as jnp
from jax import lax

P_SIZE = 2
NR = 256
NA = 4096


def draw_state(key, part):
    keys = jax.random.split(jax.random.fold_in(key, 11), 4)
    shape = (P_SIZE, NR, NA)
    density = jax.random.uniform(keys[0], shape, jnp.float32, 0.5, 2.0)
    energy = jax.random.uniform(keys[2], shape, jnp.float32, 1.0, 3.0)
    momenta = jnp.clip(jax.random.normal(keys[1], (3,) + shape, jnp.float32), -4.0, 4.0)
    dust = jnp.exp(jax.random.uniform(keys[3], shape, jnp.float32, math.log(0.1), 0.0))
    return jnp.concatenate([density[None], momenta, energy[None], dust[None]], axis=0)


def set_ends(result, rng, least, high):
    spot = [jax.random.randint(jax.random.fold_in(rng, axis), (), 0, length) for axis, length in enumerate(result.shape)]
    widest = result.shape.index(max(result.shape))
    next_to = spot[:widest] + [(spot[widest] + 1) % result.shape[widest]] + spot[widest + 1:]
    return result.at[tuple(spot)].set(least).at[tuple(next_to)].set(high)


def levels(rng, extent, cuts, low, top_value):
    def one(position, shards_of):
        heights = jax.random.uniform(jax.random.fold_in(jax.random.fold_in(rng, 6), position), (shards_of,), jnp.float32, low / len(cuts), top_value / len(cuts))
        return jnp.repeat(jnp.exp(heights), extent[position] // shards_of).reshape((-1,) + (1,) * (len(extent) - position - 1))

    factor_of = one(*cuts[0])
    for cut in cuts[1:]:
        factor_of = factor_of * one(*cut)
    return factor_of


def setup_inputs(seed: int = 0) -> dict:
    key_of = jax.random.split(jax.random.key(seed), 5)
    state = draw_state(jax.random.fold_in(key_of[4], 71), 0)
    offsets = set_ends(jax.random.randint(key_of[1], (NR,), 0, NA), jax.random.fold_in(key_of[1], 1), 0, NA - 1).astype(jnp.int32)
    viscosity = jnp.clip(jnp.exp(math.log(0.2) - 2.3025851 * jax.random.uniform(key_of[2], (P_SIZE, NR, NA), jnp.float32) ** levels(key_of[2], (P_SIZE, NR, NA), ((1, 8), (2, 4)), -0.2, 0.2)), 0.02, 0.2)
    absorb = jnp.clip(jnp.exp(math.log(8.0) - 2.7725887 * jax.random.uniform(key_of[3], (P_SIZE, NR, NA), jnp.float32) ** levels(key_of[3], (P_SIZE, NR, NA), ((1, 8), (2, 4)), -0.2, 0.2)), 0.5, 8.0)
    return {"state": state, "offsets": offsets, "viscosity": viscosity, "absorb": absorb}


AZIMUTH_COEF = 0.1


def roll_annulus(pair):
    return jnp.roll(pair[0], pair[1], axis=-1)


def reference(state, offsets, viscosity, absorb):
    annuli = jnp.moveaxis(state, 2, 0)
    shifted = lax.map(roll_annulus, (annuli, offsets))
    shifted = jnp.moveaxis(shifted, 0, 2)
    radial_pad = jnp.pad(shifted, ((0, 0), (0, 0), (1, 1), (0, 0)))
    radial_term = radial_pad[:, :, 2:] + radial_pad[:, :, :-2] - 2.0 * shifted
    azimuth_term = jnp.roll(shifted, 1, axis=3) + jnp.roll(shifted, -1, axis=3) - 2.0 * shifted
    smoothed = shifted + viscosity[None] * radial_term + AZIMUTH_COEF * azimuth_term
    depth_step = 2.0 * absorb * smoothed[5] / NR
    depth = jnp.cumsum(depth_step, axis=1) - 0.5 * depth_step
    radius = jnp.arange(NR).astype(jnp.float32) + 0.5
    stellar_flux = 1.0 / (1.0 + radius / NR)
    energy = smoothed[4] + stellar_flux[None, :, None] * jnp.exp(-depth)
    new_state = jnp.concatenate([smoothed[:4], energy[None], smoothed[5:]], axis=0)
    return new_state, depth
```

```python
import functools

import jax
import jax.numpy as jnp
from jax import lax
from jax.experimental import pallas as pl
from jax.experimental.pallas import tpu as pltpu
from jax.sharding import PartitionSpec as P

AZIMUTH_COEF = 0.1
LANES = 128
SUB = 8


def tail_planes(rest):
    cuts = [0, rest // 2, rest]
    return [(a, b - a) for a, b in zip(cuts, cuts[1:]) if b > a]


def kernel(n_rad, n_az, n_local, source, offs, visc_in, absorb_in, out, depth,
           visc, absorb, heat, state, buf, sh, eo, ei, tot_out, tot_in, ss, rs, ls):
    groups = n_az // 2
    rad = lax.axis_index("rad")
    az = lax.axis_index("az")
    core = lax.rem(az, 2)
    sibling = {"az": az + 1 - 2 * core}
    planes, rows, width = state.shape
    cols = width // LANES
    tiles = rows // SUB
    dust = planes - 2
    rest = dust
    total_rows = rows * n_rad

    def rad_at(k):
        return {"rad": lax.rem(rad + k + n_rad, n_rad)}

    def az_at(k):
        return {"az": lax.rem(az + 2 * k, n_az)}

    count = [0]

    def remote(src, dst, device):
        i = count[0]
        count[0] += 1
        return pltpu.make_async_remote_copy(
            src_ref=src, dst_ref=dst, send_sem=ss.at[i], recv_sem=rs.at[i],
            device_id=device, device_id_type=pl.DeviceIdType.MESH,
        )

    fetch = pltpu.make_async_copy(source, state, ls.at[0])
    fetches = [fetch] + [
        pltpu.make_async_copy(a, b, ls.at[n_local + i])
        for i, (a, b) in enumerate(((visc_in, visc), (absorb_in, absorb)))
    ]
    inner, outer = rad > 0, rad < n_rad - 1
    ei[...] = jnp.zeros_like(ei)
    tot_in[...] = jnp.zeros_like(tot_in)
    peers = [az_at(k) for k in range(1, groups)] + [sibling]
    barrier = pltpu.get_barrier_semaphore()
    for there, k in ((inner, -1), (outer, 1)):
        @pl.when(there)
        def _():
            pl.semaphore_signal(barrier, inc=1, device_id=rad_at(k), device_id_type=pl.DeviceIdType.MESH)
    for peer in peers:
        pl.semaphore_signal(barrier, inc=1, device_id=peer, device_id_type=pl.DeviceIdType.MESH)
    senders = len(peers)
    d = 1
    while d < n_rad:
        if d > 1:
            @pl.when(rad >= d)
            def _():
                pl.semaphore_signal(barrier, inc=1, device_id=rad_at(-d), device_id_type=pl.DeviceIdType.MESH)
            senders = senders + (rad + d < n_rad).astype(jnp.int32)
        d *= 2
    pl.semaphore_wait(barrier, senders + inner.astype(jnp.int32) + outer.astype(jnp.int32))

    pieces = [(dust, 2, 0, rows)]
    edge_tiles = [0, tiles - 1]
    for t in edge_tiles + list(range(1, tiles - 2)):
        pieces.append((0, rest, t * SUB, SUB))
    tail = tail_planes(rest)
    for p0, np_ in tail:
        pieces.append((p0, np_, (tiles - 2) * SUB, SUB))

    sent, chained = [], []
    across, beside = [], []
    for p0, np_, r0, nr in pieces:
        ps, rws = pl.ds(p0, np_), pl.ds(r0, nr)
        across.append([remote(source.at[ps, rws], buf.at[2 * k - 1, ps, rws], az_at(k)) for k in range(1, groups)])
        beside.append(remote(source.at[ps, rws], buf.at[0, ps, rws], sibling))
        for c in across[-1]:
            c.start()
            sent.append(c)
    for c in beside:
        c.start()
        sent.append(c)

    def arrive(i):
        p0, np_, r0, nr = pieces[i]
        ps, rws = pl.ds(p0, np_), pl.ds(r0, nr)
        forwards = []
        for k in range(1, groups):
            across[i][k - 1].wait_recv()
            f = remote(buf.at[2 * k - 1, ps, rws], buf.at[2 * k, ps, rws], sibling)
            f.start()
            sent.append(f)
            forwards.append(f)
        beside[i].wait_recv()
        for f in forwards:
            f.wait_recv()

    lane = lax.broadcasted_iota(jnp.int32, (SUB, LANES), 1)

    def shift_tile(tile, p0, np_):
        r = pl.ds(tile * SUB, SUB)
        sub = lax.broadcasted_iota(jnp.int32, (SUB, LANES), 0)
        amount = jnp.full((SUB, LANES), offs[tile * SUB], jnp.int32)
        for k in range(1, SUB):
            amount = jnp.where(sub == k, offs[tile * SUB + k], amount)
        block = amount // width
        within = amount - block * width
        column = within // LANES
        rem = within - column * LANES
        pick = (lane - rem) & (LANES - 1)
        low = lane < rem

        def one(p, carry):
            def load(d, c):
                cs = pl.ds(c * LANES, LANES)
                if d == 0:
                    return state[p, r, cs]
                if d % 2 == 0:
                    return buf[d - 1, p, r, cs]
                slot = jnp.where(core == 1, d, (d + 2) % n_az)
                return buf[slot - 1, p, r, cs]

            line = []
            for move, c in [(1, c) for c in range(cols)] + [(0, c) for c in range(cols)] + [(-1, 0)]:
                value = load(move % n_az, c)
                for b in range(1, n_az):
                    value = jnp.where(block == b, load((b + move) % n_az, c), value)
                line.append(value)
            step = cols // 2
            while step:
                chosen = (column & step) != 0
                line = [jnp.where(chosen, line[i - step], line[i]) for i in range(step, len(line))]
                step //= 2
            turned = [jnp.take_along_axis(v, pick, axis=1, mode="promise_in_bounds") for v in line]
            x = [turned[0]] + [jnp.where(low, turned[j - 1], turned[j]) for j in range(1, len(turned))]
            right = [pltpu.roll(v, 1, 1) for v in x[:-1]]
            left = [pltpu.roll(v, LANES - 1, 1) for v in x[1:]]
            for c in range(cols):
                cs = pl.ds(c * LANES, LANES)
                mid = x[c + 1]
                prev = jnp.where(lane == 0, right[c], right[c + 1])
                nxt = jnp.where(lane == LANES - 1, left[c + 1], left[c])
                sh[p, pl.ds(SUB + tile * SUB, SUB), cs] = mid
                out[p, r, cs] = mid + AZIMUTH_COEF * (nxt + prev - 2.0 * mid)
                if tile == 0:
                    eo[0, p, :, cs] = mid[:1]
                if tile == tiles - 1:
                    eo[1, p, :, cs] = mid[SUB - 1:]
            return carry

        lax.fori_loop(p0, p0 + np_, one, 0)

    hops = []

    def scan_send():
        i = len(hops)
        d = 1 << i
        if d < n_rad:
            c = remote(tot_out.at[i], tot_in.at[i], rad_at(d))
            goes = rad + d < n_rad
            pl.when(goes)(c.start)
            chained.append((goes, c))
            hops.append(c)

    def scan_take():
        i = len(hops) - 1
        pl.when(rad >= 1 << i)(hops[i].wait_recv)
        tot_out[i + 1] = tot_out[i] + tot_in[i]

    def send_edge(side, p0, np_):
        ps = pl.ds(p0, np_)
        c = remote(eo.at[side, ps], ei.at[1 - side, ps], rad_at(-1 if side == 0 else 1))
        goes, comes = (inner, outer) if side == 0 else (outer, inner)
        pl.when(goes)(c.start)
        chained.append((goes, c))
        return comes, c

    def edge_wait(edge):
        pl.when(edge[0])(edge[1].wait_recv)

    def place_edges(p0, np_):
        def one(p, carry):
            sh[p, SUB - 1:SUB, :] = jnp.where(rad > 0, ei[0, p], 0.0)
            sh[p, SUB + rows:SUB + rows + 1, :] = jnp.where(rad < n_rad - 1, ei[1, p], 0.0)
            return carry

        lax.fori_loop(p0, p0 + np_, one, 0)

    def smooth(tile, p0, np_):
        top = SUB + tile * SUB

        def one(p, carry):
            r = pl.ds(tile * SUB, SUB)
            mid = sh[p, top:top + SUB, :]
            up = sh[p, top - 1:top + SUB - 1, :]
            down = sh[p, top + 1:top + SUB + 1, :]
            out[p, r, :] = out[p, r, :] + visc[lax.rem(p, 2), r, :] * (down + up - 2.0 * mid)
            return carry

        lax.fori_loop(p0, p0 + np_, one, 0)

    for c in fetches:
        c.start()
    arrive(0)
    for c in fetches:
        c.wait()
    for t in range(tiles):
        shift_tile(t, dust, 2)
    edges = [send_edge(s, dust, 2) for s in (0, 1)]
    for e in edges:
        edge_wait(e)
    place_edges(dust, 2)
    for t in range(tiles):
        smooth(t, dust, 2)

    row = lax.broadcasted_iota(jnp.int32, (SUB, width), 0)
    for h in range(2):
        base = jnp.zeros((1, width), jnp.float32)
        for t in range(tiles):
            r = pl.ds(t * SUB, SUB)
            step = 2.0 * absorb[h, r, :] * out[dust + h, r, :] / total_rows
            run = step
            for k in (1, 2, 4):
                run = run + jnp.where(row >= k, pltpu.roll(run, k, 0), 0.0)
            run = run + base
            depth[h, r, :] = run - 0.5 * step
            base = run[SUB - 1:]
        tot_out[0, h] = base
    scan_send()
    arrive(1)
    shift_tile(0, 0, rest)
    edge_in = send_edge(0, 0, rest)
    scan_take()
    scan_send()
    arrive(2)
    shift_tile(tiles - 1, 0, rest)
    edge_out = send_edge(1, 0, rest)

    scan_take()
    while 1 << len(hops) < n_rad:
        scan_send()
        scan_take()
    for h in range(2):
        carried = tot_in[0, h]
        for i in range(1, len(hops)):
            carried = carried + tot_in[i, h]
        for t in range(tiles):
            r = pl.ds(t * SUB, SUB)
            radius = (rad * rows + t * SUB + row).astype(jnp.float32) + 0.5
            flux = 1.0 / (1.0 + radius / total_rows)
            depth[h, r, :] = depth[h, r, :] + carried
            heat[h, r, :] = flux * jnp.exp(-depth[h, r, :])

    def warm(tile):
        r = pl.ds(tile * SUB, SUB)
        for h in range(2):
            out[rest - 2 + h, r, :] = out[rest - 2 + h, r, :] + heat[h, r, :]

    edge_wait(edge_in)
    edge_wait(edge_out)
    place_edges(0, rest)
    i = 3
    for t in range(1, tiles - 2):
        arrive(i)
        shift_tile(t, 0, rest)
        smooth(t - 1, 0, rest)
        warm(t - 1)
        i += 1
    first = max(tiles - 3, 0)
    for p0, np_ in tail:
        arrive(i)
        shift_tile(tiles - 2, p0, np_)
        for t in range(first, tiles):
            smooth(t, p0, np_)
            if p0 + np_ == rest:
                warm(t)
        i += 1
    for goes, c in chained:
        pl.when(goes)(c.wait_send)
    for c in sent:
        c.wait_send()


def body(n_rad, n_az, state, offsets, viscosity, absorb):
    fields, polar, rows, width = state.shape
    planes = fields * polar
    groups = n_az // 2
    tiles = rows // SUB
    n_tail = len(tail_planes(planes - 2))
    n_pieces = 1 + 2 + max(tiles - 3, 0) + n_tail
    n_scan = (n_rad - 1).bit_length()
    n_local = 1
    n_sems = n_pieces * (2 * (groups - 1) + 1) + 4 + n_scan
    f32 = jnp.float32
    vm = pl.BlockSpec(memory_space=pltpu.VMEM)
    hbm = pl.BlockSpec(memory_space=pl.ANY)
    moved, local = pl.pallas_call(
        functools.partial(kernel, n_rad, n_az, n_local),
        out_shape=(
            pltpu.VMEM((planes, rows, width), f32),
            pltpu.VMEM((polar, rows, width), f32),
        ),
        in_specs=[hbm, pl.BlockSpec(memory_space=pltpu.SMEM), hbm, hbm],
        out_specs=(vm, vm),
        scratch_shapes=[
            pltpu.VMEM((polar, rows, width), f32),
            pltpu.VMEM((polar, rows, width), f32),
            pltpu.VMEM((polar, rows, width), f32),
            pltpu.VMEM((planes, rows, width), f32),
            pltpu.VMEM((n_az - 1, planes, rows, width), f32),
            pltpu.VMEM((planes, rows + 2 * SUB, width), f32),
            pltpu.VMEM((2, planes, 1, width), f32),
            pltpu.VMEM((2, planes, 1, width), f32),
            pltpu.VMEM((n_scan + 1, polar, 1, width), f32),
            pltpu.VMEM((n_scan, polar, 1, width), f32),
            pltpu.SemaphoreType.DMA((n_sems,)),
            pltpu.SemaphoreType.DMA((n_sems,)),
            pltpu.SemaphoreType.DMA((n_local + 2,)),
        ],
        compiler_params=pltpu.CompilerParams(
            collective_id=0, has_side_effects=True, vmem_limit_bytes=56 * 2**20
        ),
    )(state.reshape(planes, rows, width), offsets, viscosity, absorb)
    moved = moved.reshape(state.shape)
    return moved, local


def solution(mesh):
    in_specs = (P(None, None, "rad", "az"), P("rad"), P(None, "rad", "az"), P(None, "rad", "az"))
    out_specs = (P(None, None, "rad", "az"), P(None, "rad", "az"))
    f = functools.partial(body, mesh.shape["rad"], mesh.shape["az"])
    return jax.shard_map(f, mesh=mesh, in_specs=in_specs, out_specs=out_specs, check_vma=False)
```

```python
import functools

import jax
import jax.numpy as jnp
from jax import lax
from jax.experimental import pallas as pl
from jax.experimental.pallas import tpu as pltpu
from jax.sharding import PartitionSpec as P

AZIMUTH_COEF = 0.1
LANES = 128
SUB = 8
LANE_BITS = 7
SUB_BITS = 3


def tail_planes(rest):
    cuts = [0, rest // 2, rest]
    return [(a, b - a) for a, b in zip(cuts, cuts[1:]) if b > a]


def kernel(n_rad, n_az, n_local, source, offs, visc_in, absorb_in, out, depth,
           visc, absorb, heat, state, buf, sh, eo, ei, tot_out, tot_in, ss, rs, ls):
    groups = n_az // 2
    rad = lax.axis_index("rad")
    az = lax.axis_index("az")
    core = lax.rem(az, 2)
    sibling = {"az": az + 1 - 2 * core}
    planes, rows, width = state.shape
    cols = width // LANES
    tiles = rows // SUB
    dust = planes - 2
    rest = dust
    total_rows = rows * n_rad

    def rad_at(k):
        return {"rad": lax.rem(rad + k + n_rad, n_rad)}

    def az_at(k):
        return {"az": lax.rem(az + 2 * k, n_az)}

    count = [0]

    def remote(src, dst, device):
        i = count[0]
        count[0] += 1
        return pltpu.make_async_remote_copy(
            src_ref=src, dst_ref=dst, send_sem=ss.at[i], recv_sem=rs.at[i],
            device_id=device, device_id_type=pl.DeviceIdType.MESH,
        )

    fetch = pltpu.make_async_copy(source, state, ls.at[0])
    fetches = [fetch] + [
        pltpu.make_async_copy(a, b, ls.at[n_local + i])
        for i, (a, b) in enumerate(((visc_in, visc), (absorb_in, absorb)))
    ]
    inner, outer = rad > 0, rad < n_rad - 1
    ei[...] = jnp.zeros_like(ei)
    tot_in[...] = jnp.zeros_like(tot_in)
    peers = [az_at(k) for k in range(1, groups)] + [sibling]
    barrier = pltpu.get_barrier_semaphore()
    for there, k in ((inner, -1), (outer, 1)):
        @pl.when(there)
        def _():
            pl.semaphore_signal(barrier, inc=1, device_id=rad_at(k), device_id_type=pl.DeviceIdType.MESH)
    for peer in peers:
        pl.semaphore_signal(barrier, inc=1, device_id=peer, device_id_type=pl.DeviceIdType.MESH)
    senders = len(peers)
    d = 1
    while d < n_rad:
        if d > 1:
            @pl.when(rad >= d)
            def _():
                pl.semaphore_signal(barrier, inc=1, device_id=rad_at(-d), device_id_type=pl.DeviceIdType.MESH)
            senders = senders + (rad + d < n_rad).astype(jnp.int32)
        d *= 2
    pl.semaphore_wait(barrier, senders + inner.astype(jnp.int32) + outer.astype(jnp.int32))

    pieces = [(dust, 2, 0, rows)]
    edge_tiles = [0, tiles - 1]
    for t in edge_tiles + list(range(1, tiles - 2)):
        pieces.append((0, rest, t * SUB, SUB))
    tail = tail_planes(rest)
    for p0, np_ in tail:
        pieces.append((p0, np_, (tiles - 2) * SUB, SUB))

    sent, chained = [], []
    across, beside = [], []
    for p0, np_, r0, nr in pieces:
        ps, rws = pl.ds(p0, np_), pl.ds(r0, nr)
        across.append([remote(source.at[ps, rws], buf.at[2 * k - 1, ps, rws], az_at(k)) for k in range(1, groups)])
        beside.append(remote(source.at[ps, rws], buf.at[0, ps, rws], sibling))
        for c in across[-1]:
            c.start()
            sent.append(c)
    for c in beside:
        c.start()
        sent.append(c)

    def arrive(i):
        p0, np_, r0, nr = pieces[i]
        ps, rws = pl.ds(p0, np_), pl.ds(r0, nr)
        forwards = []
        for k in range(1, groups):
            across[i][k - 1].wait_recv()
            f = remote(buf.at[2 * k - 1, ps, rws], buf.at[2 * k, ps, rws], sibling)
            f.start()
            sent.append(f)
            forwards.append(f)
        beside[i].wait_recv()
        for f in forwards:
            f.wait_recv()

    lane = lax.broadcasted_iota(jnp.int32, (SUB, LANES), 1)

    def shift_tile(tile, p0, np_):
        r = pl.ds(tile * SUB, SUB)
        sub = lax.broadcasted_iota(jnp.int32, (SUB, LANES), 0)
        amount = jnp.full((SUB, LANES), offs[tile * SUB], jnp.int32)
        for k in range(1, SUB):
            amount = jnp.where(sub == k, offs[tile * SUB + k], amount)
        block = amount // width
        within = amount - block * width
        column = within // LANES
        rem = within - column * LANES
        pick = (lane - rem) & (LANES - 1)
        low = lane < rem

        def one(p, carry):
            def load(d, c):
                cs = pl.ds(c * LANES, LANES)
                if d == 0:
                    return state[p, r, cs]
                if d % 2 == 0:
                    return buf[d - 1, p, r, cs]
                slot = jnp.where(core == 1, d, (d + 2) % n_az)
                return buf[slot - 1, p, r, cs]

            line = []
            for move, c in [(1, c) for c in range(cols)] + [(0, c) for c in range(cols)] + [(-1, 0)]:
                value = load(move % n_az, c)
                for b in range(1, n_az):
                    value = jnp.where(block == b, load((b + move) % n_az, c), value)
                line.append(value)
            step = cols // 2
            while step:
                chosen = (column & step) != 0
                line = [jnp.where(chosen, line[i - step], line[i]) for i in range(step, len(line))]
                step //= 2
            turned = [jnp.take_along_axis(v, pick, axis=1, mode="promise_in_bounds") for v in line]
            x = [turned[0]] + [jnp.where(low, turned[j - 1], turned[j]) for j in range(1, len(turned))]
            right = [pltpu.roll(v, 1, 1) for v in x[:-1]]
            left = [pltpu.roll(v, LANES - 1, 1) for v in x[1:]]
            for c in range(cols):
                cs = pl.ds(c * LANES, LANES)
                mid = x[c + 1]
                prev = jnp.where(lane == 0, right[c], right[c + 1])
                nxt = jnp.where(lane == LANES - 1, left[c + 1], left[c])
                sh[p, pl.ds(SUB + tile * SUB, SUB), cs] = mid
                out[p, r, cs] = mid + AZIMUTH_COEF * (nxt + prev - 2.0 * mid)
                if tile == 0:
                    eo[0, p, :, cs] = mid[:1]
                if tile == tiles - 1:
                    eo[1, p, :, cs] = mid[SUB - 1:]
            return carry

        lax.fori_loop(p0, p0 + np_, one, 0)

    hops = []

    def scan_send():
        i = len(hops)
        d = 1 << i
        if d < n_rad:
            c = remote(tot_out.at[i], tot_in.at[i], rad_at(d))
            goes = rad + d < n_rad
            pl.when(goes)(c.start)
            chained.append((goes, c))
            hops.append(c)

    def scan_take():
        i = len(hops) - 1
        pl.when(rad >= 1 << i)(hops[i].wait_recv)
        tot_out[i + 1] = tot_out[i] + tot_in[i]

    def send_edge(side, p0, np_):
        ps = pl.ds(p0, np_)
        c = remote(eo.at[side, ps], ei.at[1 - side, ps], rad_at(-1 if side == 0 else 1))
        goes, comes = (inner, outer) if side == 0 else (outer, inner)
        pl.when(goes)(c.start)
        chained.append((goes, c))
        return comes, c

    def edge_wait(edge):
        pl.when(edge[0])(edge[1].wait_recv)

    def place_edges(p0, np_):
        def one(p, carry):
            sh[p, SUB - 1:SUB, :] = jnp.where(rad > 0, ei[0, p], 0.0)
            sh[p, SUB + rows:SUB + rows + 1, :] = jnp.where(rad < n_rad - 1, ei[1, p], 0.0)
            return carry

        lax.fori_loop(p0, p0 + np_, one, 0)

    def smooth(tile, p0, np_):
        top = SUB + tile * SUB

        def one(p, carry):
            r = pl.ds(tile * SUB, SUB)
            mid = sh[p, top:top + SUB, :]
            up = sh[p, top - 1:top + SUB - 1, :]
            down = sh[p, top + 1:top + SUB + 1, :]
            out[p, r, :] = out[p, r, :] + visc[lax.rem(p, 2), r, :] * (down + up - 2.0 * mid)
            return carry

        lax.fori_loop(p0, p0 + np_, one, 0)

    for c in fetches:
        c.start()
    arrive(0)
    for c in fetches:
        c.wait()
    for t in range(tiles):
        shift_tile(t, dust, 2)
    edges = [send_edge(s, dust, 2) for s in (0, 1)]
    for e in edges:
        edge_wait(e)
    place_edges(dust, 2)
    for t in range(tiles):
        smooth(t, dust, 2)

    row = lax.broadcasted_iota(jnp.int32, (SUB, width), 0)
    for h in range(2):
        base = jnp.zeros((1, width), jnp.float32)
        for t in range(tiles):
            r = pl.ds(t * SUB, SUB)
            step = 2.0 * absorb[h, r, :] * out[dust + h, r, :] / total_rows
            run = step
            for k in (1, 2, 4):
                run = run + jnp.where(row >= k, pltpu.roll(run, k, 0), 0.0)
            run = run + base
            depth[h, r, :] = run - 0.5 * step
            base = run[SUB - 1:]
        tot_out[0, h] = base
    scan_send()
    arrive(1)
    shift_tile(0, 0, rest)
    edge_in = send_edge(0, 0, rest)
    scan_take()
    scan_send()
    arrive(2)
    shift_tile(tiles - 1, 0, rest)
    edge_out = send_edge(1, 0, rest)

    scan_take()
    while 1 << len(hops) < n_rad:
        scan_send()
        scan_take()
    for h in range(2):
        carried = tot_in[0, h]
        for i in range(1, len(hops)):
            carried = carried + tot_in[i, h]
        for t in range(tiles):
            r = pl.ds(t * SUB, SUB)
            radius = (rad * rows + t * SUB + row).astype(jnp.float32) + 0.5
            flux = 1.0 / (1.0 + radius / total_rows)
            depth[h, r, :] = depth[h, r, :] + carried
            heat[h, r, :] = flux * jnp.exp(-depth[h, r, :])

    def warm(tile):
        r = pl.ds(tile * SUB, SUB)
        for h in range(2):
            out[rest - 2 + h, r, :] = out[rest - 2 + h, r, :] + heat[h, r, :]

    edge_wait(edge_in)
    edge_wait(edge_out)
    place_edges(0, rest)
    i = 3
    for t in range(1, tiles - 2):
        arrive(i)
        shift_tile(t, 0, rest)
        smooth(t - 1, 0, rest)
        warm(t - 1)
        i += 1
    first = max(tiles - 3, 0)
    for p0, np_ in tail:
        arrive(i)
        shift_tile(tiles - 2, p0, np_)
        for t in range(first, tiles):
            smooth(t, p0, np_)
            if p0 + np_ == rest:
                warm(t)
        i += 1
    for goes, c in chained:
        pl.when(goes)(c.wait_send)
    for c in sent:
        c.wait_send()


def full(n_rad, n_az, state, offsets, viscosity, absorb):
    fields, polar, rows, width = state.shape
    planes = fields * polar
    groups = n_az // 2
    tiles = rows // SUB
    n_tail = len(tail_planes(planes - 2))
    n_pieces = 1 + 2 + max(tiles - 3, 0) + n_tail
    n_scan = (n_rad - 1).bit_length()
    n_local = 1
    n_sems = n_pieces * (2 * (groups - 1) + 1) + 4 + n_scan
    f32 = jnp.float32
    vm = pl.BlockSpec(memory_space=pltpu.VMEM)
    hbm = pl.BlockSpec(memory_space=pl.ANY)
    moved, local = pl.pallas_call(
        functools.partial(kernel, n_rad, n_az, n_local),
        out_shape=(
            pltpu.VMEM((planes, rows, width), f32),
            pltpu.VMEM((polar, rows, width), f32),
        ),
        in_specs=[hbm, pl.BlockSpec(memory_space=pltpu.SMEM), hbm, hbm],
        out_specs=(vm, vm),
        scratch_shapes=[
            pltpu.VMEM((polar, rows, width), f32),
            pltpu.VMEM((polar, rows, width), f32),
            pltpu.VMEM((polar, rows, width), f32),
            pltpu.VMEM((planes, rows, width), f32),
            pltpu.VMEM((n_az - 1, planes, rows, width), f32),
            pltpu.VMEM((planes, rows + 2 * SUB, width), f32),
            pltpu.VMEM((2, planes, 1, width), f32),
            pltpu.VMEM((2, planes, 1, width), f32),
            pltpu.VMEM((n_scan + 1, polar, 1, width), f32),
            pltpu.VMEM((n_scan, polar, 1, width), f32),
            pltpu.SemaphoreType.DMA((n_sems,)),
            pltpu.SemaphoreType.DMA((n_sems,)),
            pltpu.SemaphoreType.DMA((n_local + 2,)),
        ],
        compiler_params=pltpu.CompilerParams(
            collective_id=0, has_side_effects=True, vmem_limit_bytes=56 * 2**20
        ),
    )(state.reshape(planes, rows, width), offsets, viscosity, absorb)
    return moved, local


def fast_kernel(n_rad, n_az, cap, source, offs, visc_in, absorb_in, out, depth, flag,
                visc, absorb, heat, gathered, packed, pool_mine, pool_other, early_mine, early_other,
                stage, sh, eo, ei, tot_out, tot_in, take_v, look_v, take, look, ss, rs, ls):
    rad = lax.axis_index("rad")
    az = lax.axis_index("az")
    core = lax.rem(az, 2)
    chip = az // 2
    sibling = {"az": az + 1 - 2 * core}
    across = {"az": lax.rem(az + 2, n_az)}
    planes, rows, width = out.shape
    polar = 2
    fields = planes // polar
    cols = width // LANES
    col_bits = cols.bit_length() - 1
    tiles = rows // SUB
    units = rows * cols
    half = 2 * units
    ring = 2 * cols
    span = cols + 2
    total_rows = rows * n_rad
    dust, energy = fields - 1, fields - 2
    order = [dust, energy] + list(range(energy))
    last = order[-1]
    n_scan = (n_rad - 1).bit_length()
    n_early = 2 * ring

    def rad_at(k):
        return {"rad": lax.rem(rad + k + n_rad, n_rad)}

    def rad_pair(i):
        d = 1 << i
        upper = lax.rem(rad // d, 2)
        return {"rad": rad + d - 2 * d * upper}, upper

    count = [0, 0]

    def remote(src, dst, device):
        i = count[0]
        count[0] += 1
        return pltpu.make_async_remote_copy(
            src_ref=src, dst_ref=dst, send_sem=ss.at[i], recv_sem=rs.at[i],
            device_id=device, device_id_type=pl.DeviceIdType.MESH,
        )

    def local(src, dst):
        i = count[1]
        count[1] += 1
        c = pltpu.make_async_copy(src, dst, ls.at[i])
        c.start()
        return c

    inner, outer = rad > 0, rad < n_rad - 1
    ei[...] = jnp.zeros_like(ei)
    barrier = pltpu.get_barrier_semaphore()
    for peer in [sibling, across] + [rad_pair(i)[0] for i in range(1, n_scan)]:
        pl.semaphore_signal(barrier, inc=1, device_id=peer, device_id_type=pl.DeviceIdType.MESH)
    for there, k in ((inner, -1), (outer, 1)):
        @pl.when(there)
        def _():
            pl.semaphore_signal(barrier, inc=1, device_id=rad_at(k), device_id_type=pl.DeviceIdType.MESH)

    mine = pl.ds(core * units, units)
    first_pack = [local(source.at[polar * f + core], gathered[f].at[mine]) for f in order[:2]]

    pl.semaphore_wait(barrier, 2 + n_scan - 1 + inner.astype(jnp.int32) + outer.astype(jnp.int32))

    sent, chained = [], []
    to_pack = [remote(source.at[polar * f + 1 - core], gathered[f].at[mine], sibling) for f in order]
    to_mine = [remote(source.at[polar * f + 1 - core], pool_mine[f].at[mine], sibling) for f in order]
    to_other = [remote(source.at[polar * f + core], pool_other[f].at[mine], sibling) for f in order]
    to_early = [
        remote(source.at[polar * last + 1 - core], early_mine.at[mine], sibling),
        remote(source.at[polar * last + core], early_other.at[mine], sibling),
    ]
    sent += to_pack + to_mine + to_other + to_early
    for c in to_pack[:2]:
        c.start()
    own_pack = first_pack + [local(source.at[polar * f + core], gathered[f].at[mine]) for f in order[2:]]
    own_mine = [local(source.at[polar * f + core], pool_mine[f].at[mine]) for f in order]
    own_other = [local(source.at[polar * f + 1 - core], pool_other[f].at[mine]) for f in order]
    own_early = [
        local(source.at[polar * last + core], early_mine.at[mine]),
        local(source.at[polar * last + 1 - core], early_other.at[mine]),
    ]
    params = [local(visc_in, visc), local(absorb_in, absorb)]

    lane = lax.broadcasted_iota(jnp.int32, (SUB, LANES), 1)
    sub = lax.broadcasted_iota(jnp.int32, (SUB, LANES), 0)

    def row_offsets(numbers):
        amount = jnp.full((SUB, LANES), offs[numbers[0]], jnp.int32)
        for k in range(1, len(numbers)):
            amount = jnp.where(sub == k, offs[numbers[k]], amount)
        return amount

    def block_unit(b):
        return (b >> col_bits) * units + (b & (cols - 1)) * SUB

    shifts = [row_offsets([t * SUB + k for k in range(SUB)]) for t in range(tiles)]
    leads, manys, befores = [], [], []
    used = jnp.zeros((SUB, LANES), jnp.int32)
    for off in shifts:
        lead = jnp.where(off == 0, ring - 1, jnp.where(off < 2 * width, (2 * width - 1 - off) >> LANE_BITS, 0))
        many = jnp.where(off < 2 * width, ring - lead, jnp.minimum(((4 * width - off) >> LANE_BITS) + 1, ring))
        many = jnp.where(off == 0, 2, many)
        run = many
        for k in (1, 2, 4):
            run = run + jnp.where(sub >= k, pltpu.roll(run, k, 0), 0)
        leads.append(lead)
        manys.append(many)
        befores.append(run - many + used)
        used = used + jnp.broadcast_to(run[SUB - 1:], (SUB, LANES))
    top_many = jnp.broadcast_to(manys[0][:1], (SUB, LANES))
    bottom_many = jnp.broadcast_to(manys[-1][SUB - 1:], (SUB, LANES))
    bases = []
    for t in range(tiles):
        base = befores[t] + bottom_many
        if t == 0:
            base = jnp.where(sub == 0, 0, base)
        if t == tiles - 1:
            base = jnp.where(sub == SUB - 1, top_many, base)
        bases.append(base)
    for q in range(-(-cap // LANES)):
        j = q * LANES + lane
        place = jnp.zeros((SUB, LANES), jnp.int32)
        ahead = jnp.zeros((SUB, LANES), jnp.int32)
        for t in range(tiles):
            held = (j >= bases[t]) & (j < bases[t] + manys[t])
            place = place + jnp.where(held, t * SUB * cols + sub, 0)
            ahead = ahead + jnp.where(held, leads[t] - bases[t], 0)
        for k in (4, 2, 1):
            place = place + pltpu.roll(place, k, 0)
            ahead = ahead + pltpu.roll(ahead, k, 0)
        take_v[q:q + 1, :] = (block_unit((j + ahead) & (ring - 1)) + place)[:1]
    take_copy = local(take_v, take)
    for t in range(tiles):
        b = az * cols - (shifts[t] >> LANE_BITS) - 1 + lane + 2 * ring
        near = block_unit(b & (ring - 1)) + (t * SUB * cols + sub)
        far = half + jnp.minimum(bases[t] + ((b - leads[t]) & (ring - 1)), cap - 1)
        look_v[t * SUB:(t + 1) * SUB, :] = jnp.where(((b >> (col_bits + 1)) & 1) == chip, near, far)
    look_copy = local(look_v, look)

    crossing = {f: [] for f in order}
    cuts = {f: [0, cap // 2 // SUB * SUB, cap] for f in order}
    cuts[last] = [n_early, (n_early + cap) // 2 // SUB * SUB, cap]

    def pack(some, lo, hi):
        def eight(k, carry):
            for s in range(SUB):
                u = take[k >> 4, (k & 15) * SUB + s]
                for f in some:
                    packed[f][pl.ds(k * SUB + s, 1), :] = gathered[f][pl.ds(u, 1), :]
            return carry

        lax.fori_loop(lo // SUB, hi // SUB, eight, 0)

    def pack_ready(f):
        own_pack[order.index(f)].wait()
        to_pack[order.index(f)].wait_recv()

    def pack_send(f):
        for lo, hi in zip(cuts[f], cuts[f][1:]):
            pack([f], lo, hi)
            c = remote(packed[f].at[pl.ds(lo, hi - lo)], pool_mine[f].at[pl.ds(half + lo, hi - lo)], across)
            c.start()
            sent.append(c)
            crossing[f].append(c)

    def shift_rows(numbers, shift, source_ref, slot, write):
        for s, r in enumerate(numbers):
            for i in range(span):
                u = look[r, i]
                stage[slot, i, s:s + 1, :] = source_ref[pl.ds(u, 1), :]
        rem = shift & (LANES - 1)
        pick = (lane - rem) & (LANES - 1)
        low = lane < rem
        turned = [
            jnp.take_along_axis(stage[slot, i], pick, axis=1, mode="promise_in_bounds") for i in range(span)
        ]
        x = [turned[0]] + [jnp.where(low, turned[j - 1], turned[j]) for j in range(1, span)]
        write(x)

    def shift_plane(f, source_ref, p):
        def one(tile, slot):
            r = pl.ds(pl.multiple_of(tile * SUB, SUB), SUB)
            below = pl.ds(pl.multiple_of(SUB + tile * SUB, SUB), SUB)

            def write(x):
                right = [pltpu.roll(v, 1, 1) for v in x[:-1]]
                left = [pltpu.roll(v, LANES - 1, 1) for v in x[1:]]
                for c in range(cols):
                    cs = pl.ds(c * LANES, LANES)
                    mid = x[c + 1]
                    prev = jnp.where(lane == 0, right[c], right[c + 1])
                    nxt = jnp.where(lane == LANES - 1, left[c + 1], left[c])
                    sh[p, below, cs] = mid
                    out[p, r, cs] = mid + AZIMUTH_COEF * (nxt + prev - 2.0 * mid)

            numbers = [tile * SUB + s for s in range(SUB)]
            shift_rows(numbers, row_offsets(numbers), source_ref, slot, write)

        def pair(k, carry):
            one(2 * k, 0)
            one(2 * k + 1, 1)
            return carry

        lax.fori_loop(0, tiles // 2, pair, 0)

    def send_edges(f):
        ps = pl.ds(polar * f, polar)
        got = []
        for side in range(2):
            c = remote(eo.at[side, ps], ei.at[1 - side, ps], rad_at(-1 if side == 0 else 1))
            goes, comes = (inner, outer) if side == 0 else (outer, inner)
            pl.when(goes)(c.start)
            chained.append((goes, c))
            got.append((comes, c))
        return got

    def take_edges(f, got):
        for comes, c in got:
            pl.when(comes)(c.wait_recv)
        for h in range(polar):
            p = polar * f + h
            sh[p, SUB - 1:SUB, :] = jnp.where(rad > 0, ei[0, p], 0.0)
            sh[p, SUB + rows:SUB + rows + 1, :] = jnp.where(rad < n_rad - 1, ei[1, p], 0.0)

    def smooth(f, h):
        p = polar * f + h
        for tile in range(tiles):
            top = SUB + tile * SUB
            r = pl.ds(tile * SUB, SUB)
            mid = sh[p, top:top + SUB, :]
            up = sh[p, top - 1:top + SUB - 1, :]
            down = sh[p, top + 1:top + SUB + 1, :]
            new = out[p, r, :] + visc[h, r, :] * (down + up - 2.0 * mid)
            if f == energy:
                new = new + heat[h, r, :]
            out[p, r, :] = new

    def forward(f):
        i = order.index(f)
        onward = []
        for c, lo, hi in zip(crossing[f], cuts[f], cuts[f][1:]):
            c.wait_recv()
            at = pl.ds(half + lo, hi - lo)
            c = remote(pool_mine[f].at[at], pool_other[f].at[at], sibling)
            c.start()
            sent.append(c)
            onward.append(c)
        own_mine[i].wait()
        to_mine[i].wait_recv()
        return onward

    def other_ready(f, onward):
        i = order.index(f)
        own_other[i].wait()
        to_other[i].wait_recv()
        for c in onward:
            c.wait_recv()

    def work(f):
        onward = forward(f)
        shift_plane(f, pool_mine[f], polar * f + core)
        other_ready(f, onward)
        shift_plane(f, pool_other[f], polar * f + 1 - core)
        for h in range(polar):
            p = polar * f + h
            eo[0, p] = sh[p, SUB:SUB + 1, :]
            eo[1, p] = sh[p, SUB + rows - 1:SUB + rows, :]
        return send_edges(f)

    def finish(f, got):
        take_edges(f, got)
        for h in range(polar):
            smooth(f, h)

    early_at = pl.ds(half, n_early)

    def early_edges():
        crossing_early.wait_recv()
        onward = remote(early_mine.at[early_at], early_other.at[early_at], sibling)
        onward.start()
        sent.append(onward)
        numbers = [0, rows - 1]
        for c in own_early:
            c.wait()
        for c in to_early:
            c.wait_recv()
        copies = [local(early_mine.at[early_at], pool_mine[last].at[early_at])]
        for ref, hh in ((early_mine, core), (early_other, 1 - core)):
            p = polar * last + hh
            if ref is early_other:
                onward.wait_recv()
                copies.append(local(early_other.at[early_at], pool_other[last].at[early_at]))

            def write(x):
                for c in range(cols):
                    cs = pl.ds(c * LANES, LANES)
                    eo[0, p, :, cs] = x[c + 1][:1]
                    eo[1, p, :, cs] = x[c + 1][1:2]

            shift_rows(numbers, row_offsets(numbers), ref, 0, write)
        got = send_edges(last)
        for c in copies:
            c.wait()
        return got

    take_copy.wait()
    pack_ready(dust)
    pack_send(dust)
    for c in to_pack[2:]:
        c.start()
    look_copy.wait()
    pack_ready(energy)
    pack_send(energy)
    for i in range(2):
        to_mine[i].start()
        to_other[i].start()
    for f in order[2:-1]:
        pack_ready(f)
        pack_send(f)
    pack_ready(last)
    pack([last], 0, n_early)
    crossing_early = remote(packed[last].at[pl.ds(0, n_early)], early_mine.at[early_at], across)
    crossing_early.start()
    sent.append(crossing_early)
    for c in to_early:
        c.start()
    for i in range(2, fields):
        to_mine[i].start()
        to_other[i].start()
    pack_send(last)
    for c in params:
        c.wait()

    finish(dust, work(dust))

    row = lax.broadcasted_iota(jnp.int32, (SUB, width), 0)
    for h in range(polar):
        run_last = jnp.zeros((1, width), jnp.float32)
        for t in range(tiles):
            r = pl.ds(t * SUB, SUB)
            step = 2.0 * absorb[h, r, :] * out[polar * dust + h, r, :] / total_rows
            run = step
            for k in (1, 2, 4):
                run = run + jnp.where(row >= k, pltpu.roll(run, k, 0), 0.0)
            run = run + run_last
            depth[h, r, :] = run - 0.5 * step
            run_last = run[SUB - 1:]
        tot_out[0, h] = run_last
    over = (used > cap).astype(jnp.float32)[:1]
    for c in range(cols):
        tot_out[0, polar, :, pl.ds(c * LANES, LANES)] = over

    hops = []

    def scan_send():
        i = len(hops)
        peer, upper = rad_pair(i)
        c = remote(tot_out.at[i], tot_in.at[i], peer)
        c.start()
        sent.append(c)
        hops.append((c, upper))

    def scan_take():
        i = len(hops) - 1
        hops[i][0].wait_recv()
        tot_out[i + 1] = tot_out[i] + tot_in[i]

    scan_send()
    pending = (energy, work(energy))
    scan_take()
    while len(hops) < n_scan:
        scan_send()
        scan_take()
    for h in range(polar):
        carried = jnp.where(hops[0][1] == 1, tot_in[0, h], 0.0)
        for i in range(1, n_scan):
            carried = carried + jnp.where(hops[i][1] == 1, tot_in[i, h], 0.0)
        for t in range(tiles):
            r = pl.ds(t * SUB, SUB)
            radius = (rad * rows + t * SUB + row).astype(jnp.float32) + 0.5
            flux = 1.0 / (1.0 + radius / total_rows)
            depth[h, r, :] = depth[h, r, :] + carried
            heat[h, r, :] = flux * jnp.exp(-depth[h, r, :])
    flag[0] = jnp.max(tot_out[n_scan, polar])
    for f in order[2:-1]:
        following = (f, work(f))
        finish(*pending)
        pending = following
    last_edges = early_edges()
    finish(*pending)
    take_edges(last, last_edges)
    onward = forward(last)
    shift_plane(last, pool_mine[last], polar * last + core)
    smooth(last, core)
    other_ready(last, onward)
    shift_plane(last, pool_other[last], polar * last + 1 - core)
    smooth(last, 1 - core)
    for goes, c in chained:
        pl.when(goes)(c.wait_send)
    for c in sent:
        c.wait_send()


def fast(n_rad, n_az, state, offsets, viscosity, absorb):
    fields, polar, rows, width = state.shape
    planes = fields * polar
    cols = width // LANES
    units = rows * cols
    cap = units * 2 * 23 // 32 // 16 * 16
    n_early = 4 * cols
    n_scan = (n_rad - 1).bit_length()
    n_sems = 9 * fields + 4 + n_scan
    f32, i32 = jnp.float32, jnp.int32
    vm = pl.BlockSpec(memory_space=pltpu.VMEM)
    sm = pl.BlockSpec(memory_space=pltpu.SMEM)
    hbm = pl.BlockSpec(memory_space=pl.ANY)
    source = state.reshape(planes, rows // SUB, SUB, cols, LANES).transpose(0, 1, 3, 2, 4).reshape(planes, units, LANES)
    moved, local, flag = pl.pallas_call(
        functools.partial(fast_kernel, n_rad, n_az, cap),
        out_shape=(
            pltpu.VMEM((planes, rows, width), f32),
            pltpu.VMEM((polar, rows, width), f32),
            jax.ShapeDtypeStruct((1,), f32),
        ),
        in_specs=[hbm, sm, hbm, hbm],
        out_specs=(vm, vm, sm),
        scratch_shapes=[
            pltpu.VMEM((polar, rows, width), f32),
            pltpu.VMEM((polar, rows, width), f32),
            pltpu.VMEM((polar, rows, width), f32),
            [pltpu.VMEM((2 * units, LANES), f32)] * fields,
            [pltpu.VMEM((cap, LANES), f32)] * fields,
            [pltpu.VMEM((2 * units + cap, LANES), f32)] * fields,
            [pltpu.VMEM((2 * units + cap, LANES), f32)] * fields,
            pltpu.VMEM((2 * units + n_early, LANES), f32),
            pltpu.VMEM((2 * units + n_early, LANES), f32),
            pltpu.VMEM((2, cols + 2, SUB, LANES), f32),
            pltpu.VMEM((planes, rows + 2 * SUB, width), f32),
            pltpu.VMEM((2, planes, 1, width), f32),
            pltpu.VMEM((2, planes, 1, width), f32),
            pltpu.VMEM((n_scan + 1, polar + 1, 1, width), f32),
            pltpu.VMEM((n_scan, polar + 1, 1, width), f32),
            pltpu.VMEM((SUB, LANES), i32),
            pltpu.VMEM((rows, LANES), i32),
            pltpu.SMEM((SUB, LANES), i32),
            pltpu.SMEM((rows, LANES), i32),
            pltpu.SemaphoreType.DMA((n_sems,)),
            pltpu.SemaphoreType.DMA((n_sems,)),
            pltpu.SemaphoreType.DMA((3 * fields + 8,)),
        ],
        compiler_params=pltpu.CompilerParams(
            collective_id=1, has_side_effects=True, vmem_limit_bytes=40 * 2**20
        ),
    )(source, offsets, viscosity, absorb)
    return moved, local, flag[0]


def body(n_rad, n_az, state, offsets, viscosity, absorb):
    args = (state, offsets, viscosity, absorb)
    if n_az != 4 or state.shape[1] != 2 or n_rad < 2 or n_rad & (n_rad - 1):
        moved, local = full(n_rad, n_az, *args)
    else:
        moved, local, flag = fast(n_rad, n_az, *args)
        moved, local = lax.cond(
            flag > 0, lambda m, d: tuple(full(n_rad, n_az, *args)), lambda m, d: (m, d), moved, local
        )
    return moved.reshape(state.shape), local


def solution(mesh):
    in_specs = (P(None, None, "rad", "az"), P("rad"), P(None, "rad", "az"), P(None, "rad", "az"))
    out_specs = (P(None, None, "rad", "az"), P(None, "rad", "az"))
    f = functools.partial(body, mesh.shape["rad"], mesh.shape["az"])
    return jax.shard_map(f, mesh=mesh, in_specs=in_specs, out_specs=out_specs, check_vma=False)
```

```python
import functools

import jax
import jax.numpy as jnp
from jax import lax
from jax.experimental import pallas as pl
from jax.experimental.pallas import tpu as pltpu
from jax.sharding import PartitionSpec as P

AZIMUTH_COEF = 0.1
LANES = 128
SUB = 8
LANE_BITS = 7
SUB_BITS = 3


def tail_planes(rest):
    cuts = [0, rest // 2, rest]
    return [(a, b - a) for a, b in zip(cuts, cuts[1:]) if b > a]


def kernel(n_rad, n_az, n_local, source, offs, visc_in, absorb_in, out, depth,
           visc, absorb, heat, state, buf, sh, eo, ei, tot_out, tot_in, ss, rs, ls):
    groups = n_az // 2
    rad = lax.axis_index("rad")
    az = lax.axis_index("az")
    core = lax.rem(az, 2)
    sibling = {"az": az + 1 - 2 * core}
    planes, rows, width = state.shape
    cols = width // LANES
    tiles = rows // SUB
    dust = planes - 2
    rest = dust
    total_rows = rows * n_rad

    def rad_at(k):
        return {"rad": lax.rem(rad + k + n_rad, n_rad)}

    def az_at(k):
        return {"az": lax.rem(az + 2 * k, n_az)}

    count = [0]

    def remote(src, dst, device):
        i = count[0]
        count[0] += 1
        return pltpu.make_async_remote_copy(
            src_ref=src, dst_ref=dst, send_sem=ss.at[i], recv_sem=rs.at[i],
            device_id=device, device_id_type=pl.DeviceIdType.MESH,
        )

    fetch = pltpu.make_async_copy(source, state, ls.at[0])
    fetches = [fetch] + [
        pltpu.make_async_copy(a, b, ls.at[n_local + i])
        for i, (a, b) in enumerate(((visc_in, visc), (absorb_in, absorb)))
    ]
    inner, outer = rad > 0, rad < n_rad - 1
    ei[...] = jnp.zeros_like(ei)
    tot_in[...] = jnp.zeros_like(tot_in)
    peers = [az_at(k) for k in range(1, groups)] + [sibling]
    barrier = pltpu.get_barrier_semaphore()
    for there, k in ((inner, -1), (outer, 1)):
        @pl.when(there)
        def _():
            pl.semaphore_signal(barrier, inc=1, device_id=rad_at(k), device_id_type=pl.DeviceIdType.MESH)
    for peer in peers:
        pl.semaphore_signal(barrier, inc=1, device_id=peer, device_id_type=pl.DeviceIdType.MESH)
    senders = len(peers)
    d = 1
    while d < n_rad:
        if d > 1:
            @pl.when(rad >= d)
            def _():
                pl.semaphore_signal(barrier, inc=1, device_id=rad_at(-d), device_id_type=pl.DeviceIdType.MESH)
            senders = senders + (rad + d < n_rad).astype(jnp.int32)
        d *= 2
    pl.semaphore_wait(barrier, senders + inner.astype(jnp.int32) + outer.astype(jnp.int32))

    pieces = [(dust, 2, 0, rows)]
    edge_tiles = [0, tiles - 1]
    for t in edge_tiles + list(range(1, tiles - 2)):
        pieces.append((0, rest, t * SUB, SUB))
    tail = tail_planes(rest)
    for p0, np_ in tail:
        pieces.append((p0, np_, (tiles - 2) * SUB, SUB))

    sent, chained = [], []
    across, beside = [], []
    for p0, np_, r0, nr in pieces:
        ps, rws = pl.ds(p0, np_), pl.ds(r0, nr)
        across.append([remote(source.at[ps, rws], buf.at[2 * k - 1, ps, rws], az_at(k)) for k in range(1, groups)])
        beside.append(remote(source.at[ps, rws], buf.at[0, ps, rws], sibling))
        for c in across[-1]:
            c.start()
            sent.append(c)
    for c in beside:
        c.start()
        sent.append(c)

    def arrive(i):
        p0, np_, r0, nr = pieces[i]
        ps, rws = pl.ds(p0, np_), pl.ds(r0, nr)
        forwards = []
        for k in range(1, groups):
            across[i][k - 1].wait_recv()
            f = remote(buf.at[2 * k - 1, ps, rws], buf.at[2 * k, ps, rws], sibling)
            f.start()
            sent.append(f)
            forwards.append(f)
        beside[i].wait_recv()
        for f in forwards:
            f.wait_recv()

    lane = lax.broadcasted_iota(jnp.int32, (SUB, LANES), 1)

    def shift_tile(tile, p0, np_):
        r = pl.ds(tile * SUB, SUB)
        sub = lax.broadcasted_iota(jnp.int32, (SUB, LANES), 0)
        amount = jnp.full((SUB, LANES), offs[tile * SUB], jnp.int32)
        for k in range(1, SUB):
            amount = jnp.where(sub == k, offs[tile * SUB + k], amount)
        block = amount // width
        within = amount - block * width
        column = within // LANES
        rem = within - column * LANES
        pick = (lane - rem) & (LANES - 1)
        low = lane < rem

        def one(p, carry):
            def load(d, c):
                cs = pl.ds(c * LANES, LANES)
                if d == 0:
                    return state[p, r, cs]
                if d % 2 == 0:
                    return buf[d - 1, p, r, cs]
                slot = jnp.where(core == 1, d, (d + 2) % n_az)
                return buf[slot - 1, p, r, cs]

            line = []
            for move, c in [(1, c) for c in range(cols)] + [(0, c) for c in range(cols)] + [(-1, 0)]:
                value = load(move % n_az, c)
                for b in range(1, n_az):
                    value = jnp.where(block == b, load((b + move) % n_az, c), value)
                line.append(value)
            step = cols // 2
            while step:
                chosen = (column & step) != 0
                line = [jnp.where(chosen, line[i - step], line[i]) for i in range(step, len(line))]
                step //= 2
            turned = [jnp.take_along_axis(v, pick, axis=1, mode="promise_in_bounds") for v in line]
            x = [turned[0]] + [jnp.where(low, turned[j - 1], turned[j]) for j in range(1, len(turned))]
            right = [pltpu.roll(v, 1, 1) for v in x[:-1]]
            left = [pltpu.roll(v, LANES - 1, 1) for v in x[1:]]
            for c in range(cols):
                cs = pl.ds(c * LANES, LANES)
                mid = x[c + 1]
                prev = jnp.where(lane == 0, right[c], right[c + 1])
                nxt = jnp.where(lane == LANES - 1, left[c + 1], left[c])
                sh[p, pl.ds(SUB + tile * SUB, SUB), cs] = mid
                out[p, r, cs] = mid + AZIMUTH_COEF * (nxt + prev - 2.0 * mid)
                if tile == 0:
                    eo[0, p, :, cs] = mid[:1]
                if tile == tiles - 1:
                    eo[1, p, :, cs] = mid[SUB - 1:]
            return carry

        lax.fori_loop(p0, p0 + np_, one, 0)

    hops = []

    def scan_send():
        i = len(hops)
        d = 1 << i
        if d < n_rad:
            c = remote(tot_out.at[i], tot_in.at[i], rad_at(d))
            goes = rad + d < n_rad
            pl.when(goes)(c.start)
            chained.append((goes, c))
            hops.append(c)

    def scan_take():
        i = len(hops) - 1
        pl.when(rad >= 1 << i)(hops[i].wait_recv)
        tot_out[i + 1] = tot_out[i] + tot_in[i]

    def send_edge(side, p0, np_):
        ps = pl.ds(p0, np_)
        c = remote(eo.at[side, ps], ei.at[1 - side, ps], rad_at(-1 if side == 0 else 1))
        goes, comes = (inner, outer) if side == 0 else (outer, inner)
        pl.when(goes)(c.start)
        chained.append((goes, c))
        return comes, c

    def edge_wait(edge):
        pl.when(edge[0])(edge[1].wait_recv)

    def place_edges(p0, np_):
        def one(p, carry):
            sh[p, SUB - 1:SUB, :] = jnp.where(rad > 0, ei[0, p], 0.0)
            sh[p, SUB + rows:SUB + rows + 1, :] = jnp.where(rad < n_rad - 1, ei[1, p], 0.0)
            return carry

        lax.fori_loop(p0, p0 + np_, one, 0)

    def smooth(tile, p0, np_):
        top = SUB + tile * SUB

        def one(p, carry):
            r = pl.ds(tile * SUB, SUB)
            mid = sh[p, top:top + SUB, :]
            up = sh[p, top - 1:top + SUB - 1, :]
            down = sh[p, top + 1:top + SUB + 1, :]
            out[p, r, :] = out[p, r, :] + visc[lax.rem(p, 2), r, :] * (down + up - 2.0 * mid)
            return carry

        lax.fori_loop(p0, p0 + np_, one, 0)

    for c in fetches:
        c.start()
    arrive(0)
    for c in fetches:
        c.wait()
    for t in range(tiles):
        shift_tile(t, dust, 2)
    edges = [send_edge(s, dust, 2) for s in (0, 1)]
    for e in edges:
        edge_wait(e)
    place_edges(dust, 2)
    for t in range(tiles):
        smooth(t, dust, 2)

    row = lax.broadcasted_iota(jnp.int32, (SUB, width), 0)
    for h in range(2):
        base = jnp.zeros((1, width), jnp.float32)
        for t in range(tiles):
            r = pl.ds(t * SUB, SUB)
            step = 2.0 * absorb[h, r, :] * out[dust + h, r, :] / total_rows
            run = step
            for k in (1, 2, 4):
                run = run + jnp.where(row >= k, pltpu.roll(run, k, 0), 0.0)
            run = run + base
            depth[h, r, :] = run - 0.5 * step
            base = run[SUB - 1:]
        tot_out[0, h] = base
    scan_send()
    arrive(1)
    shift_tile(0, 0, rest)
    edge_in = send_edge(0, 0, rest)
    scan_take()
    scan_send()
    arrive(2)
    shift_tile(tiles - 1, 0, rest)
    edge_out = send_edge(1, 0, rest)

    scan_take()
    while 1 << len(hops) < n_rad:
        scan_send()
        scan_take()
    for h in range(2):
        carried = tot_in[0, h]
        for i in range(1, len(hops)):
            carried = carried + tot_in[i, h]
        for t in range(tiles):
            r = pl.ds(t * SUB, SUB)
            radius = (rad * rows + t * SUB + row).astype(jnp.float32) + 0.5
            flux = 1.0 / (1.0 + radius / total_rows)
            depth[h, r, :] = depth[h, r, :] + carried
            heat[h, r, :] = flux * jnp.exp(-depth[h, r, :])

    def warm(tile):
        r = pl.ds(tile * SUB, SUB)
        for h in range(2):
            out[rest - 2 + h, r, :] = out[rest - 2 + h, r, :] + heat[h, r, :]

    edge_wait(edge_in)
    edge_wait(edge_out)
    place_edges(0, rest)
    i = 3
    for t in range(1, tiles - 2):
        arrive(i)
        shift_tile(t, 0, rest)
        smooth(t - 1, 0, rest)
        warm(t - 1)
        i += 1
    first = max(tiles - 3, 0)
    for p0, np_ in tail:
        arrive(i)
        shift_tile(tiles - 2, p0, np_)
        for t in range(first, tiles):
            smooth(t, p0, np_)
            if p0 + np_ == rest:
                warm(t)
        i += 1
    for goes, c in chained:
        pl.when(goes)(c.wait_send)
    for c in sent:
        c.wait_send()


def full(n_rad, n_az, state, offsets, viscosity, absorb):
    fields, polar, rows, width = state.shape
    planes = fields * polar
    groups = n_az // 2
    tiles = rows // SUB
    n_tail = len(tail_planes(planes - 2))
    n_pieces = 1 + 2 + max(tiles - 3, 0) + n_tail
    n_scan = (n_rad - 1).bit_length()
    n_local = 1
    n_sems = n_pieces * (2 * (groups - 1) + 1) + 4 + n_scan
    f32 = jnp.float32
    vm = pl.BlockSpec(memory_space=pltpu.VMEM)
    hbm = pl.BlockSpec(memory_space=pl.ANY)
    moved, local = pl.pallas_call(
        functools.partial(kernel, n_rad, n_az, n_local),
        out_shape=(
            pltpu.VMEM((planes, rows, width), f32),
            pltpu.VMEM((polar, rows, width), f32),
        ),
        in_specs=[hbm, pl.BlockSpec(memory_space=pltpu.SMEM), hbm, hbm],
        out_specs=(vm, vm),
        scratch_shapes=[
            pltpu.VMEM((polar, rows, width), f32),
            pltpu.VMEM((polar, rows, width), f32),
            pltpu.VMEM((polar, rows, width), f32),
            pltpu.VMEM((planes, rows, width), f32),
            pltpu.VMEM((n_az - 1, planes, rows, width), f32),
            pltpu.VMEM((planes, rows + 2 * SUB, width), f32),
            pltpu.VMEM((2, planes, 1, width), f32),
            pltpu.VMEM((2, planes, 1, width), f32),
            pltpu.VMEM((n_scan + 1, polar, 1, width), f32),
            pltpu.VMEM((n_scan, polar, 1, width), f32),
            pltpu.SemaphoreType.DMA((n_sems,)),
            pltpu.SemaphoreType.DMA((n_sems,)),
            pltpu.SemaphoreType.DMA((n_local + 2,)),
        ],
        compiler_params=pltpu.CompilerParams(
            collective_id=0, has_side_effects=True, vmem_limit_bytes=56 * 2**20
        ),
    )(state.reshape(planes, rows, width), offsets, viscosity, absorb)
    return moved, local


def fast_kernel(n_rad, n_az, cap, source, offs, visc_in, absorb_in, out, depth, flag,
                visc, absorb, heat, gathered, packed, pool_mine, pool_other, early_mine, early_other,
                stage, sh, eo, ei, tot_out, tot_in, take_v, look_v, take, look, ss, rs, ls):
    rad = lax.axis_index("rad")
    az = lax.axis_index("az")
    core = lax.rem(az, 2)
    chip = az // 2
    sibling = {"az": az + 1 - 2 * core}
    across = {"az": lax.rem(az + 2, n_az)}
    planes, rows, width = out.shape
    polar = 2
    fields = planes // polar
    cols = width // LANES
    col_bits = cols.bit_length() - 1
    tiles = rows // SUB
    units = rows * cols
    half = 2 * units
    ring = 2 * cols
    span = cols + 2
    total_rows = rows * n_rad
    dust, energy = fields - 1, fields - 2
    order = [dust, energy] + list(range(energy))
    last = order[-1]
    n_scan = (n_rad - 1).bit_length()
    n_early = 2 * ring

    def rad_at(k):
        return {"rad": lax.rem(rad + k + n_rad, n_rad)}

    def rad_pair(i):
        d = 1 << i
        upper = lax.rem(rad // d, 2)
        return {"rad": rad + d - 2 * d * upper}, upper

    count = [0, 0]

    def remote(src, dst, device):
        i = count[0]
        count[0] += 1
        return pltpu.make_async_remote_copy(
            src_ref=src, dst_ref=dst, send_sem=ss.at[i], recv_sem=rs.at[i],
            device_id=device, device_id_type=pl.DeviceIdType.MESH,
        )

    def local(src, dst):
        i = count[1]
        count[1] += 1
        c = pltpu.make_async_copy(src, dst, ls.at[i])
        c.start()
        return c

    inner, outer = rad > 0, rad < n_rad - 1
    ei[...] = jnp.zeros_like(ei)
    barrier = pltpu.get_barrier_semaphore()
    for peer in [sibling, across] + [rad_pair(i)[0] for i in range(1, n_scan)]:
        pl.semaphore_signal(barrier, inc=1, device_id=peer, device_id_type=pl.DeviceIdType.MESH)
    for there, k in ((inner, -1), (outer, 1)):
        @pl.when(there)
        def _():
            pl.semaphore_signal(barrier, inc=1, device_id=rad_at(k), device_id_type=pl.DeviceIdType.MESH)

    mine = pl.ds(core * units, units)
    first_pack = [local(source.at[polar * f + core], gathered[f].at[mine]) for f in order[:2]]

    pl.semaphore_wait(barrier, 2 + n_scan - 1 + inner.astype(jnp.int32) + outer.astype(jnp.int32))

    sent, chained = [], []
    to_pack = [remote(source.at[polar * f + 1 - core], gathered[f].at[mine], sibling) for f in order]
    to_mine = [remote(source.at[polar * f + 1 - core], pool_mine[f].at[mine], sibling) for f in order]
    to_other = [remote(source.at[polar * f + core], pool_other[f].at[mine], sibling) for f in order]
    to_early = [
        remote(source.at[polar * last + 1 - core], early_mine.at[mine], sibling),
        remote(source.at[polar * last + core], early_other.at[mine], sibling),
    ]
    sent += to_pack + to_mine + to_other + to_early
    for c in to_pack[:2]:
        c.start()
    lane = lax.broadcasted_iota(jnp.int32, (SUB, LANES), 1)
    sub = lax.broadcasted_iota(jnp.int32, (SUB, LANES), 0)

    def row_offsets(numbers):
        amount = jnp.full((SUB, LANES), offs[numbers[0]], jnp.int32)
        for k in range(1, len(numbers)):
            amount = jnp.where(sub == k, offs[numbers[k]], amount)
        return amount

    def block_unit(b):
        return (b >> col_bits) * units + (b & (cols - 1)) * SUB

    shifts = [row_offsets([t * SUB + k for k in range(SUB)]) for t in range(tiles)]
    leads, manys, befores = [], [], []
    used = jnp.zeros((SUB, LANES), jnp.int32)
    for off in shifts:
        lead = jnp.where(off == 0, ring - 1, jnp.where(off < 2 * width, (2 * width - 1 - off) >> LANE_BITS, 0))
        many = jnp.where(off < 2 * width, ring - lead, jnp.minimum(((4 * width - off) >> LANE_BITS) + 1, ring))
        many = jnp.where(off == 0, 2, many)
        run = many
        for k in (1, 2, 4):
            run = run + jnp.where(sub >= k, pltpu.roll(run, k, 0), 0)
        leads.append(lead)
        manys.append(many)
        befores.append(run - many + used)
        used = used + jnp.broadcast_to(run[SUB - 1:], (SUB, LANES))
    top_many = jnp.broadcast_to(manys[0][:1], (SUB, LANES))
    bottom_many = jnp.broadcast_to(manys[-1][SUB - 1:], (SUB, LANES))
    bases = []
    for t in range(tiles):
        base = befores[t] + bottom_many
        if t == 0:
            base = jnp.where(sub == 0, 0, base)
        if t == tiles - 1:
            base = jnp.where(sub == SUB - 1, top_many, base)
        bases.append(base)
    for q in range(-(-cap // LANES)):
        j = q * LANES + lane
        place = jnp.zeros((SUB, LANES), jnp.int32)
        ahead = jnp.zeros((SUB, LANES), jnp.int32)
        for t in range(tiles):
            held = (j >= bases[t]) & (j < bases[t] + manys[t])
            place = place + jnp.where(held, t * SUB * cols + sub, 0)
            ahead = ahead + jnp.where(held, leads[t] - bases[t], 0)
        for k in (4, 2, 1):
            place = place + pltpu.roll(place, k, 0)
            ahead = ahead + pltpu.roll(ahead, k, 0)
        take_v[q:q + 1, :] = (block_unit((j + ahead) & (ring - 1)) + place)[:1]
    take_copy = local(take_v, take)
    for t in range(tiles):
        b = az * cols - (shifts[t] >> LANE_BITS) - 1 + lane + 2 * ring
        near = block_unit(b & (ring - 1)) + (t * SUB * cols + sub)
        far = half + jnp.minimum(bases[t] + ((b - leads[t]) & (ring - 1)), cap - 1)
        look_v[t * SUB:(t + 1) * SUB, :] = jnp.where(((b >> (col_bits + 1)) & 1) == chip, near, far)
    look_copy = local(look_v, look)

    crossing = {f: [] for f in order}
    cuts = {f: [0, cap // 2 // SUB * SUB, cap] for f in order}
    cuts[last] = [n_early, (n_early + cap) // 2 // SUB * SUB, cap]

    def pack(some, lo, hi):
        def eight(k, carry):
            for s in range(SUB):
                u = take[k >> 4, (k & 15) * SUB + s]
                for f in some:
                    packed[f][pl.ds(k * SUB + s, 1), :] = gathered[f][pl.ds(u, 1), :]
            return carry

        lax.fori_loop(lo // SUB, hi // SUB, eight, 0)

    def pack_ready(f):
        own_pack[order.index(f)].wait()
        to_pack[order.index(f)].wait_recv()

    def pack_send(f):
        for lo, hi in zip(cuts[f], cuts[f][1:]):
            pack([f], lo, hi)
            c = remote(packed[f].at[pl.ds(lo, hi - lo)], pool_mine[f].at[pl.ds(half + lo, hi - lo)], across)
            c.start()
            sent.append(c)
            crossing[f].append(c)

    def shift_rows(numbers, shift, source_ref, slot, write):
        for s, r in enumerate(numbers):
            for i in range(span):
                u = look[r, i]
                stage[slot, i, s:s + 1, :] = source_ref[pl.ds(u, 1), :]
        rem = shift & (LANES - 1)
        pick = (lane - rem) & (LANES - 1)
        low = lane < rem
        turned = [
            jnp.take_along_axis(stage[slot, i], pick, axis=1, mode="promise_in_bounds") for i in range(span)
        ]
        x = [turned[0]] + [jnp.where(low, turned[j - 1], turned[j]) for j in range(1, span)]
        write(x)

    def shift_plane(f, source_ref, p):
        def one(tile, slot):
            r = pl.ds(pl.multiple_of(tile * SUB, SUB), SUB)
            below = pl.ds(pl.multiple_of(SUB + tile * SUB, SUB), SUB)

            def write(x):
                right = [pltpu.roll(v, 1, 1) for v in x[:-1]]
                left = [pltpu.roll(v, LANES - 1, 1) for v in x[1:]]
                for c in range(cols):
                    cs = pl.ds(c * LANES, LANES)
                    mid = x[c + 1]
                    prev = jnp.where(lane == 0, right[c], right[c + 1])
                    nxt = jnp.where(lane == LANES - 1, left[c + 1], left[c])
                    sh[p, below, cs] = mid
                    out[p, r, cs] = mid + AZIMUTH_COEF * (nxt + prev - 2.0 * mid)

            numbers = [tile * SUB + s for s in range(SUB)]
            shift_rows(numbers, row_offsets(numbers), source_ref, slot, write)

        def pair(k, carry):
            one(2 * k, 0)
            one(2 * k + 1, 1)
            return carry

        lax.fori_loop(0, tiles // 2, pair, 0)

    def send_edges(f):
        ps = pl.ds(polar * f, polar)
        got = []
        for side in range(2):
            c = remote(eo.at[side, ps], ei.at[1 - side, ps], rad_at(-1 if side == 0 else 1))
            goes, comes = (inner, outer) if side == 0 else (outer, inner)
            pl.when(goes)(c.start)
            chained.append((goes, c))
            got.append((comes, c))
        return got

    def take_edges(f, got):
        for comes, c in got:
            pl.when(comes)(c.wait_recv)
        for h in range(polar):
            p = polar * f + h
            sh[p, SUB - 1:SUB, :] = jnp.where(rad > 0, ei[0, p], 0.0)
            sh[p, SUB + rows:SUB + rows + 1, :] = jnp.where(rad < n_rad - 1, ei[1, p], 0.0)

    def smooth(f, h):
        p = polar * f + h
        for tile in range(tiles):
            top = SUB + tile * SUB
            r = pl.ds(tile * SUB, SUB)
            mid = sh[p, top:top + SUB, :]
            up = sh[p, top - 1:top + SUB - 1, :]
            down = sh[p, top + 1:top + SUB + 1, :]
            new = out[p, r, :] + visc[h, r, :] * (down + up - 2.0 * mid)
            if f == energy:
                new = new + heat[h, r, :]
            out[p, r, :] = new

    def forward(f):
        i = order.index(f)
        onward = []
        for c, lo, hi in zip(crossing[f], cuts[f], cuts[f][1:]):
            c.wait_recv()
            at = pl.ds(half + lo, hi - lo)
            c = remote(pool_mine[f].at[at], pool_other[f].at[at], sibling)
            c.start()
            sent.append(c)
            onward.append(c)
        own_mine[i].wait()
        to_mine[i].wait_recv()
        return onward

    def other_ready(f, onward):
        i = order.index(f)
        own_other[i].wait()
        to_other[i].wait_recv()
        for c in onward:
            c.wait_recv()

    def work(f):
        onward = forward(f)
        shift_plane(f, pool_mine[f], polar * f + core)
        other_ready(f, onward)
        shift_plane(f, pool_other[f], polar * f + 1 - core)
        for h in range(polar):
            p = polar * f + h
            eo[0, p] = sh[p, SUB:SUB + 1, :]
            eo[1, p] = sh[p, SUB + rows - 1:SUB + rows, :]
        return send_edges(f)

    def finish(f, got):
        take_edges(f, got)
        for h in range(polar):
            smooth(f, h)

    def flush(but=()):
        for goes, c in chained:
            pl.when(goes)(c.wait_send)
        for c in sent:
            if not any(c is b for b in but):
                c.wait_send()
        sent[:] = but
        chained.clear()

    early_at = pl.ds(half, n_early)

    def early_edges():
        crossing_early.wait_recv()
        onward = remote(early_mine.at[early_at], early_other.at[early_at], sibling)
        onward.start()
        sent.append(onward)
        numbers = [0, rows - 1]
        for c in own_early:
            c.wait()
        for c in to_early:
            c.wait_recv()
        copies = [local(early_mine.at[early_at], pool_mine[last].at[early_at])]
        for ref, hh in ((early_mine, core), (early_other, 1 - core)):
            p = polar * last + hh
            if ref is early_other:
                onward.wait_recv()
                copies.append(local(early_other.at[early_at], pool_other[last].at[early_at]))

            def write(x):
                for c in range(cols):
                    cs = pl.ds(c * LANES, LANES)
                    eo[0, p, :, cs] = x[c + 1][:1]
                    eo[1, p, :, cs] = x[c + 1][1:2]

            shift_rows(numbers, row_offsets(numbers), ref, 0, write)
        got = send_edges(last)
        for c in copies:
            c.wait()
        return got

    own_pack = first_pack
    take_copy.wait()
    pack_ready(dust)
    pack_send(dust)
    own_pack = first_pack + [local(source.at[polar * f + core], gathered[f].at[mine]) for f in order[2:]]
    for c in to_pack[2:]:
        c.start()
    look_copy.wait()
    pack_ready(energy)
    pack_send(energy)
    own_mine, own_other = [], []

    def fill_pools(i):
        f = order[i]
        to_mine[i].start()
        to_other[i].start()
        own_mine.append(local(source.at[polar * f + core], pool_mine[f].at[mine]))
        own_other.append(local(source.at[polar * f + 1 - core], pool_other[f].at[mine]))

    fill_pools(0)
    params = [local(visc_in, visc), local(absorb_in, absorb)]
    pack_ready(last)
    pack([last], 0, n_early)
    crossing_early = remote(packed[last].at[pl.ds(0, n_early)], early_mine.at[early_at], across)
    crossing_early.start()
    sent.append(crossing_early)
    for i in range(2, fields - 1):
        pack_ready(order[i])
        pack_send(order[i])
        fill_pools(i - 1)
    own_early = [
        local(source.at[polar * last + core], early_mine.at[mine]),
        local(source.at[polar * last + 1 - core], early_other.at[mine]),
    ]
    for c in to_early:
        c.start()
    pack_send(last)
    for i in range(fields - 2, fields):
        fill_pools(i)
    for c in params:
        c.wait()

    finish(dust, work(dust))

    row = lax.broadcasted_iota(jnp.int32, (SUB, width), 0)
    for h in range(polar):
        run_last = jnp.zeros((1, width), jnp.float32)
        for t in range(tiles):
            r = pl.ds(t * SUB, SUB)
            step = 2.0 * absorb[h, r, :] * out[polar * dust + h, r, :] / total_rows
            run = step
            for k in (1, 2, 4):
                run = run + jnp.where(row >= k, pltpu.roll(run, k, 0), 0.0)
            run = run + run_last
            depth[h, r, :] = run - 0.5 * step
            run_last = run[SUB - 1:]
        tot_out[0, h] = run_last
    over = (used > cap).astype(jnp.float32)[:1]
    for c in range(cols):
        tot_out[0, polar, :, pl.ds(c * LANES, LANES)] = over

    hops = []

    def scan_send():
        i = len(hops)
        peer, upper = rad_pair(i)
        c = remote(tot_out.at[i], tot_in.at[i], peer)
        c.start()
        sent.append(c)
        hops.append((c, upper))

    def scan_take():
        i = len(hops) - 1
        hops[i][0].wait_recv()
        tot_out[i + 1] = tot_out[i] + tot_in[i]

    def irradiate():
        for h in range(polar):
            carried = jnp.where(hops[0][1] == 1, tot_in[0, h], 0.0)
            for i in range(1, n_scan):
                carried = carried + jnp.where(hops[i][1] == 1, tot_in[i, h], 0.0)
            for t in range(tiles):
                r = pl.ds(t * SUB, SUB)
                radius = (rad * rows + t * SUB + row).astype(jnp.float32) + 0.5
                flux = 1.0 / (1.0 + radius / total_rows)
                depth[h, r, :] = depth[h, r, :] + carried
                heat[h, r, :] = flux * jnp.exp(-depth[h, r, :])
        flag[0] = jnp.max(tot_out[n_scan, polar])

    scan_send()
    pending = []
    for f in order[1:-1]:
        if f == order[2]:
            last_edges = early_edges()
        pending.append((f, work(f)))
        if len(hops) < n_scan:
            scan_take()
            scan_send()
            ready = [w for w in pending[:-1] if w[0] != energy]
        else:
            if energy in [w[0] for w in pending]:
                scan_take()
                irradiate()
            ready = pending[:-1]
        for w in ready:
            finish(*w)
            pending.remove(w)
    take_edges(last, last_edges)
    flush(crossing[last])
    onward = forward(last)
    for w in pending:
        finish(*w)
    shift_plane(last, pool_mine[last], polar * last + core)
    smooth(last, core)
    other_ready(last, onward)
    shift_plane(last, pool_other[last], polar * last + 1 - core)
    smooth(last, 1 - core)
    flush()


def fast(n_rad, n_az, state, offsets, viscosity, absorb):
    fields, polar, rows, width = state.shape
    planes = fields * polar
    cols = width // LANES
    units = rows * cols
    cap = units * 2 * 11 // 16 // 16 * 16
    n_early = 4 * cols
    n_scan = (n_rad - 1).bit_length()
    n_sems = 9 * fields + 4 + n_scan
    f32, i32 = jnp.float32, jnp.int32
    vm = pl.BlockSpec(memory_space=pltpu.VMEM)
    sm = pl.BlockSpec(memory_space=pltpu.SMEM)
    hbm = pl.BlockSpec(memory_space=pl.ANY)
    source = state.reshape(planes, rows // SUB, SUB, cols, LANES).transpose(0, 1, 3, 2, 4).reshape(planes, units, LANES)
    moved, local, flag = pl.pallas_call(
        functools.partial(fast_kernel, n_rad, n_az, cap),
        out_shape=(
            pltpu.VMEM((planes, rows, width), f32),
            pltpu.VMEM((polar, rows, width), f32),
            jax.ShapeDtypeStruct((1,), f32),
        ),
        in_specs=[hbm, sm, hbm, hbm],
        out_specs=(vm, vm, sm),
        scratch_shapes=[
            pltpu.VMEM((polar, rows, width), f32),
            pltpu.VMEM((polar, rows, width), f32),
            pltpu.VMEM((polar, rows, width), f32),
            [pltpu.VMEM((2 * units, LANES), f32)] * fields,
            [pltpu.VMEM((cap, LANES), f32)] * fields,
            [pltpu.VMEM((2 * units + cap, LANES), f32)] * fields,
            [pltpu.VMEM((2 * units + cap, LANES), f32)] * fields,
            pltpu.VMEM((2 * units + n_early, LANES), f32),
            pltpu.VMEM((2 * units + n_early, LANES), f32),
            pltpu.VMEM((2, cols + 2, SUB, LANES), f32),
            pltpu.VMEM((planes, rows + 2 * SUB, width), f32),
            pltpu.VMEM((2, planes, 1, width), f32),
            pltpu.VMEM((2, planes, 1, width), f32),
            pltpu.VMEM((n_scan + 1, polar + 1, 1, width), f32),
            pltpu.VMEM((n_scan, polar + 1, 1, width), f32),
            pltpu.VMEM((SUB, LANES), i32),
            pltpu.VMEM((rows, LANES), i32),
            pltpu.SMEM((SUB, LANES), i32),
            pltpu.SMEM((rows, LANES), i32),
            pltpu.SemaphoreType.DMA((n_sems,)),
            pltpu.SemaphoreType.DMA((n_sems,)),
            pltpu.SemaphoreType.DMA((3 * fields + 8,)),
        ],
        compiler_params=pltpu.CompilerParams(
            collective_id=1, has_side_effects=True, vmem_limit_bytes=40 * 2**20
        ),
    )(source, offsets, viscosity, absorb)
    return moved, local, flag[0]


def body(n_rad, n_az, state, offsets, viscosity, absorb):
    args = (state, offsets, viscosity, absorb)
    if n_az != 4 or state.shape[1] != 2 or n_rad not in (2, 4, 8, 16):
        moved, local = full(n_rad, n_az, *args)
    else:
        moved, local, flag = fast(n_rad, n_az, *args)
        moved, local = lax.cond(
            flag > 0, lambda m, d: tuple(full(n_rad, n_az, *args)), lambda m, d: (m, d), moved, local
        )
    return moved.reshape(state.shape), local


def solution(mesh):
    in_specs = (P(None, None, "rad", "az"), P("rad"), P(None, "rad", "az"), P(None, "rad", "az"))
    out_specs = (P(None, None, "rad", "az"), P(None, "rad", "az"))
    f = functools.partial(body, mesh.shape["rad"], mesh.shape["az"])
    return jax.shard_map(f, mesh=mesh, in_specs=in_specs, out_specs=out_specs, check_vma=False)
```

```python
import functools

import jax
import jax.numpy as jnp
from jax import lax
from jax.experimental import pallas as pl
from jax.experimental.pallas import tpu as pltpu
from jax.sharding import PartitionSpec as P

AZIMUTH_COEF = 0.1
LANES = 128
SUB = 8
LANE_BITS = 7
SUB_BITS = 3


def tail_planes(rest):
    cuts = [0, rest // 2, rest]
    return [(a, b - a) for a, b in zip(cuts, cuts[1:]) if b > a]


def kernel(n_rad, n_az, n_local, source, offs, visc_in, absorb_in, out, depth,
           visc, absorb, heat, state, buf, sh, eo, ei, tot_out, tot_in, ss, rs, ls):
    groups = n_az // 2
    rad = lax.axis_index("rad")
    az = lax.axis_index("az")
    core = lax.rem(az, 2)
    sibling = {"az": az + 1 - 2 * core}
    planes, rows, width = state.shape
    cols = width // LANES
    tiles = rows // SUB
    dust = planes - 2
    rest = dust
    total_rows = rows * n_rad

    def rad_at(k):
        return {"rad": lax.rem(rad + k + n_rad, n_rad)}

    def az_at(k):
        return {"az": lax.rem(az + 2 * k, n_az)}

    count = [0]

    def remote(src, dst, device):
        i = count[0]
        count[0] += 1
        return pltpu.make_async_remote_copy(
            src_ref=src, dst_ref=dst, send_sem=ss.at[i], recv_sem=rs.at[i],
            device_id=device, device_id_type=pl.DeviceIdType.MESH,
        )

    fetch = pltpu.make_async_copy(source, state, ls.at[0])
    fetches = [fetch] + [
        pltpu.make_async_copy(a, b, ls.at[n_local + i])
        for i, (a, b) in enumerate(((visc_in, visc), (absorb_in, absorb)))
    ]
    inner, outer = rad > 0, rad < n_rad - 1
    ei[...] = jnp.zeros_like(ei)
    tot_in[...] = jnp.zeros_like(tot_in)
    peers = [az_at(k) for k in range(1, groups)] + [sibling]
    barrier = pltpu.get_barrier_semaphore()
    for there, k in ((inner, -1), (outer, 1)):
        @pl.when(there)
        def _():
            pl.semaphore_signal(barrier, inc=1, device_id=rad_at(k), device_id_type=pl.DeviceIdType.MESH)
    for peer in peers:
        pl.semaphore_signal(barrier, inc=1, device_id=peer, device_id_type=pl.DeviceIdType.MESH)
    senders = len(peers)
    d = 1
    while d < n_rad:
        if d > 1:
            @pl.when(rad >= d)
            def _():
                pl.semaphore_signal(barrier, inc=1, device_id=rad_at(-d), device_id_type=pl.DeviceIdType.MESH)
            senders = senders + (rad + d < n_rad).astype(jnp.int32)
        d *= 2
    pl.semaphore_wait(barrier, senders + inner.astype(jnp.int32) + outer.astype(jnp.int32))

    pieces = [(dust, 2, 0, rows)]
    edge_tiles = [0, tiles - 1]
    for t in edge_tiles + list(range(1, tiles - 2)):
        pieces.append((0, rest, t * SUB, SUB))
    tail = tail_planes(rest)
    for p0, np_ in tail:
        pieces.append((p0, np_, (tiles - 2) * SUB, SUB))

    sent, chained = [], []
    across, beside = [], []
    for p0, np_, r0, nr in pieces:
        ps, rws = pl.ds(p0, np_), pl.ds(r0, nr)
        across.append([remote(source.at[ps, rws], buf.at[2 * k - 1, ps, rws], az_at(k)) for k in range(1, groups)])
        beside.append(remote(source.at[ps, rws], buf.at[0, ps, rws], sibling))
        for c in across[-1]:
            c.start()
            sent.append(c)
    for c in beside:
        c.start()
        sent.append(c)

    def arrive(i):
        p0, np_, r0, nr = pieces[i]
        ps, rws = pl.ds(p0, np_), pl.ds(r0, nr)
        forwards = []
        for k in range(1, groups):
            across[i][k - 1].wait_recv()
            f = remote(buf.at[2 * k - 1, ps, rws], buf.at[2 * k, ps, rws], sibling)
            f.start()
            sent.append(f)
            forwards.append(f)
        beside[i].wait_recv()
        for f in forwards:
            f.wait_recv()

    lane = lax.broadcasted_iota(jnp.int32, (SUB, LANES), 1)

    def shift_tile(tile, p0, np_):
        r = pl.ds(tile * SUB, SUB)
        sub = lax.broadcasted_iota(jnp.int32, (SUB, LANES), 0)
        amount = jnp.full((SUB, LANES), offs[tile * SUB], jnp.int32)
        for k in range(1, SUB):
            amount = jnp.where(sub == k, offs[tile * SUB + k], amount)
        block = amount // width
        within = amount - block * width
        column = within // LANES
        rem = within - column * LANES
        pick = (lane - rem) & (LANES - 1)
        low = lane < rem

        def one(p, carry):
            def load(d, c):
                cs = pl.ds(c * LANES, LANES)
                if d == 0:
                    return state[p, r, cs]
                if d % 2 == 0:
                    return buf[d - 1, p, r, cs]
                slot = jnp.where(core == 1, d, (d + 2) % n_az)
                return buf[slot - 1, p, r, cs]

            line = []
            for move, c in [(1, c) for c in range(cols)] + [(0, c) for c in range(cols)] + [(-1, 0)]:
                value = load(move % n_az, c)
                for b in range(1, n_az):
                    value = jnp.where(block == b, load((b + move) % n_az, c), value)
                line.append(value)
            step = cols // 2
            while step:
                chosen = (column & step) != 0
                line = [jnp.where(chosen, line[i - step], line[i]) for i in range(step, len(line))]
                step //= 2
            turned = [jnp.take_along_axis(v, pick, axis=1, mode="promise_in_bounds") for v in line]
            x = [turned[0]] + [jnp.where(low, turned[j - 1], turned[j]) for j in range(1, len(turned))]
            right = [pltpu.roll(v, 1, 1) for v in x[:-1]]
            left = [pltpu.roll(v, LANES - 1, 1) for v in x[1:]]
            for c in range(cols):
                cs = pl.ds(c * LANES, LANES)
                mid = x[c + 1]
                prev = jnp.where(lane == 0, right[c], right[c + 1])
                nxt = jnp.where(lane == LANES - 1, left[c + 1], left[c])
                sh[p, pl.ds(SUB + tile * SUB, SUB), cs] = mid
                out[p, r, cs] = mid + AZIMUTH_COEF * (nxt + prev - 2.0 * mid)
                if tile == 0:
                    eo[0, p, :, cs] = mid[:1]
                if tile == tiles - 1:
                    eo[1, p, :, cs] = mid[SUB - 1:]
            return carry

        lax.fori_loop(p0, p0 + np_, one, 0)

    hops = []

    def scan_send():
        i = len(hops)
        d = 1 << i
        if d < n_rad:
            c = remote(tot_out.at[i], tot_in.at[i], rad_at(d))
            goes = rad + d < n_rad
            pl.when(goes)(c.start)
            chained.append((goes, c))
            hops.append(c)

    def scan_take():
        i = len(hops) - 1
        pl.when(rad >= 1 << i)(hops[i].wait_recv)
        tot_out[i + 1] = tot_out[i] + tot_in[i]

    def send_edge(side, p0, np_):
        ps = pl.ds(p0, np_)
        c = remote(eo.at[side, ps], ei.at[1 - side, ps], rad_at(-1 if side == 0 else 1))
        goes, comes = (inner, outer) if side == 0 else (outer, inner)
        pl.when(goes)(c.start)
        chained.append((goes, c))
        return comes, c

    def edge_wait(edge):
        pl.when(edge[0])(edge[1].wait_recv)

    def place_edges(p0, np_):
        def one(p, carry):
            sh[p, SUB - 1:SUB, :] = jnp.where(rad > 0, ei[0, p], 0.0)
            sh[p, SUB + rows:SUB + rows + 1, :] = jnp.where(rad < n_rad - 1, ei[1, p], 0.0)
            return carry

        lax.fori_loop(p0, p0 + np_, one, 0)

    def smooth(tile, p0, np_):
        top = SUB + tile * SUB

        def one(p, carry):
            r = pl.ds(tile * SUB, SUB)
            mid = sh[p, top:top + SUB, :]
            up = sh[p, top - 1:top + SUB - 1, :]
            down = sh[p, top + 1:top + SUB + 1, :]
            out[p, r, :] = out[p, r, :] + visc[lax.rem(p, 2), r, :] * (down + up - 2.0 * mid)
            return carry

        lax.fori_loop(p0, p0 + np_, one, 0)

    for c in fetches:
        c.start()
    arrive(0)
    for c in fetches:
        c.wait()
    for t in range(tiles):
        shift_tile(t, dust, 2)
    edges = [send_edge(s, dust, 2) for s in (0, 1)]
    for e in edges:
        edge_wait(e)
    place_edges(dust, 2)
    for t in range(tiles):
        smooth(t, dust, 2)

    row = lax.broadcasted_iota(jnp.int32, (SUB, width), 0)
    for h in range(2):
        base = jnp.zeros((1, width), jnp.float32)
        for t in range(tiles):
            r = pl.ds(t * SUB, SUB)
            step = 2.0 * absorb[h, r, :] * out[dust + h, r, :] / total_rows
            run = step
            for k in (1, 2, 4):
                run = run + jnp.where(row >= k, pltpu.roll(run, k, 0), 0.0)
            run = run + base
            depth[h, r, :] = run - 0.5 * step
            base = run[SUB - 1:]
        tot_out[0, h] = base
    scan_send()
    arrive(1)
    shift_tile(0, 0, rest)
    edge_in = send_edge(0, 0, rest)
    scan_take()
    scan_send()
    arrive(2)
    shift_tile(tiles - 1, 0, rest)
    edge_out = send_edge(1, 0, rest)

    scan_take()
    while 1 << len(hops) < n_rad:
        scan_send()
        scan_take()
    for h in range(2):
        carried = tot_in[0, h]
        for i in range(1, len(hops)):
            carried = carried + tot_in[i, h]
        for t in range(tiles):
            r = pl.ds(t * SUB, SUB)
            radius = (rad * rows + t * SUB + row).astype(jnp.float32) + 0.5
            flux = 1.0 / (1.0 + radius / total_rows)
            depth[h, r, :] = depth[h, r, :] + carried
            heat[h, r, :] = flux * jnp.exp(-depth[h, r, :])

    def warm(tile):
        r = pl.ds(tile * SUB, SUB)
        for h in range(2):
            out[rest - 2 + h, r, :] = out[rest - 2 + h, r, :] + heat[h, r, :]

    edge_wait(edge_in)
    edge_wait(edge_out)
    place_edges(0, rest)
    i = 3
    for t in range(1, tiles - 2):
        arrive(i)
        shift_tile(t, 0, rest)
        smooth(t - 1, 0, rest)
        warm(t - 1)
        i += 1
    first = max(tiles - 3, 0)
    for p0, np_ in tail:
        arrive(i)
        shift_tile(tiles - 2, p0, np_)
        for t in range(first, tiles):
            smooth(t, p0, np_)
            if p0 + np_ == rest:
                warm(t)
        i += 1
    for goes, c in chained:
        pl.when(goes)(c.wait_send)
    for c in sent:
        c.wait_send()


def full(n_rad, n_az, state, offsets, viscosity, absorb):
    fields, polar, rows, width = state.shape
    planes = fields * polar
    groups = n_az // 2
    tiles = rows // SUB
    n_tail = len(tail_planes(planes - 2))
    n_pieces = 1 + 2 + max(tiles - 3, 0) + n_tail
    n_scan = (n_rad - 1).bit_length()
    n_local = 1
    n_sems = n_pieces * (2 * (groups - 1) + 1) + 4 + n_scan
    f32 = jnp.float32
    vm = pl.BlockSpec(memory_space=pltpu.VMEM)
    hbm = pl.BlockSpec(memory_space=pl.ANY)
    moved, local = pl.pallas_call(
        functools.partial(kernel, n_rad, n_az, n_local),
        out_shape=(
            pltpu.VMEM((planes, rows, width), f32),
            pltpu.VMEM((polar, rows, width), f32),
        ),
        in_specs=[hbm, pl.BlockSpec(memory_space=pltpu.SMEM), hbm, hbm],
        out_specs=(vm, vm),
        scratch_shapes=[
            pltpu.VMEM((polar, rows, width), f32),
            pltpu.VMEM((polar, rows, width), f32),
            pltpu.VMEM((polar, rows, width), f32),
            pltpu.VMEM((planes, rows, width), f32),
            pltpu.VMEM((n_az - 1, planes, rows, width), f32),
            pltpu.VMEM((planes, rows + 2 * SUB, width), f32),
            pltpu.VMEM((2, planes, 1, width), f32),
            pltpu.VMEM((2, planes, 1, width), f32),
            pltpu.VMEM((n_scan + 1, polar, 1, width), f32),
            pltpu.VMEM((n_scan, polar, 1, width), f32),
            pltpu.SemaphoreType.DMA((n_sems,)),
            pltpu.SemaphoreType.DMA((n_sems,)),
            pltpu.SemaphoreType.DMA((n_local + 2,)),
        ],
        compiler_params=pltpu.CompilerParams(
            collective_id=0, has_side_effects=True, vmem_limit_bytes=56 * 2**20
        ),
    )(state.reshape(planes, rows, width), offsets, viscosity, absorb)
    return moved, local


def fast_kernel(n_rad, n_az, cap, source, offs_in, visc_in, absorb_in, out, depth, flag,
                visc, absorb, heat, gathered, packed, pool_mine, pool_other, early_mine, early_other,
                stage, sh, eo, ei, tot_out, tot_in, take_v, look_v, take, look, offs, ss, rs, ls):
    rad = lax.axis_index("rad")
    az = lax.axis_index("az")
    core = lax.rem(az, 2)
    chip = az // 2
    sibling = {"az": az + 1 - 2 * core}
    across = {"az": lax.rem(az + 2, n_az)}
    planes, rows, width = out.shape
    polar = 2
    fields = planes // polar
    cols = width // LANES
    col_bits = cols.bit_length() - 1
    tiles = rows // SUB
    units = rows * cols
    half = 2 * units
    ring = 2 * cols
    span = cols + 2
    total_rows = rows * n_rad
    dust, energy = fields - 1, fields - 2
    order = [dust, energy] + list(range(energy))
    last = order[-1]
    n_scan = (n_rad - 1).bit_length()
    n_early = 2 * ring

    def rad_at(k):
        return {"rad": lax.rem(rad + k + n_rad, n_rad)}

    def rad_pair(i):
        d = 1 << i
        upper = lax.rem(rad // d, 2)
        return {"rad": rad + d - 2 * d * upper}, upper

    count = [0, 0]

    def remote(src, dst, device):
        i = count[0]
        count[0] += 1
        return pltpu.make_async_remote_copy(
            src_ref=src, dst_ref=dst, send_sem=ss.at[i], recv_sem=rs.at[i],
            device_id=device, device_id_type=pl.DeviceIdType.MESH,
        )

    def local(src, dst):
        i = count[1]
        count[1] += 1
        c = pltpu.make_async_copy(src, dst, ls.at[i])
        c.start()
        return c

    offs_copy = local(offs_in, offs)
    inner, outer = rad > 0, rad < n_rad - 1
    ei[...] = jnp.zeros_like(ei)
    barrier = pltpu.get_barrier_semaphore()
    for peer in [sibling, across] + [rad_pair(i)[0] for i in range(1, n_scan)]:
        pl.semaphore_signal(barrier, inc=1, device_id=peer, device_id_type=pl.DeviceIdType.MESH)
    for there, k in ((inner, -1), (outer, 1)):
        @pl.when(there)
        def _():
            pl.semaphore_signal(barrier, inc=1, device_id=rad_at(k), device_id_type=pl.DeviceIdType.MESH)

    mine = pl.ds(core * units, units)
    first_pack = [local(source.at[polar * f + core], gathered[f].at[mine]) for f in order[:2]]

    pl.semaphore_wait(barrier, 2 + n_scan - 1 + inner.astype(jnp.int32) + outer.astype(jnp.int32))

    sent, chained = [], []
    to_pack = [remote(source.at[polar * f + 1 - core], gathered[f].at[mine], sibling) for f in order]
    to_mine = [remote(source.at[polar * f + 1 - core], pool_mine[f].at[mine], sibling) for f in order]
    to_other = [remote(source.at[polar * f + core], pool_other[f].at[mine], sibling) for f in order]
    to_early = [
        remote(source.at[polar * last + 1 - core], early_mine.at[mine], sibling),
        remote(source.at[polar * last + core], early_other.at[mine], sibling),
    ]
    sent += to_pack + to_mine + to_other + to_early
    for c in to_pack[:2]:
        c.start()
    lane = lax.broadcasted_iota(jnp.int32, (SUB, LANES), 1)
    sub = lax.broadcasted_iota(jnp.int32, (SUB, LANES), 0)

    def row_offsets(numbers):
        amount = jnp.full((SUB, LANES), offs[numbers[0]], jnp.int32)
        for k in range(1, len(numbers)):
            amount = jnp.where(sub == k, offs[numbers[k]], amount)
        return amount

    def block_unit(b):
        return (b >> col_bits) * units + (b & (cols - 1)) * SUB

    offs_copy.wait()
    shifts = [row_offsets([t * SUB + k for k in range(SUB)]) for t in range(tiles)]
    leads, manys, befores = [], [], []
    used = jnp.zeros((SUB, LANES), jnp.int32)
    for off in shifts:
        lead = jnp.where(off == 0, ring - 1, jnp.where(off < 2 * width, (2 * width - 1 - off) >> LANE_BITS, 0))
        many = jnp.where(off < 2 * width, ring - lead, jnp.minimum(((4 * width - off) >> LANE_BITS) + 1, ring))
        many = jnp.where(off == 0, 2, many)
        run = many
        for k in (1, 2, 4):
            run = run + jnp.where(sub >= k, pltpu.roll(run, k, 0), 0)
        leads.append(lead)
        manys.append(many)
        befores.append(run - many + used)
        used = used + jnp.broadcast_to(run[SUB - 1:], (SUB, LANES))
    top_many = jnp.broadcast_to(manys[0][:1], (SUB, LANES))
    bottom_many = jnp.broadcast_to(manys[-1][SUB - 1:], (SUB, LANES))
    bases = []
    for t in range(tiles):
        base = befores[t] + bottom_many
        if t == 0:
            base = jnp.where(sub == 0, 0, base)
        if t == tiles - 1:
            base = jnp.where(sub == SUB - 1, top_many, base)
        bases.append(base)
    for q in range(-(-cap // LANES)):
        j = q * LANES + lane
        place = jnp.zeros((SUB, LANES), jnp.int32)
        ahead = jnp.zeros((SUB, LANES), jnp.int32)
        for t in range(tiles):
            held = (j >= bases[t]) & (j < bases[t] + manys[t])
            place = place + jnp.where(held, t * SUB * cols + sub, 0)
            ahead = ahead + jnp.where(held, leads[t] - bases[t], 0)
        for k in (4, 2, 1):
            place = place + pltpu.roll(place, k, 0)
            ahead = ahead + pltpu.roll(ahead, k, 0)
        take_v[q:q + 1, :] = (block_unit((j + ahead) & (ring - 1)) + place)[:1]
    take_copy = local(take_v, take)
    for t in range(tiles):
        b = az * cols - (shifts[t] >> LANE_BITS) - 1 + lane + 2 * ring
        near = block_unit(b & (ring - 1)) + (t * SUB * cols + sub)
        far = half + jnp.minimum(bases[t] + ((b - leads[t]) & (ring - 1)), cap - 1)
        look_v[t * SUB:(t + 1) * SUB, :] = jnp.where(((b >> (col_bits + 1)) & 1) == chip, near, far)
    look_copy = local(look_v, look)

    crossing = {f: [] for f in order}
    cuts = {f: [0, cap // 2 // SUB * SUB, cap] for f in order}
    cuts[last] = [n_early, (n_early + cap) // 2 // SUB * SUB, cap]

    def pack(some, lo, hi):
        def eight(k, carry):
            for s in range(SUB):
                u = take[k >> 4, (k & 15) * SUB + s]
                for f in some:
                    packed[f][pl.ds(k * SUB + s, 1), :] = gathered[f][pl.ds(u, 1), :]
            return carry

        lax.fori_loop(lo // SUB, hi // SUB, eight, 0)

    def pack_ready(f):
        own_pack[order.index(f)].wait()
        to_pack[order.index(f)].wait_recv()

    def pack_send(f):
        for lo, hi in zip(cuts[f], cuts[f][1:]):
            pack([f], lo, hi)
            c = remote(packed[f].at[pl.ds(lo, hi - lo)], pool_mine[f].at[pl.ds(half + lo, hi - lo)], across)
            c.start()
            sent.append(c)
            crossing[f].append(c)

    def shift_rows(numbers, shift, source_ref, slot, write):
        for s, r in enumerate(numbers):
            for i in range(span):
                u = look[r, i]
                stage[slot, i, s:s + 1, :] = source_ref[pl.ds(u, 1), :]
        rem = shift & (LANES - 1)
        pick = (lane - rem) & (LANES - 1)
        low = lane < rem
        turned = [
            jnp.take_along_axis(stage[slot, i], pick, axis=1, mode="promise_in_bounds") for i in range(span)
        ]
        x = [turned[0]] + [jnp.where(low, turned[j - 1], turned[j]) for j in range(1, span)]
        write(x)

    def shift_plane(f, source_ref, p):
        def one(tile, slot):
            r = pl.ds(pl.multiple_of(tile * SUB, SUB), SUB)
            below = pl.ds(pl.multiple_of(SUB + tile * SUB, SUB), SUB)

            def write(x):
                right = [pltpu.roll(v, 1, 1) for v in x[:-1]]
                left = [pltpu.roll(v, LANES - 1, 1) for v in x[1:]]
                for c in range(cols):
                    cs = pl.ds(c * LANES, LANES)
                    mid = x[c + 1]
                    prev = jnp.where(lane == 0, right[c], right[c + 1])
                    nxt = jnp.where(lane == LANES - 1, left[c + 1], left[c])
                    sh[p, below, cs] = mid
                    out[p, r, cs] = mid + AZIMUTH_COEF * (nxt + prev - 2.0 * mid)

            numbers = [tile * SUB + s for s in range(SUB)]
            shift_rows(numbers, row_offsets(numbers), source_ref, slot, write)

        def pair(k, carry):
            one(2 * k, 0)
            one(2 * k + 1, 1)
            return carry

        lax.fori_loop(0, tiles // 2, pair, 0)

    def send_edges(f):
        ps = pl.ds(polar * f, polar)
        got = []
        for side in range(2):
            c = remote(eo.at[side, ps], ei.at[1 - side, ps], rad_at(-1 if side == 0 else 1))
            goes, comes = (inner, outer) if side == 0 else (outer, inner)
            pl.when(goes)(c.start)
            chained.append((goes, c))
            got.append((comes, c))
        return got

    def take_edges(f, got):
        for comes, c in got:
            pl.when(comes)(c.wait_recv)
        for h in range(polar):
            p = polar * f + h
            sh[p, SUB - 1:SUB, :] = jnp.where(rad > 0, ei[0, p], 0.0)
            sh[p, SUB + rows:SUB + rows + 1, :] = jnp.where(rad < n_rad - 1, ei[1, p], 0.0)

    def smooth(f, h):
        p = polar * f + h
        for tile in range(tiles):
            top = SUB + tile * SUB
            r = pl.ds(tile * SUB, SUB)
            mid = sh[p, top:top + SUB, :]
            up = sh[p, top - 1:top + SUB - 1, :]
            down = sh[p, top + 1:top + SUB + 1, :]
            new = out[p, r, :] + visc[h, r, :] * (down + up - 2.0 * mid)
            if f == energy:
                new = new + heat[h, r, :]
            out[p, r, :] = new

    def forward(f):
        i = order.index(f)
        onward = []
        for c, lo, hi in zip(crossing[f], cuts[f], cuts[f][1:]):
            c.wait_recv()
            at = pl.ds(half + lo, hi - lo)
            c = remote(pool_mine[f].at[at], pool_other[f].at[at], sibling)
            c.start()
            sent.append(c)
            onward.append(c)
        own_mine[i].wait()
        to_mine[i].wait_recv()
        return onward

    def other_ready(f, onward):
        i = order.index(f)
        own_other[i].wait()
        to_other[i].wait_recv()
        for c in onward:
            c.wait_recv()

    def work(f):
        onward = forward(f)
        shift_plane(f, pool_mine[f], polar * f + core)
        other_ready(f, onward)
        shift_plane(f, pool_other[f], polar * f + 1 - core)
        for h in range(polar):
            p = polar * f + h
            eo[0, p] = sh[p, SUB:SUB + 1, :]
            eo[1, p] = sh[p, SUB + rows - 1:SUB + rows, :]
        return send_edges(f)

    def finish(f, got):
        take_edges(f, got)
        for h in range(polar):
            smooth(f, h)

    def flush(but=()):
        for goes, c in chained:
            pl.when(goes)(c.wait_send)
        for c in sent:
            if not any(c is b for b in but):
                c.wait_send()
        sent[:] = but
        chained.clear()

    early_at = pl.ds(half, n_early)

    def early_edges():
        crossing_early.wait_recv()
        onward = remote(early_mine.at[early_at], early_other.at[early_at], sibling)
        onward.start()
        sent.append(onward)
        numbers = [0, rows - 1]
        for c in own_early:
            c.wait()
        for c in to_early:
            c.wait_recv()
        copies = [local(early_mine.at[early_at], pool_mine[last].at[early_at])]
        for ref, hh in ((early_mine, core), (early_other, 1 - core)):
            p = polar * last + hh
            if ref is early_other:
                onward.wait_recv()
                copies.append(local(early_other.at[early_at], pool_other[last].at[early_at]))

            def write(x):
                for c in range(cols):
                    cs = pl.ds(c * LANES, LANES)
                    eo[0, p, :, cs] = x[c + 1][:1]
                    eo[1, p, :, cs] = x[c + 1][1:2]

            shift_rows(numbers, row_offsets(numbers), ref, 0, write)
        got = send_edges(last)
        for c in copies:
            c.wait()
        return got

    own_pack = first_pack
    take_copy.wait()
    pack_ready(dust)
    pack_send(dust)
    own_pack = first_pack + [local(source.at[polar * f + core], gathered[f].at[mine]) for f in order[2:]]
    for c in to_pack[2:]:
        c.start()
    look_copy.wait()
    pack_ready(energy)
    pack_send(energy)
    own_mine, own_other = [], []

    def fill_pools(i):
        f = order[i]
        to_mine[i].start()
        to_other[i].start()
        own_mine.append(local(source.at[polar * f + core], pool_mine[f].at[mine]))
        own_other.append(local(source.at[polar * f + 1 - core], pool_other[f].at[mine]))

    fill_pools(0)
    params = [local(visc_in, visc), local(absorb_in, absorb)]
    pack_ready(last)
    pack([last], 0, n_early)
    crossing_early = remote(packed[last].at[pl.ds(0, n_early)], early_mine.at[early_at], across)
    crossing_early.start()
    sent.append(crossing_early)
    for i in range(2, fields - 1):
        pack_ready(order[i])
        pack_send(order[i])
        fill_pools(i - 1)
    own_early = [
        local(source.at[polar * last + core], early_mine.at[mine]),
        local(source.at[polar * last + 1 - core], early_other.at[mine]),
    ]
    for c in to_early:
        c.start()
    pack_send(last)
    for i in range(fields - 2, fields):
        fill_pools(i)
    for c in params:
        c.wait()

    finish(dust, work(dust))

    row = lax.broadcasted_iota(jnp.int32, (SUB, width), 0)
    for h in range(polar):
        run_last = jnp.zeros((1, width), jnp.float32)
        for t in range(tiles):
            r = pl.ds(t * SUB, SUB)
            step = 2.0 * absorb[h, r, :] * out[polar * dust + h, r, :] / total_rows
            run = step
            for k in (1, 2, 4):
                run = run + jnp.where(row >= k, pltpu.roll(run, k, 0), 0.0)
            run = run + run_last
            depth[h, r, :] = run - 0.5 * step
            run_last = run[SUB - 1:]
        tot_out[0, h] = run_last
    over = (used > cap).astype(jnp.float32)[:1]
    for c in range(cols):
        tot_out[0, polar, :, pl.ds(c * LANES, LANES)] = over

    hops = []

    def scan_send():
        i = len(hops)
        peer, upper = rad_pair(i)
        c = remote(tot_out.at[i], tot_in.at[i], peer)
        c.start()
        sent.append(c)
        hops.append((c, upper))

    def scan_take():
        i = len(hops) - 1
        hops[i][0].wait_recv()
        tot_out[i + 1] = tot_out[i] + tot_in[i]

    def irradiate():
        for h in range(polar):
            carried = jnp.where(hops[0][1] == 1, tot_in[0, h], 0.0)
            for i in range(1, n_scan):
                carried = carried + jnp.where(hops[i][1] == 1, tot_in[i, h], 0.0)
            for t in range(tiles):
                r = pl.ds(t * SUB, SUB)
                radius = (rad * rows + t * SUB + row).astype(jnp.float32) + 0.5
                flux = 1.0 / (1.0 + radius / total_rows)
                depth[h, r, :] = depth[h, r, :] + carried
                heat[h, r, :] = flux * jnp.exp(-depth[h, r, :])
        flag[0] = jnp.max(tot_out[n_scan, polar])

    scan_send()
    pending = []
    for f in order[1:-1]:
        if f == order[2]:
            last_edges = early_edges()
        pending.append((f, work(f)))
        if len(hops) < n_scan:
            scan_take()
            scan_send()
            ready = [w for w in pending[:-1] if w[0] != energy]
        else:
            if energy in [w[0] for w in pending]:
                scan_take()
                irradiate()
            ready = pending[:-1]
        for w in ready:
            finish(*w)
            pending.remove(w)
    take_edges(last, last_edges)
    flush(crossing[last])
    onward = forward(last)
    for w in pending:
        finish(*w)
    shift_plane(last, pool_mine[last], polar * last + core)
    smooth(last, core)
    other_ready(last, onward)
    shift_plane(last, pool_other[last], polar * last + 1 - core)
    smooth(last, 1 - core)
    flush()


def fast(n_rad, n_az, state, offsets, viscosity, absorb):
    fields, polar, rows, width = state.shape
    planes = fields * polar
    cols = width // LANES
    units = rows * cols
    cap = units * 2 * 11 // 16 // 16 * 16
    n_early = 4 * cols
    n_scan = (n_rad - 1).bit_length()
    n_sems = 9 * fields + 4 + n_scan
    f32, i32 = jnp.float32, jnp.int32
    vm = pl.BlockSpec(memory_space=pltpu.VMEM)
    hbm = pl.BlockSpec(memory_space=pl.ANY)
    source = state.reshape(planes, rows // SUB, SUB, cols, LANES).transpose(0, 1, 3, 2, 4).reshape(planes, units, LANES)
    moved, local, flag = pl.pallas_call(
        functools.partial(fast_kernel, n_rad, n_az, cap),
        out_shape=(
            pltpu.VMEM((planes, rows, width), f32),
            pltpu.VMEM((polar, rows, width), f32),
            pltpu.SMEM((1,), f32),
        ),
        in_specs=[hbm, hbm, hbm, hbm],
        out_specs=(vm, vm, pl.BlockSpec(memory_space=pltpu.SMEM)),
        scratch_shapes=[
            pltpu.VMEM((polar, rows, width), f32),
            pltpu.VMEM((polar, rows, width), f32),
            pltpu.VMEM((polar, rows, width), f32),
            [pltpu.VMEM((2 * units, LANES), f32)] * fields,
            [pltpu.VMEM((cap, LANES), f32)] * fields,
            [pltpu.VMEM((2 * units + cap, LANES), f32)] * fields,
            [pltpu.VMEM((2 * units + cap, LANES), f32)] * fields,
            pltpu.VMEM((2 * units + n_early, LANES), f32),
            pltpu.VMEM((2 * units + n_early, LANES), f32),
            pltpu.VMEM((2, cols + 2, SUB, LANES), f32),
            pltpu.VMEM((planes, rows + 2 * SUB, width), f32),
            pltpu.VMEM((2, planes, 1, width), f32),
            pltpu.VMEM((2, planes, 1, width), f32),
            pltpu.VMEM((n_scan + 1, polar + 1, 1, width), f32),
            pltpu.VMEM((n_scan, polar + 1, 1, width), f32),
            pltpu.VMEM((SUB, LANES), i32),
            pltpu.VMEM((rows, LANES), i32),
            pltpu.SMEM((SUB, LANES), i32),
            pltpu.SMEM((rows, LANES), i32),
            pltpu.SMEM((rows,), i32),
            pltpu.SemaphoreType.DMA((n_sems,)),
            pltpu.SemaphoreType.DMA((n_sems,)),
            pltpu.SemaphoreType.DMA((3 * fields + 10,)),
        ],
        compiler_params=pltpu.CompilerParams(
            collective_id=1, has_side_effects=True, vmem_limit_bytes=61 * 2**20
        ),
    )(source, offsets, viscosity, absorb)
    return moved, local, flag[0]


def hand_out(moved, local):
    def store(a, b, x, y, sems):
        copies = [pltpu.make_async_copy(a, x, sems.at[0]), pltpu.make_async_copy(b, y, sems.at[1])]
        for c in copies:
            c.start()
        for c in copies:
            c.wait()

    hbm = pl.BlockSpec(memory_space=pl.ANY)
    vm = pl.BlockSpec(memory_space=pltpu.VMEM)
    return pl.pallas_call(
        store,
        out_shape=(pltpu.HBM(moved.shape, moved.dtype), pltpu.HBM(local.shape, local.dtype)),
        in_specs=[vm, vm],
        out_specs=(hbm, hbm),
        scratch_shapes=[pltpu.SemaphoreType.DMA((2,))],
    )(moved, local)


def body(n_rad, n_az, state, offsets, viscosity, absorb):
    args = (state, offsets, viscosity, absorb)
    if n_az != 4 or state.shape[1] != 2 or n_rad not in (2, 4, 8, 16):
        moved, local = full(n_rad, n_az, *args)
    else:
        moved, local, flag = fast(n_rad, n_az, *args)
        moved, local = lax.cond(
            flag > 0, lambda m, d: tuple(full(n_rad, n_az, *args)), lambda m, d: (m, d), moved, local
        )
    moved, local = hand_out(moved, local)
    return moved.reshape(state.shape), local


def solution(mesh):
    in_specs = (P(None, None, "rad", "az"), P("rad"), P(None, "rad", "az"), P(None, "rad", "az"))
    out_specs = (P(None, None, "rad", "az"), P(None, "rad", "az"))
    f = functools.partial(body, mesh.shape["rad"], mesh.shape["az"])
    return jax.shard_map(f, mesh=mesh, in_specs=in_specs, out_specs=out_specs, check_vma=False)
```

```python
import functools

import jax
import jax.numpy as jnp
from jax import lax
from jax.experimental import pallas as pl
from jax.experimental.pallas import tpu as pltpu
from jax.sharding import PartitionSpec as P

AZIMUTH_COEF = 0.1
LANES = 128
SUB = 8
LANE_BITS = 7
SUB_BITS = 3


def tail_planes(rest):
    cuts = [0, rest // 2, rest]
    return [(a, b - a) for a, b in zip(cuts, cuts[1:]) if b > a]


def kernel(n_rad, n_az, n_local, source, offs, visc_in, absorb_in, out, depth,
           visc, absorb, heat, state, buf, sh, eo, ei, tot_out, tot_in, ss, rs, ls):
    groups = n_az // 2
    rad = lax.axis_index("rad")
    az = lax.axis_index("az")
    core = lax.rem(az, 2)
    sibling = {"az": az + 1 - 2 * core}
    planes, rows, width = state.shape
    cols = width // LANES
    tiles = rows // SUB
    dust = planes - 2
    rest = dust
    total_rows = rows * n_rad

    def rad_at(k):
        return {"rad": lax.rem(rad + k + n_rad, n_rad)}

    def az_at(k):
        return {"az": lax.rem(az + 2 * k, n_az)}

    count = [0]

    def remote(src, dst, device):
        i = count[0]
        count[0] += 1
        return pltpu.make_async_remote_copy(
            src_ref=src, dst_ref=dst, send_sem=ss.at[i], recv_sem=rs.at[i],
            device_id=device, device_id_type=pl.DeviceIdType.MESH,
        )

    fetch = pltpu.make_async_copy(source, state, ls.at[0])
    fetches = [fetch] + [
        pltpu.make_async_copy(a, b, ls.at[n_local + i])
        for i, (a, b) in enumerate(((visc_in, visc), (absorb_in, absorb)))
    ]
    inner, outer = rad > 0, rad < n_rad - 1
    ei[...] = jnp.zeros_like(ei)
    tot_in[...] = jnp.zeros_like(tot_in)
    peers = [az_at(k) for k in range(1, groups)] + [sibling]
    barrier = pltpu.get_barrier_semaphore()
    for there, k in ((inner, -1), (outer, 1)):
        @pl.when(there)
        def _():
            pl.semaphore_signal(barrier, inc=1, device_id=rad_at(k), device_id_type=pl.DeviceIdType.MESH)
    for peer in peers:
        pl.semaphore_signal(barrier, inc=1, device_id=peer, device_id_type=pl.DeviceIdType.MESH)
    senders = len(peers)
    d = 1
    while d < n_rad:
        if d > 1:
            @pl.when(rad >= d)
            def _():
                pl.semaphore_signal(barrier, inc=1, device_id=rad_at(-d), device_id_type=pl.DeviceIdType.MESH)
            senders = senders + (rad + d < n_rad).astype(jnp.int32)
        d *= 2
    pl.semaphore_wait(barrier, senders + inner.astype(jnp.int32) + outer.astype(jnp.int32))

    pieces = [(dust, 2, 0, rows)]
    edge_tiles = [0, tiles - 1]
    for t in edge_tiles + list(range(1, tiles - 2)):
        pieces.append((0, rest, t * SUB, SUB))
    tail = tail_planes(rest)
    for p0, np_ in tail:
        pieces.append((p0, np_, (tiles - 2) * SUB, SUB))

    sent, chained = [], []
    across, beside = [], []
    for p0, np_, r0, nr in pieces:
        ps, rws = pl.ds(p0, np_), pl.ds(r0, nr)
        across.append([remote(source.at[ps, rws], buf.at[2 * k - 1, ps, rws], az_at(k)) for k in range(1, groups)])
        beside.append(remote(source.at[ps, rws], buf.at[0, ps, rws], sibling))
        for c in across[-1]:
            c.start()
            sent.append(c)
    for c in beside:
        c.start()
        sent.append(c)

    def arrive(i):
        p0, np_, r0, nr = pieces[i]
        ps, rws = pl.ds(p0, np_), pl.ds(r0, nr)
        forwards = []
        for k in range(1, groups):
            across[i][k - 1].wait_recv()
            f = remote(buf.at[2 * k - 1, ps, rws], buf.at[2 * k, ps, rws], sibling)
            f.start()
            sent.append(f)
            forwards.append(f)
        beside[i].wait_recv()
        for f in forwards:
            f.wait_recv()

    lane = lax.broadcasted_iota(jnp.int32, (SUB, LANES), 1)

    def shift_tile(tile, p0, np_):
        r = pl.ds(tile * SUB, SUB)
        sub = lax.broadcasted_iota(jnp.int32, (SUB, LANES), 0)
        amount = jnp.full((SUB, LANES), offs[tile * SUB], jnp.int32)
        for k in range(1, SUB):
            amount = jnp.where(sub == k, offs[tile * SUB + k], amount)
        block = amount // width
        within = amount - block * width
        column = within // LANES
        rem = within - column * LANES
        pick = (lane - rem) & (LANES - 1)
        low = lane < rem

        def one(p, carry):
            def load(d, c):
                cs = pl.ds(c * LANES, LANES)
                if d == 0:
                    return state[p, r, cs]
                if d % 2 == 0:
                    return buf[d - 1, p, r, cs]
                slot = jnp.where(core == 1, d, (d + 2) % n_az)
                return buf[slot - 1, p, r, cs]

            line = []
            for move, c in [(1, c) for c in range(cols)] + [(0, c) for c in range(cols)] + [(-1, 0)]:
                value = load(move % n_az, c)
                for b in range(1, n_az):
                    value = jnp.where(block == b, load((b + move) % n_az, c), value)
                line.append(value)
            step = cols // 2
            while step:
                chosen = (column & step) != 0
                line = [jnp.where(chosen, line[i - step], line[i]) for i in range(step, len(line))]
                step //= 2
            turned = [jnp.take_along_axis(v, pick, axis=1, mode="promise_in_bounds") for v in line]
            x = [turned[0]] + [jnp.where(low, turned[j - 1], turned[j]) for j in range(1, len(turned))]
            right = [pltpu.roll(v, 1, 1) for v in x[:-1]]
            left = [pltpu.roll(v, LANES - 1, 1) for v in x[1:]]
            for c in range(cols):
                cs = pl.ds(c * LANES, LANES)
                mid = x[c + 1]
                prev = jnp.where(lane == 0, right[c], right[c + 1])
                nxt = jnp.where(lane == LANES - 1, left[c + 1], left[c])
                sh[p, pl.ds(SUB + tile * SUB, SUB), cs] = mid
                out[p, r, cs] = mid + AZIMUTH_COEF * (nxt + prev - 2.0 * mid)
                if tile == 0:
                    eo[0, p, :, cs] = mid[:1]
                if tile == tiles - 1:
                    eo[1, p, :, cs] = mid[SUB - 1:]
            return carry

        lax.fori_loop(p0, p0 + np_, one, 0)

    hops = []

    def scan_send():
        i = len(hops)
        d = 1 << i
        if d < n_rad:
            c = remote(tot_out.at[i], tot_in.at[i], rad_at(d))
            goes = rad + d < n_rad
            pl.when(goes)(c.start)
            chained.append((goes, c))
            hops.append(c)

    def scan_take():
        i = len(hops) - 1
        pl.when(rad >= 1 << i)(hops[i].wait_recv)
        tot_out[i + 1] = tot_out[i] + tot_in[i]

    def send_edge(side, p0, np_):
        ps = pl.ds(p0, np_)
        c = remote(eo.at[side, ps], ei.at[1 - side, ps], rad_at(-1 if side == 0 else 1))
        goes, comes = (inner, outer) if side == 0 else (outer, inner)
        pl.when(goes)(c.start)
        chained.append((goes, c))
        return comes, c

    def edge_wait(edge):
        pl.when(edge[0])(edge[1].wait_recv)

    def place_edges(p0, np_):
        def one(p, carry):
            sh[p, SUB - 1:SUB, :] = jnp.where(rad > 0, ei[0, p], 0.0)
            sh[p, SUB + rows:SUB + rows + 1, :] = jnp.where(rad < n_rad - 1, ei[1, p], 0.0)
            return carry

        lax.fori_loop(p0, p0 + np_, one, 0)

    def smooth(tile, p0, np_):
        top = SUB + tile * SUB

        def one(p, carry):
            r = pl.ds(tile * SUB, SUB)
            mid = sh[p, top:top + SUB, :]
            up = sh[p, top - 1:top + SUB - 1, :]
            down = sh[p, top + 1:top + SUB + 1, :]
            out[p, r, :] = out[p, r, :] + visc[lax.rem(p, 2), r, :] * (down + up - 2.0 * mid)
            return carry

        lax.fori_loop(p0, p0 + np_, one, 0)

    for c in fetches:
        c.start()
    arrive(0)
    for c in fetches:
        c.wait()
    for t in range(tiles):
        shift_tile(t, dust, 2)
    edges = [send_edge(s, dust, 2) for s in (0, 1)]
    for e in edges:
        edge_wait(e)
    place_edges(dust, 2)
    for t in range(tiles):
        smooth(t, dust, 2)

    row = lax.broadcasted_iota(jnp.int32, (SUB, width), 0)
    for h in range(2):
        base = jnp.zeros((1, width), jnp.float32)
        for t in range(tiles):
            r = pl.ds(t * SUB, SUB)
            step = 2.0 * absorb[h, r, :] * out[dust + h, r, :] / total_rows
            run = step
            for k in (1, 2, 4):
                run = run + jnp.where(row >= k, pltpu.roll(run, k, 0), 0.0)
            run = run + base
            depth[h, r, :] = run - 0.5 * step
            base = run[SUB - 1:]
        tot_out[0, h] = base
    scan_send()
    arrive(1)
    shift_tile(0, 0, rest)
    edge_in = send_edge(0, 0, rest)
    scan_take()
    scan_send()
    arrive(2)
    shift_tile(tiles - 1, 0, rest)
    edge_out = send_edge(1, 0, rest)

    scan_take()
    while 1 << len(hops) < n_rad:
        scan_send()
        scan_take()
    for h in range(2):
        carried = tot_in[0, h]
        for i in range(1, len(hops)):
            carried = carried + tot_in[i, h]
        for t in range(tiles):
            r = pl.ds(t * SUB, SUB)
            radius = (rad * rows + t * SUB + row).astype(jnp.float32) + 0.5
            flux = 1.0 / (1.0 + radius / total_rows)
            depth[h, r, :] = depth[h, r, :] + carried
            heat[h, r, :] = flux * jnp.exp(-depth[h, r, :])

    def warm(tile):
        r = pl.ds(tile * SUB, SUB)
        for h in range(2):
            out[rest - 2 + h, r, :] = out[rest - 2 + h, r, :] + heat[h, r, :]

    edge_wait(edge_in)
    edge_wait(edge_out)
    place_edges(0, rest)
    i = 3
    for t in range(1, tiles - 2):
        arrive(i)
        shift_tile(t, 0, rest)
        smooth(t - 1, 0, rest)
        warm(t - 1)
        i += 1
    first = max(tiles - 3, 0)
    for p0, np_ in tail:
        arrive(i)
        shift_tile(tiles - 2, p0, np_)
        for t in range(first, tiles):
            smooth(t, p0, np_)
            if p0 + np_ == rest:
                warm(t)
        i += 1
    for goes, c in chained:
        pl.when(goes)(c.wait_send)
    for c in sent:
        c.wait_send()


def full(n_rad, n_az, state, offsets, viscosity, absorb):
    fields, polar, rows, width = state.shape
    planes = fields * polar
    groups = n_az // 2
    tiles = rows // SUB
    n_tail = len(tail_planes(planes - 2))
    n_pieces = 1 + 2 + max(tiles - 3, 0) + n_tail
    n_scan = (n_rad - 1).bit_length()
    n_local = 1
    n_sems = n_pieces * (2 * (groups - 1) + 1) + 4 + n_scan
    f32 = jnp.float32
    vm = pl.BlockSpec(memory_space=pltpu.VMEM)
    hbm = pl.BlockSpec(memory_space=pl.ANY)
    moved, local = pl.pallas_call(
        functools.partial(kernel, n_rad, n_az, n_local),
        out_shape=(
            pltpu.VMEM((planes, rows, width), f32),
            pltpu.VMEM((polar, rows, width), f32),
        ),
        in_specs=[hbm, pl.BlockSpec(memory_space=pltpu.SMEM), hbm, hbm],
        out_specs=(vm, vm),
        scratch_shapes=[
            pltpu.VMEM((polar, rows, width), f32),
            pltpu.VMEM((polar, rows, width), f32),
            pltpu.VMEM((polar, rows, width), f32),
            pltpu.VMEM((planes, rows, width), f32),
            pltpu.VMEM((n_az - 1, planes, rows, width), f32),
            pltpu.VMEM((planes, rows + 2 * SUB, width), f32),
            pltpu.VMEM((2, planes, 1, width), f32),
            pltpu.VMEM((2, planes, 1, width), f32),
            pltpu.VMEM((n_scan + 1, polar, 1, width), f32),
            pltpu.VMEM((n_scan, polar, 1, width), f32),
            pltpu.SemaphoreType.DMA((n_sems,)),
            pltpu.SemaphoreType.DMA((n_sems,)),
            pltpu.SemaphoreType.DMA((n_local + 2,)),
        ],
        compiler_params=pltpu.CompilerParams(
            collective_id=0, has_side_effects=True, vmem_limit_bytes=56 * 2**20
        ),
    )(state.reshape(planes, rows, width), offsets, viscosity, absorb)
    return moved, local


def fast_kernel(n_rad, n_az, cap, dust_cap, source, offs_in, visc_in, absorb_in, out, depth, flag,
                visc, absorb, heat, gathered, packed, pool_mine, pool_other, early_mine, early_other,
                stage, sh, eo, ei, tot_out, tot_in, take_v, look_v, take, look, offs, ss, rs, ls):
    rad = lax.axis_index("rad")
    az = lax.axis_index("az")
    core = lax.rem(az, 2)
    chip = az // 2
    sibling = {"az": az + 1 - 2 * core}
    across = {"az": lax.rem(az + 2, n_az)}
    planes, rows, width = out.shape
    polar = 2
    fields = planes // polar
    cols = width // LANES
    col_bits = cols.bit_length() - 1
    tiles = rows // SUB
    units = rows * cols
    half = 2 * units
    ring = 2 * cols
    span = cols + 2
    total_rows = rows * n_rad
    dust, energy = fields - 1, fields - 2
    order = [dust, energy] + list(range(energy))
    last = order[-1]
    n_scan = (n_rad - 1).bit_length()
    n_early = 2 * ring
    n_raw = SUB * cols
    raw_at = half + cap
    take_rows = -(-cap // LANES)

    def rad_at(k):
        return {"rad": lax.rem(rad + k + n_rad, n_rad)}

    def rad_pair(i):
        d = 1 << i
        upper = lax.rem(rad // d, 2)
        return {"rad": rad + d - 2 * d * upper}, upper

    count = [0, 0]

    def remote(src, dst, device):
        i = count[0]
        count[0] += 1
        return pltpu.make_async_remote_copy(
            src_ref=src, dst_ref=dst, send_sem=ss.at[i], recv_sem=rs.at[i],
            device_id=device, device_id_type=pl.DeviceIdType.MESH,
        )

    def local(src, dst):
        i = count[1]
        count[1] += 1
        c = pltpu.make_async_copy(src, dst, ls.at[i])
        c.start()
        return c

    offs_copy = local(offs_in, offs)
    inner, outer = rad > 0, rad < n_rad - 1
    ei[...] = jnp.zeros_like(ei)
    barrier = pltpu.get_barrier_semaphore()
    for peer in [sibling, across] + [rad_pair(i)[0] for i in range(1, n_scan)]:
        pl.semaphore_signal(barrier, inc=1, device_id=peer, device_id_type=pl.DeviceIdType.MESH)
    for there, k in ((inner, -1), (outer, 1)):
        @pl.when(there)
        def _():
            pl.semaphore_signal(barrier, inc=1, device_id=rad_at(k), device_id_type=pl.DeviceIdType.MESH)

    mine = pl.ds(core * units, units)
    first_pack = [local(source.at[polar * f + core], gathered[f].at[mine]) for f in order[:1]]

    pl.semaphore_wait(barrier, 2 + n_scan - 1 + inner.astype(jnp.int32) + outer.astype(jnp.int32))

    sent, chained = [], []
    to_pack = [remote(source.at[polar * f + 1 - core], gathered[f].at[mine], sibling) for f in order]
    to_mine = [remote(source.at[polar * f + 1 - core], pool_mine[f].at[mine], sibling) for f in order]
    to_other = [remote(source.at[polar * f + core], pool_other[f].at[mine], sibling) for f in order]
    to_early = [
        remote(source.at[polar * last + 1 - core], early_mine.at[mine], sibling),
        remote(source.at[polar * last + core], early_other.at[mine], sibling),
    ]
    sent += to_pack + to_mine + to_other + to_early
    to_pack[0].start()
    raw_mine = remote(
        source.at[polar * dust + core, pl.ds(0, n_raw)],
        pool_mine[dust].at[pl.ds(raw_at + core * n_raw, n_raw)], across,
    )
    raw_other = remote(
        source.at[polar * dust + 1 - core, pl.ds(0, n_raw)],
        pool_other[dust].at[pl.ds(raw_at + core * n_raw, n_raw)], across,
    )
    for c in (raw_mine, raw_other):
        c.start()
        sent.append(c)
    lane = lax.broadcasted_iota(jnp.int32, (SUB, LANES), 1)
    sub = lax.broadcasted_iota(jnp.int32, (SUB, LANES), 0)

    def row_offsets(numbers):
        amount = jnp.full((SUB, LANES), offs[numbers[0]], jnp.int32)
        for k in range(1, len(numbers)):
            amount = jnp.where(sub == k, offs[numbers[k]], amount)
        return amount

    def block_unit(b):
        return (b >> col_bits) * units + (b & (cols - 1)) * SUB

    offs_copy.wait()
    shifts = [row_offsets([t * SUB + k for k in range(SUB)]) for t in range(tiles)]
    leads, manys, befores = [], [], []
    used = jnp.zeros((SUB, LANES), jnp.int32)
    for off in shifts:
        lead = jnp.where(off == 0, ring - 1, jnp.where(off < 2 * width, (2 * width - 1 - off) >> LANE_BITS, 0))
        many = jnp.where(off < 2 * width, ring - lead, jnp.minimum(((4 * width - off) >> LANE_BITS) + 1, ring))
        many = jnp.where(off == 0, 2, many)
        run = many
        for k in (1, 2, 4):
            run = run + jnp.where(sub >= k, pltpu.roll(run, k, 0), 0)
        leads.append(lead)
        manys.append(many)
        befores.append(run - many + used)
        used = used + jnp.broadcast_to(run[SUB - 1:], (SUB, LANES))
    top_many = jnp.broadcast_to(manys[0][:1], (SUB, LANES))
    bottom_many = jnp.broadcast_to(manys[-1][SUB - 1:], (SUB, LANES))
    bases = []
    for t in range(tiles):
        base = befores[t] + bottom_many
        if t == 0:
            base = jnp.where(sub == 0, 0, base)
        if t == tiles - 1:
            base = jnp.where(sub == SUB - 1, top_many, base)
        bases.append(base)
    top_used = befores[1]
    top_used = jnp.broadcast_to(top_used[:1], (SUB, LANES))
    dust_bases = [None] + [before - top_used for before in befores[1:]]
    for size, heads, first, at in ((dust_cap, dust_bases, 1, take_rows), (cap, bases, 0, 0)):
        for q in range(-(-size // LANES)):
            j = q * LANES + lane
            place = jnp.zeros((SUB, LANES), jnp.int32)
            ahead = jnp.zeros((SUB, LANES), jnp.int32)
            for t in range(first, tiles):
                held = (j >= heads[t]) & (j < heads[t] + manys[t])
                place = place + jnp.where(held, t * SUB * cols + sub, 0)
                ahead = ahead + jnp.where(held, leads[t] - heads[t], 0)
            for k in (4, 2, 1):
                place = place + pltpu.roll(place, k, 0)
                ahead = ahead + pltpu.roll(ahead, k, 0)
            take_v[at + q:at + q + 1, :] = (block_unit((j + ahead) & (ring - 1)) + place)[:1]
    take_copy = local(take_v, take)
    for t in range(tiles):
        b = az * cols - (shifts[t] >> LANE_BITS) - 1 + lane + 2 * ring
        near = block_unit(b & (ring - 1)) + (t * SUB * cols + sub)
        here = ((b >> (col_bits + 1)) & 1) == chip
        step = (b - leads[t]) & (ring - 1)
        far = half + jnp.minimum(bases[t] + step, cap - 1)
        look_v[t * SUB:(t + 1) * SUB, :] = jnp.where(here, near, far)
        if t == 0:
            far = raw_at + ((b & (ring - 1)) >> col_bits) * n_raw + (b & (cols - 1)) * SUB + sub
        else:
            far = half + jnp.minimum(dust_bases[t] + step, dust_cap - 1)
        look_v[rows + t * SUB:rows + (t + 1) * SUB, :] = jnp.where(here, near, far)
    look_copy = local(look_v, look)

    crossing = {f: [] for f in order}
    cuts = {f: [0, cap // 2 // SUB * SUB, cap] for f in order}
    cuts[dust] = [0, dust_cap // 4 // SUB * SUB, dust_cap * 5 // 8 // SUB * SUB, dust_cap]
    cuts[last] = [n_early, (n_early + cap) // 2 // SUB * SUB, cap]

    def pack(some, lo, hi):
        def eight(k, carry):
            for s in range(SUB):
                u = take[(k >> 4) + (take_rows if some[0] == dust else 0), (k & 15) * SUB + s]
                for f in some:
                    packed[f][pl.ds(k * SUB + s, 1), :] = gathered[f][pl.ds(u, 1), :]
            return carry

        lax.fori_loop(lo // SUB, hi // SUB, eight, 0)

    def pack_ready(f):
        own_pack[order.index(f)].wait()
        to_pack[order.index(f)].wait_recv()

    def pack_send(f):
        for lo, hi in zip(cuts[f], cuts[f][1:]):
            pack([f], lo, hi)
            c = remote(packed[f].at[pl.ds(lo, hi - lo)], pool_mine[f].at[pl.ds(half + lo, hi - lo)], across)
            c.start()
            sent.append(c)
            crossing[f].append(c)

    def shift_rows(f, numbers, shift, source_ref, slot, write):
        for s, r in enumerate(numbers):
            for i in range(span):
                u = look[r + (rows if f == dust else 0), i]
                stage[slot, i, s:s + 1, :] = source_ref[pl.ds(u, 1), :]
        rem = shift & (LANES - 1)
        pick = (lane - rem) & (LANES - 1)
        low = lane < rem
        turned = [
            jnp.take_along_axis(stage[slot, i], pick, axis=1, mode="promise_in_bounds") for i in range(span)
        ]
        x = [turned[0]] + [jnp.where(low, turned[j - 1], turned[j]) for j in range(1, span)]
        write(x)

    def shift_plane(f, source_ref, p):
        def one(tile):
            r = pl.ds(tile * SUB, SUB)
            below = pl.ds(SUB + tile * SUB, SUB)

            def write(x):
                right = [pltpu.roll(v, 1, 1) for v in x[:-1]]
                left = [pltpu.roll(v, LANES - 1, 1) for v in x[1:]]
                for c in range(cols):
                    cs = pl.ds(c * LANES, LANES)
                    mid = x[c + 1]
                    prev = jnp.where(lane == 0, right[c], right[c + 1])
                    nxt = jnp.where(lane == LANES - 1, left[c + 1], left[c])
                    sh[p, below, cs] = mid
                    out[p, r, cs] = mid + AZIMUTH_COEF * (nxt + prev - 2.0 * mid)

            numbers = [tile * SUB + s for s in range(SUB)]
            shift_rows(f, numbers, row_offsets(numbers), source_ref, tile, write)

        for t in range(tiles):
            one(t)

    def send_edges(f):
        ps = pl.ds(polar * f, polar)
        got = []
        for side in range(2):
            c = remote(eo.at[side, ps], ei.at[1 - side, ps], rad_at(-1 if side == 0 else 1))
            goes, comes = (inner, outer) if side == 0 else (outer, inner)
            pl.when(goes)(c.start)
            chained.append((goes, c))
            got.append((comes, c))
        return got

    def take_edges(f, got):
        for comes, c in got:
            pl.when(comes)(c.wait_recv)
        for h in range(polar):
            p = polar * f + h
            sh[p, SUB - 1:SUB, :] = jnp.where(rad > 0, ei[0, p], 0.0)
            sh[p, SUB + rows:SUB + rows + 1, :] = jnp.where(rad < n_rad - 1, ei[1, p], 0.0)

    def smooth(f, h):
        p = polar * f + h
        for tile in range(tiles):
            top = SUB + tile * SUB
            r = pl.ds(tile * SUB, SUB)
            mid = sh[p, top:top + SUB, :]
            up = sh[p, top - 1:top + SUB - 1, :]
            down = sh[p, top + 1:top + SUB + 1, :]
            new = out[p, r, :] + visc[h, r, :] * (down + up - 2.0 * mid)
            if f == energy:
                new = new + heat[h, r, :]
            out[p, r, :] = new

    def forward(f):
        i = order.index(f)
        onward = []
        for c, lo, hi in zip(crossing[f], cuts[f], cuts[f][1:]):
            c.wait_recv()
            at = pl.ds(half + lo, hi - lo)
            c = remote(pool_mine[f].at[at], pool_other[f].at[at], sibling)
            c.start()
            sent.append(c)
            onward.append(c)
        own_mine[i].wait()
        to_mine[i].wait_recv()
        return onward

    def other_ready(f, onward):
        i = order.index(f)
        own_other[i].wait()
        to_other[i].wait_recv()
        for c in onward:
            c.wait_recv()

    def work(f):
        onward = forward(f)
        shift_plane(f, pool_mine[f], polar * f + core)
        other_ready(f, onward)
        shift_plane(f, pool_other[f], polar * f + 1 - core)
        for h in range(polar):
            p = polar * f + h
            eo[0, p] = sh[p, SUB:SUB + 1, :]
            eo[1, p] = sh[p, SUB + rows - 1:SUB + rows, :]
        return send_edges(f)

    def finish(f, got):
        take_edges(f, got)
        for h in range(polar):
            smooth(f, h)

    def flush(but=()):
        for goes, c in chained:
            pl.when(goes)(c.wait_send)
        for c in sent:
            if not any(c is b for b in but):
                c.wait_send()
        sent[:] = but
        chained.clear()

    early_at = pl.ds(half, n_early)

    def early_edges():
        crossing_early.wait_recv()
        onward = remote(early_mine.at[early_at], early_other.at[early_at], sibling)
        onward.start()
        sent.append(onward)
        numbers = [0, rows - 1]
        for c in own_early:
            c.wait()
        for c in to_early:
            c.wait_recv()
        copies = [local(early_mine.at[early_at], pool_mine[last].at[early_at])]
        for ref, hh in ((early_mine, core), (early_other, 1 - core)):
            p = polar * last + hh
            if ref is early_other:
                onward.wait_recv()
                copies.append(local(early_other.at[early_at], pool_other[last].at[early_at]))

            def write(x):
                for c in range(cols):
                    cs = pl.ds(c * LANES, LANES)
                    eo[0, p, :, cs] = x[c + 1][:1]
                    eo[1, p, :, cs] = x[c + 1][1:2]

            shift_rows(last, numbers, row_offsets(numbers), ref, 0, write)
        got = send_edges(last)
        for c in copies:
            c.wait()
        return got

    own_pack = first_pack
    take_copy.wait()
    to_pack[1].start()
    pack_ready(dust)
    pack_send(dust)
    own_pack = first_pack + [local(source.at[polar * f + core], gathered[f].at[mine]) for f in order[1:]]
    for c in to_pack[2:]:
        c.start()
    look_copy.wait()
    pack_ready(energy)
    pack_send(energy)
    raw_here = pl.ds(raw_at + core * n_raw, n_raw)
    raw_onward = []
    for c, src, dst in ((raw_mine, pool_mine, pool_other), (raw_other, pool_other, pool_mine)):
        c.wait_recv()
        c = remote(src[dust].at[raw_here], dst[dust].at[raw_here], sibling)
        c.start()
        sent.append(c)
        raw_onward.append(c)
    own_mine, own_other = [], []

    def fill_pools(i):
        f = order[i]
        to_mine[i].start()
        to_other[i].start()
        own_mine.append(local(source.at[polar * f + core], pool_mine[f].at[mine]))
        own_other.append(local(source.at[polar * f + 1 - core], pool_other[f].at[mine]))

    fill_pools(0)
    params = [local(visc_in, visc), local(absorb_in, absorb)]
    pack_ready(last)
    pack([last], 0, n_early)
    crossing_early = remote(packed[last].at[pl.ds(0, n_early)], early_mine.at[early_at], across)
    crossing_early.start()
    sent.append(crossing_early)
    for i in range(2, fields - 1):
        pack_ready(order[i])
        pack_send(order[i])
        fill_pools(i - 1)
    own_early = [
        local(source.at[polar * last + core], early_mine.at[mine]),
        local(source.at[polar * last + 1 - core], early_other.at[mine]),
    ]
    for c in to_early:
        c.start()
    pack_send(last)
    for i in range(fields - 2, fields):
        fill_pools(i)
    for c in params:
        c.wait()

    for c in raw_onward:
        c.wait_recv()
    finish(dust, work(dust))

    row = lax.broadcasted_iota(jnp.int32, (SUB, width), 0)
    for h in range(polar):
        run_last = jnp.zeros((1, width), jnp.float32)
        for t in range(tiles):
            r = pl.ds(t * SUB, SUB)
            step = 2.0 * absorb[h, r, :] * out[polar * dust + h, r, :] / total_rows
            run = step
            for k in (1, 2, 4):
                run = run + jnp.where(row >= k, pltpu.roll(run, k, 0), 0.0)
            run = run + run_last
            depth[h, r, :] = run - 0.5 * step
            run_last = run[SUB - 1:]
        tot_out[0, h] = run_last
    over = ((used > cap) | (used - top_used > dust_cap)).astype(jnp.float32)[:1]
    for c in range(cols):
        tot_out[0, polar, :, pl.ds(c * LANES, LANES)] = over

    hops = []

    def scan_send():
        i = len(hops)
        peer, upper = rad_pair(i)
        c = remote(tot_out.at[i], tot_in.at[i], peer)
        c.start()
        sent.append(c)
        hops.append((c, upper))

    def scan_take():
        i = len(hops) - 1
        hops[i][0].wait_recv()
        tot_out[i + 1] = tot_out[i] + tot_in[i]

    def irradiate():
        for h in range(polar):
            carried = jnp.where(hops[0][1] == 1, tot_in[0, h], 0.0)
            for i in range(1, n_scan):
                carried = carried + jnp.where(hops[i][1] == 1, tot_in[i, h], 0.0)
            for t in range(tiles):
                r = pl.ds(t * SUB, SUB)
                radius = (rad * rows + t * SUB + row).astype(jnp.float32) + 0.5
                flux = 1.0 / (1.0 + radius / total_rows)
                depth[h, r, :] = depth[h, r, :] + carried
                heat[h, r, :] = flux * jnp.exp(-depth[h, r, :])
        flag[0] = jnp.max(tot_out[n_scan, polar])

    scan_send()
    pending = []
    for f in order[1:-1]:
        if f == order[2]:
            last_edges = early_edges()
        pending.append((f, work(f)))
        if len(hops) < n_scan:
            scan_take()
            scan_send()
            ready = [w for w in pending[:-1] if w[0] != energy]
        else:
            if energy in [w[0] for w in pending]:
                scan_take()
                irradiate()
            ready = pending[:-1]
        for w in ready:
            finish(*w)
            pending.remove(w)
    take_edges(last, last_edges)
    flush(crossing[last])
    onward = forward(last)
    for w in pending:
        finish(*w)
    shift_plane(last, pool_mine[last], polar * last + core)
    smooth(last, core)
    other_ready(last, onward)
    shift_plane(last, pool_other[last], polar * last + 1 - core)
    smooth(last, 1 - core)
    flush()


def fast(n_rad, n_az, state, offsets, viscosity, absorb):
    fields, polar, rows, width = state.shape
    planes = fields * polar
    cols = width // LANES
    units = rows * cols
    cap = units * 2 * 11 // 16 // 16 * 16
    dust_cap = (units - SUB * cols) * 2 * 73 // 100 // SUB * SUB
    n_early = 4 * cols
    n_take = -(-(-(-cap // LANES) - (-dust_cap // LANES)) // SUB) * SUB
    n_scan = (n_rad - 1).bit_length()
    n_sems = 9 * fields + 2 + 4 + 4 + n_scan
    pools = [2 * units + cap] * (fields - 1) + [2 * units + cap + 2 * SUB * cols]
    f32, i32 = jnp.float32, jnp.int32
    vm = pl.BlockSpec(memory_space=pltpu.VMEM)
    hbm = pl.BlockSpec(memory_space=pl.ANY)
    source = state.reshape(planes, rows // SUB, SUB, cols, LANES).transpose(0, 1, 3, 2, 4).reshape(planes, units, LANES)
    moved, local, flag = pl.pallas_call(
        functools.partial(fast_kernel, n_rad, n_az, cap, dust_cap),
        out_shape=(
            pltpu.VMEM((planes, rows, width), f32),
            pltpu.VMEM((polar, rows, width), f32),
            pltpu.SMEM((1,), f32),
        ),
        in_specs=[hbm, hbm, hbm, hbm],
        out_specs=(vm, vm, pl.BlockSpec(memory_space=pltpu.SMEM)),
        scratch_shapes=[
            pltpu.VMEM((polar, rows, width), f32),
            pltpu.VMEM((polar, rows, width), f32),
            pltpu.VMEM((polar, rows, width), f32),
            [pltpu.VMEM((2 * units, LANES), f32)] * fields,
            [pltpu.VMEM((cap, LANES), f32)] * fields,
            [pltpu.VMEM((n, LANES), f32) for n in pools],
            [pltpu.VMEM((n, LANES), f32) for n in pools],
            pltpu.VMEM((2 * units + n_early, LANES), f32),
            pltpu.VMEM((2 * units + n_early, LANES), f32),
            pltpu.VMEM((rows // SUB, cols + 2, SUB, LANES), f32),
            pltpu.VMEM((planes, rows + 2 * SUB, width), f32),
            pltpu.VMEM((2, planes, 1, width), f32),
            pltpu.VMEM((2, planes, 1, width), f32),
            pltpu.VMEM((n_scan + 1, polar + 1, 1, width), f32),
            pltpu.VMEM((n_scan, polar + 1, 1, width), f32),
            pltpu.VMEM((n_take, LANES), i32),
            pltpu.VMEM((2 * rows, LANES), i32),
            pltpu.SMEM((n_take, LANES), i32),
            pltpu.SMEM((2 * rows, LANES), i32),
            pltpu.SMEM((rows,), i32),
            pltpu.SemaphoreType.DMA((n_sems,)),
            pltpu.SemaphoreType.DMA((n_sems,)),
            pltpu.SemaphoreType.DMA((3 * fields + 10,)),
        ],
        compiler_params=pltpu.CompilerParams(
            collective_id=1, has_side_effects=True, vmem_limit_bytes=61 * 2**20
        ),
    )(source, offsets, viscosity, absorb)
    return moved, local, flag[0]


def hand_out(moved, local):
    def store(a, b, x, y, sems):
        copies = [pltpu.make_async_copy(a, x, sems.at[0]), pltpu.make_async_copy(b, y, sems.at[1])]
        for c in copies:
            c.start()
        for c in copies:
            c.wait()

    hbm = pl.BlockSpec(memory_space=pl.ANY)
    vm = pl.BlockSpec(memory_space=pltpu.VMEM)
    return pl.pallas_call(
        store,
        out_shape=(pltpu.HBM(moved.shape, moved.dtype), pltpu.HBM(local.shape, local.dtype)),
        in_specs=[vm, vm],
        out_specs=(hbm, hbm),
        scratch_shapes=[pltpu.SemaphoreType.DMA((2,))],
    )(moved, local)


def body(n_rad, n_az, state, offsets, viscosity, absorb):
    args = (state, offsets, viscosity, absorb)
    if n_az != 4 or state.shape[1] != 2 or n_rad not in (2, 4, 8, 16):
        moved, local = full(n_rad, n_az, *args)
    else:
        moved, local, flag = fast(n_rad, n_az, *args)
        moved, local = lax.cond(
            flag > 0, lambda m, d: tuple(full(n_rad, n_az, *args)), lambda m, d: (m, d), moved, local
        )
    moved, local = hand_out(moved, local)
    return moved.reshape(state.shape), local


def solution(mesh):
    in_specs = (P(None, None, "rad", "az"), P("rad"), P(None, "rad", "az"), P(None, "rad", "az"))
    out_specs = (P(None, None, "rad", "az"), P(None, "rad", "az"))
    f = functools.partial(body, mesh.shape["rad"], mesh.shape["az"])
    return jax.shard_map(f, mesh=mesh, in_specs=in_specs, out_specs=out_specs, check_vma=False)
```

```python
import functools

import jax
import jax.numpy as jnp
from jax import lax
from jax.experimental import pallas as pl
from jax.experimental.pallas import tpu as pltpu
from jax.sharding import PartitionSpec as P

AZIMUTH_COEF = 0.1
LANES = 128
SUB = 8
LANE_BITS = 7
SUB_BITS = 3


def tail_planes(rest):
    cuts = [0, rest // 2, rest]
    return [(a, b - a) for a, b in zip(cuts, cuts[1:]) if b > a]


def kernel(n_rad, n_az, n_local, source, offs, visc_in, absorb_in, out, depth,
           visc, absorb, heat, state, buf, sh, eo, ei, tot_out, tot_in, ss, rs, ls):
    groups = n_az // 2
    rad = lax.axis_index("rad")
    az = lax.axis_index("az")
    core = lax.rem(az, 2)
    sibling = {"az": az + 1 - 2 * core}
    planes, rows, width = state.shape
    cols = width // LANES
    tiles = rows // SUB
    dust = planes - 2
    rest = dust
    total_rows = rows * n_rad

    def rad_at(k):
        return {"rad": lax.rem(rad + k + n_rad, n_rad)}

    def az_at(k):
        return {"az": lax.rem(az + 2 * k, n_az)}

    count = [0]

    def remote(src, dst, device):
        i = count[0]
        count[0] += 1
        return pltpu.make_async_remote_copy(
            src_ref=src, dst_ref=dst, send_sem=ss.at[i], recv_sem=rs.at[i],
            device_id=device, device_id_type=pl.DeviceIdType.MESH,
        )

    fetch = pltpu.make_async_copy(source, state, ls.at[0])
    fetches = [fetch] + [
        pltpu.make_async_copy(a, b, ls.at[n_local + i])
        for i, (a, b) in enumerate(((visc_in, visc), (absorb_in, absorb)))
    ]
    inner, outer = rad > 0, rad < n_rad - 1
    ei[...] = jnp.zeros_like(ei)
    tot_in[...] = jnp.zeros_like(tot_in)
    peers = [az_at(k) for k in range(1, groups)] + [sibling]
    barrier = pltpu.get_barrier_semaphore()
    for there, k in ((inner, -1), (outer, 1)):
        @pl.when(there)
        def _():
            pl.semaphore_signal(barrier, inc=1, device_id=rad_at(k), device_id_type=pl.DeviceIdType.MESH)
    for peer in peers:
        pl.semaphore_signal(barrier, inc=1, device_id=peer, device_id_type=pl.DeviceIdType.MESH)
    senders = len(peers)
    d = 1
    while d < n_rad:
        if d > 1:
            @pl.when(rad >= d)
            def _():
                pl.semaphore_signal(barrier, inc=1, device_id=rad_at(-d), device_id_type=pl.DeviceIdType.MESH)
            senders = senders + (rad + d < n_rad).astype(jnp.int32)
        d *= 2
    pl.semaphore_wait(barrier, senders + inner.astype(jnp.int32) + outer.astype(jnp.int32))

    pieces = [(dust, 2, 0, rows)]
    edge_tiles = [0, tiles - 1]
    for t in edge_tiles + list(range(1, tiles - 2)):
        pieces.append((0, rest, t * SUB, SUB))
    tail = tail_planes(rest)
    for p0, np_ in tail:
        pieces.append((p0, np_, (tiles - 2) * SUB, SUB))

    sent, chained = [], []
    across, beside = [], []
    for p0, np_, r0, nr in pieces:
        ps, rws = pl.ds(p0, np_), pl.ds(r0, nr)
        across.append([remote(source.at[ps, rws], buf.at[2 * k - 1, ps, rws], az_at(k)) for k in range(1, groups)])
        beside.append(remote(source.at[ps, rws], buf.at[0, ps, rws], sibling))
        for c in across[-1]:
            c.start()
            sent.append(c)
    for c in beside:
        c.start()
        sent.append(c)

    def arrive(i):
        p0, np_, r0, nr = pieces[i]
        ps, rws = pl.ds(p0, np_), pl.ds(r0, nr)
        forwards = []
        for k in range(1, groups):
            across[i][k - 1].wait_recv()
            f = remote(buf.at[2 * k - 1, ps, rws], buf.at[2 * k, ps, rws], sibling)
            f.start()
            sent.append(f)
            forwards.append(f)
        beside[i].wait_recv()
        for f in forwards:
            f.wait_recv()

    lane = lax.broadcasted_iota(jnp.int32, (SUB, LANES), 1)

    def shift_tile(tile, p0, np_):
        r = pl.ds(tile * SUB, SUB)
        sub = lax.broadcasted_iota(jnp.int32, (SUB, LANES), 0)
        amount = jnp.full((SUB, LANES), offs[tile * SUB], jnp.int32)
        for k in range(1, SUB):
            amount = jnp.where(sub == k, offs[tile * SUB + k], amount)
        block = amount // width
        within = amount - block * width
        column = within // LANES
        rem = within - column * LANES
        pick = (lane - rem) & (LANES - 1)
        low = lane < rem

        def one(p, carry):
            def load(d, c):
                cs = pl.ds(c * LANES, LANES)
                if d == 0:
                    return state[p, r, cs]
                if d % 2 == 0:
                    return buf[d - 1, p, r, cs]
                slot = jnp.where(core == 1, d, (d + 2) % n_az)
                return buf[slot - 1, p, r, cs]

            line = []
            for move, c in [(1, c) for c in range(cols)] + [(0, c) for c in range(cols)] + [(-1, 0)]:
                value = load(move % n_az, c)
                for b in range(1, n_az):
                    value = jnp.where(block == b, load((b + move) % n_az, c), value)
                line.append(value)
            step = cols // 2
            while step:
                chosen = (column & step) != 0
                line = [jnp.where(chosen, line[i - step], line[i]) for i in range(step, len(line))]
                step //= 2
            turned = [jnp.take_along_axis(v, pick, axis=1, mode="promise_in_bounds") for v in line]
            x = [turned[0]] + [jnp.where(low, turned[j - 1], turned[j]) for j in range(1, len(turned))]
            right = [pltpu.roll(v, 1, 1) for v in x[:-1]]
            left = [pltpu.roll(v, LANES - 1, 1) for v in x[1:]]
            for c in range(cols):
                cs = pl.ds(c * LANES, LANES)
                mid = x[c + 1]
                prev = jnp.where(lane == 0, right[c], right[c + 1])
                nxt = jnp.where(lane == LANES - 1, left[c + 1], left[c])
                sh[p, pl.ds(SUB + tile * SUB, SUB), cs] = mid
                out[p, r, cs] = mid + AZIMUTH_COEF * (nxt + prev - 2.0 * mid)
                if tile == 0:
                    eo[0, p, :, cs] = mid[:1]
                if tile == tiles - 1:
                    eo[1, p, :, cs] = mid[SUB - 1:]
            return carry

        lax.fori_loop(p0, p0 + np_, one, 0)

    hops = []

    def scan_send():
        i = len(hops)
        d = 1 << i
        if d < n_rad:
            c = remote(tot_out.at[i], tot_in.at[i], rad_at(d))
            goes = rad + d < n_rad
            pl.when(goes)(c.start)
            chained.append((goes, c))
            hops.append(c)

    def scan_take():
        i = len(hops) - 1
        pl.when(rad >= 1 << i)(hops[i].wait_recv)
        tot_out[i + 1] = tot_out[i] + tot_in[i]

    def send_edge(side, p0, np_):
        ps = pl.ds(p0, np_)
        c = remote(eo.at[side, ps], ei.at[1 - side, ps], rad_at(-1 if side == 0 else 1))
        goes, comes = (inner, outer) if side == 0 else (outer, inner)
        pl.when(goes)(c.start)
        chained.append((goes, c))
        return comes, c

    def edge_wait(edge):
        pl.when(edge[0])(edge[1].wait_recv)

    def place_edges(p0, np_):
        def one(p, carry):
            sh[p, SUB - 1:SUB, :] = jnp.where(rad > 0, ei[0, p], 0.0)
            sh[p, SUB + rows:SUB + rows + 1, :] = jnp.where(rad < n_rad - 1, ei[1, p], 0.0)
            return carry

        lax.fori_loop(p0, p0 + np_, one, 0)

    def smooth(tile, p0, np_):
        top = SUB + tile * SUB

        def one(p, carry):
            r = pl.ds(tile * SUB, SUB)
            mid = sh[p, top:top + SUB, :]
            up = sh[p, top - 1:top + SUB - 1, :]
            down = sh[p, top + 1:top + SUB + 1, :]
            out[p, r, :] = out[p, r, :] + visc[lax.rem(p, 2), r, :] * (down + up - 2.0 * mid)
            return carry

        lax.fori_loop(p0, p0 + np_, one, 0)

    for c in fetches:
        c.start()
    arrive(0)
    for c in fetches:
        c.wait()
    for t in range(tiles):
        shift_tile(t, dust, 2)
    edges = [send_edge(s, dust, 2) for s in (0, 1)]
    for e in edges:
        edge_wait(e)
    place_edges(dust, 2)
    for t in range(tiles):
        smooth(t, dust, 2)

    row = lax.broadcasted_iota(jnp.int32, (SUB, width), 0)
    for h in range(2):
        base = jnp.zeros((1, width), jnp.float32)
        for t in range(tiles):
            r = pl.ds(t * SUB, SUB)
            step = 2.0 * absorb[h, r, :] * out[dust + h, r, :] / total_rows
            run = step
            for k in (1, 2, 4):
                run = run + jnp.where(row >= k, pltpu.roll(run, k, 0), 0.0)
            run = run + base
            depth[h, r, :] = run - 0.5 * step
            base = run[SUB - 1:]
        tot_out[0, h] = base
    scan_send()
    arrive(1)
    shift_tile(0, 0, rest)
    edge_in = send_edge(0, 0, rest)
    scan_take()
    scan_send()
    arrive(2)
    shift_tile(tiles - 1, 0, rest)
    edge_out = send_edge(1, 0, rest)

    scan_take()
    while 1 << len(hops) < n_rad:
        scan_send()
        scan_take()
    for h in range(2):
        carried = tot_in[0, h]
        for i in range(1, len(hops)):
            carried = carried + tot_in[i, h]
        for t in range(tiles):
            r = pl.ds(t * SUB, SUB)
            radius = (rad * rows + t * SUB + row).astype(jnp.float32) + 0.5
            flux = 1.0 / (1.0 + radius / total_rows)
            depth[h, r, :] = depth[h, r, :] + carried
            heat[h, r, :] = flux * jnp.exp(-depth[h, r, :])

    def warm(tile):
        r = pl.ds(tile * SUB, SUB)
        for h in range(2):
            out[rest - 2 + h, r, :] = out[rest - 2 + h, r, :] + heat[h, r, :]

    edge_wait(edge_in)
    edge_wait(edge_out)
    place_edges(0, rest)
    i = 3
    for t in range(1, tiles - 2):
        arrive(i)
        shift_tile(t, 0, rest)
        smooth(t - 1, 0, rest)
        warm(t - 1)
        i += 1
    first = max(tiles - 3, 0)
    for p0, np_ in tail:
        arrive(i)
        shift_tile(tiles - 2, p0, np_)
        for t in range(first, tiles):
            smooth(t, p0, np_)
            if p0 + np_ == rest:
                warm(t)
        i += 1
    for goes, c in chained:
        pl.when(goes)(c.wait_send)
    for c in sent:
        c.wait_send()


def full(n_rad, n_az, state, offsets, viscosity, absorb):
    fields, polar, rows, width = state.shape
    planes = fields * polar
    groups = n_az // 2
    tiles = rows // SUB
    n_tail = len(tail_planes(planes - 2))
    n_pieces = 1 + 2 + max(tiles - 3, 0) + n_tail
    n_scan = (n_rad - 1).bit_length()
    n_local = 1
    n_sems = n_pieces * (2 * (groups - 1) + 1) + 4 + n_scan
    f32 = jnp.float32
    vm = pl.BlockSpec(memory_space=pltpu.VMEM)
    hbm = pl.BlockSpec(memory_space=pl.ANY)
    moved, local = pl.pallas_call(
        functools.partial(kernel, n_rad, n_az, n_local),
        out_shape=(
            pltpu.VMEM((planes, rows, width), f32),
            pltpu.VMEM((polar, rows, width), f32),
        ),
        in_specs=[hbm, pl.BlockSpec(memory_space=pltpu.SMEM), hbm, hbm],
        out_specs=(vm, vm),
        scratch_shapes=[
            pltpu.VMEM((polar, rows, width), f32),
            pltpu.VMEM((polar, rows, width), f32),
            pltpu.VMEM((polar, rows, width), f32),
            pltpu.VMEM((planes, rows, width), f32),
            pltpu.VMEM((n_az - 1, planes, rows, width), f32),
            pltpu.VMEM((planes, rows + 2 * SUB, width), f32),
            pltpu.VMEM((2, planes, 1, width), f32),
            pltpu.VMEM((2, planes, 1, width), f32),
            pltpu.VMEM((n_scan + 1, polar, 1, width), f32),
            pltpu.VMEM((n_scan, polar, 1, width), f32),
            pltpu.SemaphoreType.DMA((n_sems,)),
            pltpu.SemaphoreType.DMA((n_sems,)),
            pltpu.SemaphoreType.DMA((n_local + 2,)),
        ],
        compiler_params=pltpu.CompilerParams(
            collective_id=0, has_side_effects=True, vmem_limit_bytes=56 * 2**20
        ),
    )(state.reshape(planes, rows, width), offsets, viscosity, absorb)
    return moved, local


def fast_kernel(n_rad, n_az, cap, dust_cap, source, offs_in, visc_in, absorb_in, out, depth, flag,
                visc, absorb, heat, gathered, packed, pool_mine, pool_other, early_mine, early_other,
                stage, sh, eo, ei, tot_out, tot_in, take_v, look_v, take, look, offs, ss, rs, ls):
    rad = lax.axis_index("rad")
    az = lax.axis_index("az")
    core = lax.rem(az, 2)
    chip = az // 2
    sibling = {"az": az + 1 - 2 * core}
    across = {"az": lax.rem(az + 2, n_az)}
    planes, rows, width = out.shape
    polar = 2
    fields = planes // polar
    cols = width // LANES
    col_bits = cols.bit_length() - 1
    tiles = rows // SUB
    units = rows * cols
    half = 2 * units
    ring = 2 * cols
    span = cols + 2
    total_rows = rows * n_rad
    dust, energy = fields - 1, fields - 2
    order = [dust, energy] + list(range(energy))
    last = order[-1]
    n_scan = (n_rad - 1).bit_length()
    n_early = 2 * ring
    n_raw = SUB * cols
    raw_at = half + cap
    take_rows = -(-cap // LANES)

    def rad_at(k):
        return {"rad": lax.rem(rad + k + n_rad, n_rad)}

    def rad_pair(i):
        d = 1 << i
        upper = lax.rem(rad // d, 2)
        return {"rad": rad + d - 2 * d * upper}, upper

    count = [0, 0]

    def remote(src, dst, device):
        i = count[0]
        count[0] += 1
        return pltpu.make_async_remote_copy(
            src_ref=src, dst_ref=dst, send_sem=ss.at[i], recv_sem=rs.at[i],
            device_id=device, device_id_type=pl.DeviceIdType.MESH,
        )

    def local(src, dst):
        i = count[1]
        count[1] += 1
        c = pltpu.make_async_copy(src, dst, ls.at[i])
        c.start()
        return c

    offs_copy = local(offs_in, offs)
    inner, outer = rad > 0, rad < n_rad - 1
    barrier = pltpu.get_barrier_semaphore()
    for peer in [rad_pair(i)[0] for i in reversed(range(1, n_scan))]:
        pl.semaphore_signal(barrier, inc=1, device_id=peer, device_id_type=pl.DeviceIdType.MESH)
    for there, k in ((inner, -1), (outer, 1)):
        @pl.when(there)
        def _():
            pl.semaphore_signal(barrier, inc=1, device_id=rad_at(k), device_id_type=pl.DeviceIdType.MESH)
    for peer in [sibling, across]:
        pl.semaphore_signal(barrier, inc=1, device_id=peer, device_id_type=pl.DeviceIdType.MESH)
    for edge, k in ((rad == 0, 0), (rad == n_rad - 1, 1)):
        @pl.when(edge)
        def _():
            ei[k] = jnp.zeros(ei.shape[1:], jnp.float32)

    mine = pl.ds(core * units, units)
    first_pack = [local(source.at[polar * f + core], gathered[f].at[mine]) for f in order[:1]]

    pl.semaphore_wait(barrier, 2 + n_scan - 1 + inner.astype(jnp.int32) + outer.astype(jnp.int32))

    sent, chained = [], []
    to_pack = [remote(source.at[polar * f + 1 - core], gathered[f].at[mine], sibling) for f in order]
    to_mine = [remote(source.at[polar * f + 1 - core], pool_mine[f].at[mine], sibling) for f in order]
    to_other = [remote(source.at[polar * f + core], pool_other[f].at[mine], sibling) for f in order]
    to_early = [
        remote(source.at[polar * last + 1 - core], early_mine.at[mine], sibling),
        remote(source.at[polar * last + core], early_other.at[mine], sibling),
    ]
    sent += to_pack + to_mine + to_other + to_early
    to_pack[0].start()
    raw_mine = remote(
        source.at[polar * dust + core, pl.ds(0, n_raw)],
        pool_mine[dust].at[pl.ds(raw_at + core * n_raw, n_raw)], across,
    )
    raw_other = remote(
        source.at[polar * dust + 1 - core, pl.ds(0, n_raw)],
        pool_other[dust].at[pl.ds(raw_at + core * n_raw, n_raw)], across,
    )
    for c in (raw_mine, raw_other):
        c.start()
        sent.append(c)
    lane = lax.broadcasted_iota(jnp.int32, (SUB, LANES), 1)
    sub = lax.broadcasted_iota(jnp.int32, (SUB, LANES), 0)

    def row_offsets(numbers):
        amount = jnp.full((SUB, LANES), offs[numbers[0]], jnp.int32)
        for k in range(1, len(numbers)):
            amount = jnp.where(sub == k, offs[numbers[k]], amount)
        return amount

    def block_unit(b):
        return (b >> col_bits) * units + (b & (cols - 1)) * SUB

    offs_copy.wait()
    shifts = [row_offsets([t * SUB + k for k in range(SUB)]) for t in range(tiles)]
    leads, manys, befores = [], [], []
    used = jnp.zeros((SUB, LANES), jnp.int32)
    for off in shifts:
        lead = jnp.where(off == 0, ring - 1, jnp.where(off < 2 * width, (2 * width - 1 - off) >> LANE_BITS, 0))
        many = jnp.where(off < 2 * width, ring - lead, jnp.minimum(((4 * width - off) >> LANE_BITS) + 1, ring))
        many = jnp.where(off == 0, 2, many)
        run = many
        for k in (1, 2, 4):
            run = run + jnp.where(sub >= k, pltpu.roll(run, k, 0), 0)
        leads.append(lead)
        manys.append(many)
        befores.append(run - many + used)
        used = used + jnp.broadcast_to(run[SUB - 1:], (SUB, LANES))
    top_many = jnp.broadcast_to(manys[0][:1], (SUB, LANES))
    bottom_many = jnp.broadcast_to(manys[-1][SUB - 1:], (SUB, LANES))
    bases = []
    for t in range(tiles):
        base = befores[t] + bottom_many
        if t == 0:
            base = jnp.where(sub == 0, 0, base)
        if t == tiles - 1:
            base = jnp.where(sub == SUB - 1, top_many, base)
        bases.append(base)
    top_used = befores[1]
    top_used = jnp.broadcast_to(top_used[:1], (SUB, LANES))
    dust_bases = [None] + [before - top_used for before in befores[1:]]
    for size, heads, first, at in ((dust_cap, dust_bases, 1, take_rows), (cap, bases, 0, 0)):
        for q in range(-(-size // LANES)):
            j = q * LANES + lane
            place = jnp.zeros((SUB, LANES), jnp.int32)
            ahead = jnp.zeros((SUB, LANES), jnp.int32)
            for t in range(first, tiles):
                held = (j >= heads[t]) & (j < heads[t] + manys[t])
                place = place + jnp.where(held, t * SUB * cols + sub, 0)
                ahead = ahead + jnp.where(held, leads[t] - heads[t], 0)
            for k in (4, 2, 1):
                place = place + pltpu.roll(place, k, 0)
                ahead = ahead + pltpu.roll(ahead, k, 0)
            take_v[at + q:at + q + 1, :] = (block_unit((j + ahead) & (ring - 1)) + place)[:1]
    take_copy = local(take_v, take)
    for t in range(tiles):
        b = az * cols - (shifts[t] >> LANE_BITS) - 1 + lane + 2 * ring
        near = block_unit(b & (ring - 1)) + (t * SUB * cols + sub)
        here = ((b >> (col_bits + 1)) & 1) == chip
        step = (b - leads[t]) & (ring - 1)
        far = half + jnp.minimum(bases[t] + step, cap - 1)
        look_v[t * SUB:(t + 1) * SUB, :] = jnp.where(here, near, far)
        if t == 0:
            far = raw_at + ((b & (ring - 1)) >> col_bits) * n_raw + (b & (cols - 1)) * SUB + sub
        else:
            far = half + jnp.minimum(dust_bases[t] + step, dust_cap - 1)
        look_v[rows + t * SUB:rows + (t + 1) * SUB, :] = jnp.where(here, near, far)
    look_copy = local(look_v, look)

    crossing = {f: [] for f in order}
    cuts = {f: [0, cap // 2 // SUB * SUB, cap] for f in order}
    cuts[dust] = [0, dust_cap // 4 // SUB * SUB, dust_cap * 5 // 8 // SUB * SUB, dust_cap]
    cuts[last] = [n_early, (n_early + cap) // 2 // SUB * SUB, cap]

    def pack(some, lo, hi):
        def eight(k, carry):
            for s in range(SUB):
                u = take[(k >> 4) + (take_rows if some[0] == dust else 0), (k & 15) * SUB + s]
                for f in some:
                    packed[f][pl.ds(k * SUB + s, 1), :] = gathered[f][pl.ds(u, 1), :]
            return carry

        lax.fori_loop(lo // SUB, hi // SUB, eight, 0)

    def pack_ready(f):
        own_pack[order.index(f)].wait()
        to_pack[order.index(f)].wait_recv()

    def pack_send(f):
        for lo, hi in zip(cuts[f], cuts[f][1:]):
            pack([f], lo, hi)
            c = remote(packed[f].at[pl.ds(lo, hi - lo)], pool_mine[f].at[pl.ds(half + lo, hi - lo)], across)
            c.start()
            sent.append(c)
            crossing[f].append(c)

    def shift_rows(f, numbers, shift, source_ref, slot, write):
        for s, r in enumerate(numbers):
            for i in range(span):
                u = look[r + (rows if f == dust else 0), i]
                stage[slot, i, s:s + 1, :] = source_ref[pl.ds(u, 1), :]
        rem = shift & (LANES - 1)
        pick = (lane - rem) & (LANES - 1)
        low = lane < rem
        turned = [
            jnp.take_along_axis(stage[slot, i], pick, axis=1, mode="promise_in_bounds") for i in range(span)
        ]
        x = [turned[0]] + [jnp.where(low, turned[j - 1], turned[j]) for j in range(1, span)]
        write(x)

    def shift_plane(f, source_ref, p):
        def one(tile):
            r = pl.ds(tile * SUB, SUB)
            below = pl.ds(SUB + tile * SUB, SUB)

            def write(x):
                right = [pltpu.roll(v, 1, 1) for v in x[:-1]]
                left = [pltpu.roll(v, LANES - 1, 1) for v in x[1:]]
                for c in range(cols):
                    cs = pl.ds(c * LANES, LANES)
                    mid = x[c + 1]
                    prev = jnp.where(lane == 0, right[c], right[c + 1])
                    nxt = jnp.where(lane == LANES - 1, left[c + 1], left[c])
                    sh[p, below, cs] = mid
                    out[p, r, cs] = mid + AZIMUTH_COEF * (nxt + prev - 2.0 * mid)

            numbers = [tile * SUB + s for s in range(SUB)]
            shift_rows(f, numbers, row_offsets(numbers), source_ref, tile, write)

        for t in range(tiles):
            one(t)

    def send_edges(f):
        ps = pl.ds(polar * f, polar)
        got = []
        for side in range(2):
            c = remote(eo.at[side, ps], ei.at[1 - side, ps], rad_at(-1 if side == 0 else 1))
            goes, comes = (inner, outer) if side == 0 else (outer, inner)
            pl.when(goes)(c.start)
            chained.append((goes, c))
            got.append((comes, c))
        return got

    def take_edges(f, got):
        for comes, c in got:
            pl.when(comes)(c.wait_recv)
        for h in range(polar):
            p = polar * f + h
            sh[p, SUB - 1:SUB, :] = jnp.where(rad > 0, ei[0, p], 0.0)
            sh[p, SUB + rows:SUB + rows + 1, :] = jnp.where(rad < n_rad - 1, ei[1, p], 0.0)

    def smooth(f, h):
        p = polar * f + h
        for tile in range(tiles):
            top = SUB + tile * SUB
            r = pl.ds(tile * SUB, SUB)
            mid = sh[p, top:top + SUB, :]
            up = sh[p, top - 1:top + SUB - 1, :]
            down = sh[p, top + 1:top + SUB + 1, :]
            new = out[p, r, :] + visc[h, r, :] * (down + up - 2.0 * mid)
            if f == energy:
                new = new + heat[h, r, :]
            out[p, r, :] = new

    def forward(f):
        i = order.index(f)
        onward = []
        for c, lo, hi in zip(crossing[f], cuts[f], cuts[f][1:]):
            c.wait_recv()
            at = pl.ds(half + lo, hi - lo)
            c = remote(pool_mine[f].at[at], pool_other[f].at[at], sibling)
            c.start()
            sent.append(c)
            onward.append(c)
        own_mine[i].wait()
        to_mine[i].wait_recv()
        return onward

    def other_ready(f, onward):
        i = order.index(f)
        own_other[i].wait()
        to_other[i].wait_recv()
        for c in onward:
            c.wait_recv()

    def work(f):
        onward = forward(f)
        shift_plane(f, pool_mine[f], polar * f + core)
        other_ready(f, onward)
        shift_plane(f, pool_other[f], polar * f + 1 - core)
        for h in range(polar):
            p = polar * f + h
            eo[0, p] = sh[p, SUB:SUB + 1, :]
            eo[1, p] = sh[p, SUB + rows - 1:SUB + rows, :]
        return send_edges(f)

    def finish(f, got):
        take_edges(f, got)
        for h in range(polar):
            smooth(f, h)

    def flush(but=()):
        for goes, c in chained:
            pl.when(goes)(c.wait_send)
        for c in sent:
            if not any(c is b for b in but):
                c.wait_send()
        sent[:] = but
        chained.clear()

    early_at = pl.ds(half, n_early)

    def early_edges():
        crossing_early.wait_recv()
        onward = remote(early_mine.at[early_at], early_other.at[early_at], sibling)
        onward.start()
        sent.append(onward)
        numbers = [0, rows - 1]
        for c in own_early:
            c.wait()
        for c in to_early:
            c.wait_recv()
        copies = [local(early_mine.at[early_at], pool_mine[last].at[early_at])]
        for ref, hh in ((early_mine, core), (early_other, 1 - core)):
            p = polar * last + hh
            if ref is early_other:
                onward.wait_recv()
                copies.append(local(early_other.at[early_at], pool_other[last].at[early_at]))

            def write(x):
                for c in range(cols):
                    cs = pl.ds(c * LANES, LANES)
                    eo[0, p, :, cs] = x[c + 1][:1]
                    eo[1, p, :, cs] = x[c + 1][1:2]

            shift_rows(last, numbers, row_offsets(numbers), ref, 0, write)
        got = send_edges(last)
        for c in copies:
            c.wait()
        return got

    own_pack = first_pack
    take_copy.wait()
    to_pack[1].start()
    pack_ready(dust)
    pack_send(dust)
    own_pack = first_pack + [local(source.at[polar * f + core], gathered[f].at[mine]) for f in order[1:]]
    for c in to_pack[2:]:
        c.start()
    look_copy.wait()
    pack_ready(energy)
    pack_send(energy)
    raw_here = pl.ds(raw_at + core * n_raw, n_raw)
    raw_onward = []
    for c, src, dst in ((raw_mine, pool_mine, pool_other), (raw_other, pool_other, pool_mine)):
        c.wait_recv()
        c = remote(src[dust].at[raw_here], dst[dust].at[raw_here], sibling)
        c.start()
        sent.append(c)
        raw_onward.append(c)
    own_mine, own_other = [], []

    def fill_pools(i):
        f = order[i]
        to_mine[i].start()
        to_other[i].start()
        own_mine.append(local(source.at[polar * f + core], pool_mine[f].at[mine]))
        own_other.append(local(source.at[polar * f + 1 - core], pool_other[f].at[mine]))

    fill_pools(0)
    params = [local(visc_in, visc), local(absorb_in, absorb)]
    pack_ready(last)
    pack([last], 0, n_early)
    crossing_early = remote(packed[last].at[pl.ds(0, n_early)], early_mine.at[early_at], across)
    crossing_early.start()
    sent.append(crossing_early)
    for i in range(2, fields - 1):
        pack_ready(order[i])
        pack_send(order[i])
        fill_pools(i - 1)
    own_early = [
        local(source.at[polar * last + core], early_mine.at[mine]),
        local(source.at[polar * last + 1 - core], early_other.at[mine]),
    ]
    for c in to_early:
        c.start()
    pack_send(last)
    for i in range(fields - 2, fields):
        fill_pools(i)
    for c in params:
        c.wait()

    for c in raw_onward:
        c.wait_recv()
    finish(dust, work(dust))

    row = lax.broadcasted_iota(jnp.int32, (SUB, width), 0)
    for h in range(polar):
        run_last = jnp.zeros((1, width), jnp.float32)
        for t in range(tiles):
            r = pl.ds(t * SUB, SUB)
            step = 2.0 * absorb[h, r, :] * out[polar * dust + h, r, :] / total_rows
            run = step
            for k in (1, 2, 4):
                run = run + jnp.where(row >= k, pltpu.roll(run, k, 0), 0.0)
            run = run + run_last
            depth[h, r, :] = run - 0.5 * step
            run_last = run[SUB - 1:]
        tot_out[0, h] = run_last
    over = ((used > cap) | (used - top_used > dust_cap)).astype(jnp.float32)[:1]
    for c in range(cols):
        tot_out[0, polar, :, pl.ds(c * LANES, LANES)] = over

    hops = []

    def scan_send():
        i = len(hops)
        peer, upper = rad_pair(i)
        c = remote(tot_out.at[i], tot_in.at[i], peer)
        c.start()
        sent.append(c)
        hops.append((c, upper))

    def scan_take():
        i = len(hops) - 1
        hops[i][0].wait_recv()
        tot_out[i + 1] = tot_out[i] + tot_in[i]

    def irradiate():
        for h in range(polar):
            carried = jnp.where(hops[0][1] == 1, tot_in[0, h], 0.0)
            for i in range(1, n_scan):
                carried = carried + jnp.where(hops[i][1] == 1, tot_in[i, h], 0.0)
            for t in range(tiles):
                r = pl.ds(t * SUB, SUB)
                radius = (rad * rows + t * SUB + row).astype(jnp.float32) + 0.5
                flux = 1.0 / (1.0 + radius / total_rows)
                depth[h, r, :] = depth[h, r, :] + carried
                heat[h, r, :] = flux * jnp.exp(-depth[h, r, :])
        flag[0] = jnp.max(tot_out[n_scan, polar])

    scan_send()
    pending = []
    for f in order[1:-1]:
        if f == order[2]:
            last_edges = early_edges()
        pending.append((f, work(f)))
        if len(hops) < n_scan:
            scan_take()
            scan_send()
            ready = [w for w in pending[:-1] if w[0] != energy]
        else:
            if energy in [w[0] for w in pending]:
                scan_take()
                irradiate()
            ready = pending[:-1]
        for w in ready:
            finish(*w)
            pending.remove(w)
    take_edges(last, last_edges)
    flush(crossing[last])
    onward = forward(last)
    shift_plane(last, pool_mine[last], polar * last + core)
    smooth(last, core)
    other_ready(last, onward)
    shift_plane(last, pool_other[last], polar * last + 1 - core)
    smooth(last, 1 - core)
    for w in pending:
        finish(*w)
    flush()


def fast(n_rad, n_az, state, offsets, viscosity, absorb):
    fields, polar, rows, width = state.shape
    planes = fields * polar
    cols = width // LANES
    units = rows * cols
    cap = units * 2 * 11 // 16 // 16 * 16
    dust_cap = (units - SUB * cols) * 2 * 73 // 100 // SUB * SUB
    n_early = 4 * cols
    n_take = -(-(-(-cap // LANES) - (-dust_cap // LANES)) // SUB) * SUB
    n_scan = (n_rad - 1).bit_length()
    n_sems = 9 * fields + 2 + 4 + 4 + n_scan
    pools = [2 * units + cap] * (fields - 1) + [2 * units + cap + 2 * SUB * cols]
    f32, i32 = jnp.float32, jnp.int32
    vm = pl.BlockSpec(memory_space=pltpu.VMEM)
    hbm = pl.BlockSpec(memory_space=pl.ANY)
    source = state.reshape(planes, rows // SUB, SUB, cols, LANES).transpose(0, 1, 3, 2, 4).reshape(planes, units, LANES)
    moved, local, flag = pl.pallas_call(
        functools.partial(fast_kernel, n_rad, n_az, cap, dust_cap),
        out_shape=(
            pltpu.VMEM((planes, rows, width), f32),
            pltpu.VMEM((polar, rows, width), f32),
            pltpu.SMEM((1,), f32),
        ),
        in_specs=[hbm, hbm, hbm, hbm],
        out_specs=(vm, vm, pl.BlockSpec(memory_space=pltpu.SMEM)),
        scratch_shapes=[
            pltpu.VMEM((polar, rows, width), f32),
            pltpu.VMEM((polar, rows, width), f32),
            pltpu.VMEM((polar, rows, width), f32),
            [pltpu.VMEM((2 * units, LANES), f32)] * fields,
            [pltpu.VMEM((cap, LANES), f32)] * fields,
            [pltpu.VMEM((n, LANES), f32) for n in pools],
            [pltpu.VMEM((n, LANES), f32) for n in pools],
            pltpu.VMEM((2 * units + n_early, LANES), f32),
            pltpu.VMEM((2 * units + n_early, LANES), f32),
            pltpu.VMEM((rows // SUB, cols + 2, SUB, LANES), f32),
            pltpu.VMEM((planes, rows + 2 * SUB, width), f32),
            pltpu.VMEM((2, planes, 1, width), f32),
            pltpu.VMEM((2, planes, 1, width), f32),
            pltpu.VMEM((n_scan + 1, polar + 1, 1, width), f32),
            pltpu.VMEM((n_scan, polar + 1, 1, width), f32),
            pltpu.VMEM((n_take, LANES), i32),
            pltpu.VMEM((2 * rows, LANES), i32),
            pltpu.SMEM((n_take, LANES), i32),
            pltpu.SMEM((2 * rows, LANES), i32),
            pltpu.SMEM((rows,), i32),
            pltpu.SemaphoreType.DMA((n_sems,)),
            pltpu.SemaphoreType.DMA((n_sems,)),
            pltpu.SemaphoreType.DMA((3 * fields + 10,)),
        ],
        compiler_params=pltpu.CompilerParams(
            collective_id=1, has_side_effects=True, vmem_limit_bytes=61 * 2**20
        ),
    )(source, offsets, viscosity, absorb)
    return moved, local, flag[0]


def hand_out(moved, local):
    def store(a, b, x, y, sems):
        copies = [pltpu.make_async_copy(a, x, sems.at[0]), pltpu.make_async_copy(b, y, sems.at[1])]
        for c in copies:
            c.start()
        for c in copies:
            c.wait()

    hbm = pl.BlockSpec(memory_space=pl.ANY)
    vm = pl.BlockSpec(memory_space=pltpu.VMEM)
    return pl.pallas_call(
        store,
        out_shape=(pltpu.HBM(moved.shape, moved.dtype), pltpu.HBM(local.shape, local.dtype)),
        in_specs=[vm, vm],
        out_specs=(hbm, hbm),
        scratch_shapes=[pltpu.SemaphoreType.DMA((2,))],
    )(moved, local)


def body(n_rad, n_az, state, offsets, viscosity, absorb):
    args = (state, offsets, viscosity, absorb)
    if n_az != 4 or state.shape[1] != 2 or n_rad not in (2, 4, 8, 16):
        moved, local = full(n_rad, n_az, *args)
    else:
        moved, local, flag = fast(n_rad, n_az, *args)
        moved, local = lax.cond(
            flag > 0, lambda m, d: tuple(full(n_rad, n_az, *args)), lambda m, d: (m, d), moved, local
        )
    moved, local = hand_out(moved, local)
    return moved.reshape(state.shape), local


def solution(mesh):
    in_specs = (P(None, None, "rad", "az"), P("rad"), P(None, "rad", "az"), P(None, "rad", "az"))
    out_specs = (P(None, None, "rad", "az"), P(None, "rad", "az"))
    f = functools.partial(body, mesh.shape["rad"], mesh.shape["az"])
    return jax.shard_map(f, mesh=mesh, in_specs=in_specs, out_specs=out_specs, check_vma=False)
```

```python
import functools

import jax
import jax.numpy as jnp
from jax import lax
from jax.experimental import pallas as pl
from jax.experimental.pallas import tpu as pltpu
from jax.sharding import PartitionSpec as P

AZIMUTH_COEF = 0.1
LANES = 128
SUB = 8
LANE_BITS = 7
SUB_BITS = 3


def tail_planes(rest):
    cuts = [0, rest // 2, rest]
    return [(a, b - a) for a, b in zip(cuts, cuts[1:]) if b > a]


def kernel(n_rad, n_az, n_local, source, offs, visc_in, absorb_in, out, depth,
           visc, absorb, heat, state, buf, sh, eo, ei, tot_out, tot_in, ss, rs, ls):
    groups = n_az // 2
    rad = lax.axis_index("rad")
    az = lax.axis_index("az")
    core = lax.rem(az, 2)
    sibling = {"az": az + 1 - 2 * core}
    planes, rows, width = state.shape
    cols = width // LANES
    tiles = rows // SUB
    dust = planes - 2
    rest = dust
    total_rows = rows * n_rad

    def rad_at(k):
        return {"rad": lax.rem(rad + k + n_rad, n_rad)}

    def az_at(k):
        return {"az": lax.rem(az + 2 * k, n_az)}

    count = [0]

    def remote(src, dst, device):
        i = count[0]
        count[0] += 1
        return pltpu.make_async_remote_copy(
            src_ref=src, dst_ref=dst, send_sem=ss.at[i], recv_sem=rs.at[i],
            device_id=device, device_id_type=pl.DeviceIdType.MESH,
        )

    fetch = pltpu.make_async_copy(source, state, ls.at[0])
    fetches = [fetch] + [
        pltpu.make_async_copy(a, b, ls.at[n_local + i])
        for i, (a, b) in enumerate(((visc_in, visc), (absorb_in, absorb)))
    ]
    inner, outer = rad > 0, rad < n_rad - 1
    ei[...] = jnp.zeros_like(ei)
    tot_in[...] = jnp.zeros_like(tot_in)
    peers = [az_at(k) for k in range(1, groups)] + [sibling]
    barrier = pltpu.get_barrier_semaphore()
    for there, k in ((inner, -1), (outer, 1)):
        @pl.when(there)
        def _():
            pl.semaphore_signal(barrier, inc=1, device_id=rad_at(k), device_id_type=pl.DeviceIdType.MESH)
    for peer in peers:
        pl.semaphore_signal(barrier, inc=1, device_id=peer, device_id_type=pl.DeviceIdType.MESH)
    senders = len(peers)
    d = 1
    while d < n_rad:
        if d > 1:
            @pl.when(rad >= d)
            def _():
                pl.semaphore_signal(barrier, inc=1, device_id=rad_at(-d), device_id_type=pl.DeviceIdType.MESH)
            senders = senders + (rad + d < n_rad).astype(jnp.int32)
        d *= 2
    pl.semaphore_wait(barrier, senders + inner.astype(jnp.int32) + outer.astype(jnp.int32))

    pieces = [(dust, 2, 0, rows)]
    edge_tiles = [0, tiles - 1]
    for t in edge_tiles + list(range(1, tiles - 2)):
        pieces.append((0, rest, t * SUB, SUB))
    tail = tail_planes(rest)
    for p0, np_ in tail:
        pieces.append((p0, np_, (tiles - 2) * SUB, SUB))

    sent, chained = [], []
    across, beside = [], []
    for p0, np_, r0, nr in pieces:
        ps, rws = pl.ds(p0, np_), pl.ds(r0, nr)
        across.append([remote(source.at[ps, rws], buf.at[2 * k - 1, ps, rws], az_at(k)) for k in range(1, groups)])
        beside.append(remote(source.at[ps, rws], buf.at[0, ps, rws], sibling))
        for c in across[-1]:
            c.start()
            sent.append(c)
    for c in beside:
        c.start()
        sent.append(c)

    def arrive(i):
        p0, np_, r0, nr = pieces[i]
        ps, rws = pl.ds(p0, np_), pl.ds(r0, nr)
        forwards = []
        for k in range(1, groups):
            across[i][k - 1].wait_recv()
            f = remote(buf.at[2 * k - 1, ps, rws], buf.at[2 * k, ps, rws], sibling)
            f.start()
            sent.append(f)
            forwards.append(f)
        beside[i].wait_recv()
        for f in forwards:
            f.wait_recv()

    lane = lax.broadcasted_iota(jnp.int32, (SUB, LANES), 1)

    def shift_tile(tile, p0, np_):
        r = pl.ds(tile * SUB, SUB)
        sub = lax.broadcasted_iota(jnp.int32, (SUB, LANES), 0)
        amount = jnp.full((SUB, LANES), offs[tile * SUB], jnp.int32)
        for k in range(1, SUB):
            amount = jnp.where(sub == k, offs[tile * SUB + k], amount)
        block = amount // width
        within = amount - block * width
        column = within // LANES
        rem = within - column * LANES
        pick = (lane - rem) & (LANES - 1)
        low = lane < rem

        def one(p, carry):
            def load(d, c):
                cs = pl.ds(c * LANES, LANES)
                if d == 0:
                    return state[p, r, cs]
                if d % 2 == 0:
                    return buf[d - 1, p, r, cs]
                slot = jnp.where(core == 1, d, (d + 2) % n_az)
                return buf[slot - 1, p, r, cs]

            line = []
            for move, c in [(1, c) for c in range(cols)] + [(0, c) for c in range(cols)] + [(-1, 0)]:
                value = load(move % n_az, c)
                for b in range(1, n_az):
                    value = jnp.where(block == b, load((b + move) % n_az, c), value)
                line.append(value)
            step = cols // 2
            while step:
                chosen = (column & step) != 0
                line = [jnp.where(chosen, line[i - step], line[i]) for i in range(step, len(line))]
                step //= 2
            turned = [jnp.take_along_axis(v, pick, axis=1, mode="promise_in_bounds") for v in line]
            x = [turned[0]] + [jnp.where(low, turned[j - 1], turned[j]) for j in range(1, len(turned))]
            right = [pltpu.roll(v, 1, 1) for v in x[:-1]]
            left = [pltpu.roll(v, LANES - 1, 1) for v in x[1:]]
            for c in range(cols):
                cs = pl.ds(c * LANES, LANES)
                mid = x[c + 1]
                prev = jnp.where(lane == 0, right[c], right[c + 1])
                nxt = jnp.where(lane == LANES - 1, left[c + 1], left[c])
                sh[p, pl.ds(SUB + tile * SUB, SUB), cs] = mid
                out[p, r, cs] = mid + AZIMUTH_COEF * (nxt + prev - 2.0 * mid)
                if tile == 0:
                    eo[0, p, :, cs] = mid[:1]
                if tile == tiles - 1:
                    eo[1, p, :, cs] = mid[SUB - 1:]
            return carry

        lax.fori_loop(p0, p0 + np_, one, 0)

    hops = []

    def scan_send():
        i = len(hops)
        d = 1 << i
        if d < n_rad:
            c = remote(tot_out.at[i], tot_in.at[i], rad_at(d))
            goes = rad + d < n_rad
            pl.when(goes)(c.start)
            chained.append((goes, c))
            hops.append(c)

    def scan_take():
        i = len(hops) - 1
        pl.when(rad >= 1 << i)(hops[i].wait_recv)
        tot_out[i + 1] = tot_out[i] + tot_in[i]

    def send_edge(side, p0, np_):
        ps = pl.ds(p0, np_)
        c = remote(eo.at[side, ps], ei.at[1 - side, ps], rad_at(-1 if side == 0 else 1))
        goes, comes = (inner, outer) if side == 0 else (outer, inner)
        pl.when(goes)(c.start)
        chained.append((goes, c))
        return comes, c

    def edge_wait(edge):
        pl.when(edge[0])(edge[1].wait_recv)

    def place_edges(p0, np_):
        def one(p, carry):
            sh[p, SUB - 1:SUB, :] = jnp.where(rad > 0, ei[0, p], 0.0)
            sh[p, SUB + rows:SUB + rows + 1, :] = jnp.where(rad < n_rad - 1, ei[1, p], 0.0)
            return carry

        lax.fori_loop(p0, p0 + np_, one, 0)

    def smooth(tile, p0, np_):
        top = SUB + tile * SUB

        def one(p, carry):
            r = pl.ds(tile * SUB, SUB)
            mid = sh[p, top:top + SUB, :]
            up = sh[p, top - 1:top + SUB - 1, :]
            down = sh[p, top + 1:top + SUB + 1, :]
            out[p, r, :] = out[p, r, :] + visc[lax.rem(p, 2), r, :] * (down + up - 2.0 * mid)
            return carry

        lax.fori_loop(p0, p0 + np_, one, 0)

    for c in fetches:
        c.start()
    arrive(0)
    for c in fetches:
        c.wait()
    for t in range(tiles):
        shift_tile(t, dust, 2)
    edges = [send_edge(s, dust, 2) for s in (0, 1)]
    for e in edges:
        edge_wait(e)
    place_edges(dust, 2)
    for t in range(tiles):
        smooth(t, dust, 2)

    row = lax.broadcasted_iota(jnp.int32, (SUB, width), 0)
    for h in range(2):
        base = jnp.zeros((1, width), jnp.float32)
        for t in range(tiles):
            r = pl.ds(t * SUB, SUB)
            step = 2.0 * absorb[h, r, :] * out[dust + h, r, :] / total_rows
            run = step
            for k in (1, 2, 4):
                run = run + jnp.where(row >= k, pltpu.roll(run, k, 0), 0.0)
            run = run + base
            depth[h, r, :] = run - 0.5 * step
            base = run[SUB - 1:]
        tot_out[0, h] = base
    scan_send()
    arrive(1)
    shift_tile(0, 0, rest)
    edge_in = send_edge(0, 0, rest)
    scan_take()
    scan_send()
    arrive(2)
    shift_tile(tiles - 1, 0, rest)
    edge_out = send_edge(1, 0, rest)

    scan_take()
    while 1 << len(hops) < n_rad:
        scan_send()
        scan_take()
    for h in range(2):
        carried = tot_in[0, h]
        for i in range(1, len(hops)):
            carried = carried + tot_in[i, h]
        for t in range(tiles):
            r = pl.ds(t * SUB, SUB)
            radius = (rad * rows + t * SUB + row).astype(jnp.float32) + 0.5
            flux = 1.0 / (1.0 + radius / total_rows)
            depth[h, r, :] = depth[h, r, :] + carried
            heat[h, r, :] = flux * jnp.exp(-depth[h, r, :])

    def warm(tile):
        r = pl.ds(tile * SUB, SUB)
        for h in range(2):
            out[rest - 2 + h, r, :] = out[rest - 2 + h, r, :] + heat[h, r, :]

    edge_wait(edge_in)
    edge_wait(edge_out)
    place_edges(0, rest)
    i = 3
    for t in range(1, tiles - 2):
        arrive(i)
        shift_tile(t, 0, rest)
        smooth(t - 1, 0, rest)
        warm(t - 1)
        i += 1
    first = max(tiles - 3, 0)
    for p0, np_ in tail:
        arrive(i)
        shift_tile(tiles - 2, p0, np_)
        for t in range(first, tiles):
            smooth(t, p0, np_)
            if p0 + np_ == rest:
                warm(t)
        i += 1
    for goes, c in chained:
        pl.when(goes)(c.wait_send)
    for c in sent:
        c.wait_send()


def full(n_rad, n_az, state, offsets, viscosity, absorb):
    fields, polar, rows, width = state.shape
    planes = fields * polar
    groups = n_az // 2
    tiles = rows // SUB
    n_tail = len(tail_planes(planes - 2))
    n_pieces = 1 + 2 + max(tiles - 3, 0) + n_tail
    n_scan = (n_rad - 1).bit_length()
    n_local = 1
    n_sems = n_pieces * (2 * (groups - 1) + 1) + 4 + n_scan
    f32 = jnp.float32
    vm = pl.BlockSpec(memory_space=pltpu.VMEM)
    hbm = pl.BlockSpec(memory_space=pl.ANY)
    moved, local = pl.pallas_call(
        functools.partial(kernel, n_rad, n_az, n_local),
        out_shape=(
            pltpu.VMEM((planes, rows, width), f32),
            pltpu.VMEM((polar, rows, width), f32),
        ),
        in_specs=[hbm, pl.BlockSpec(memory_space=pltpu.SMEM), hbm, hbm],
        out_specs=(vm, vm),
        scratch_shapes=[
            pltpu.VMEM((polar, rows, width), f32),
            pltpu.VMEM((polar, rows, width), f32),
            pltpu.VMEM((polar, rows, width), f32),
            pltpu.VMEM((planes, rows, width), f32),
            pltpu.VMEM((n_az - 1, planes, rows, width), f32),
            pltpu.VMEM((planes, rows + 2 * SUB, width), f32),
            pltpu.VMEM((2, planes, 1, width), f32),
            pltpu.VMEM((2, planes, 1, width), f32),
            pltpu.VMEM((n_scan + 1, polar, 1, width), f32),
            pltpu.VMEM((n_scan, polar, 1, width), f32),
            pltpu.SemaphoreType.DMA((n_sems,)),
            pltpu.SemaphoreType.DMA((n_sems,)),
            pltpu.SemaphoreType.DMA((n_local + 2,)),
        ],
        compiler_params=pltpu.CompilerParams(
            collective_id=0, has_side_effects=True, vmem_limit_bytes=56 * 2**20
        ),
    )(state.reshape(planes, rows, width), offsets, viscosity, absorb)
    return moved, local


def fast_kernel(n_rad, n_az, cap, dust_cap, source, offs_in, visc_in, absorb_in, out, depth, flag,
                visc, absorb, heat, gathered, packed, pool_mine, pool_other, early_mine, early_other,
                stage, sh, eo, ei, tot_out, tot_in, take_v, look_v, take, look, offs, ss, rs, ls):
    rad = lax.axis_index("rad")
    az = lax.axis_index("az")
    core = lax.rem(az, 2)
    chip = az // 2
    sibling = {"az": az + 1 - 2 * core}
    across = {"az": lax.rem(az + 2, n_az)}
    planes, rows, width = out.shape
    polar = 2
    fields = planes // polar
    cols = width // LANES
    col_bits = cols.bit_length() - 1
    tiles = rows // SUB
    units = rows * cols
    half = 2 * units
    ring = 2 * cols
    span = cols + 2
    total_rows = rows * n_rad
    dust, energy = fields - 1, fields - 2
    order = [dust, energy] + list(range(energy))
    last = order[-1]
    n_scan = (n_rad - 1).bit_length()
    n_early = 2 * ring
    n_raw = SUB * cols
    raw_at = half + cap
    take_rows = -(-cap // LANES)

    def rad_at(k):
        return {"rad": lax.rem(rad + k + n_rad, n_rad)}

    def rad_pair(i):
        d = 1 << i
        upper = lax.rem(rad // d, 2)
        return {"rad": rad + d - 2 * d * upper}, upper

    count = [0, 0]

    def remote(src, dst, device):
        i = count[0]
        count[0] += 1
        return pltpu.make_async_remote_copy(
            src_ref=src, dst_ref=dst, send_sem=ss.at[i], recv_sem=rs.at[i],
            device_id=device, device_id_type=pl.DeviceIdType.MESH,
        )

    def local(src, dst):
        i = count[1]
        count[1] += 1
        c = pltpu.make_async_copy(src, dst, ls.at[i])
        c.start()
        return c

    offs_copy = local(offs_in, offs)
    inner, outer = rad > 0, rad < n_rad - 1
    barrier = pltpu.get_barrier_semaphore()
    for peer in [rad_pair(i)[0] for i in reversed(range(1, n_scan))]:
        pl.semaphore_signal(barrier, inc=1, device_id=peer, device_id_type=pl.DeviceIdType.MESH)
    for there, k in ((inner, -1), (outer, 1)):
        @pl.when(there)
        def _():
            pl.semaphore_signal(barrier, inc=1, device_id=rad_at(k), device_id_type=pl.DeviceIdType.MESH)
    for peer in [sibling, across]:
        pl.semaphore_signal(barrier, inc=1, device_id=peer, device_id_type=pl.DeviceIdType.MESH)
    for edge, k in ((rad == 0, 0), (rad == n_rad - 1, 1)):
        @pl.when(edge)
        def _():
            ei[k] = jnp.zeros(ei.shape[1:], jnp.float32)

    mine = pl.ds(core * units, units)
    first_pack = [local(source.at[polar * f + core], gathered[f].at[mine]) for f in order[:1]]

    pl.semaphore_wait(barrier, 2 + n_scan - 1 + inner.astype(jnp.int32) + outer.astype(jnp.int32))

    sent, chained = [], []
    to_pack = [remote(source.at[polar * f + 1 - core], gathered[f].at[mine], sibling) for f in order]
    to_mine = [remote(source.at[polar * f + 1 - core], pool_mine[f].at[mine], sibling) for f in order]
    to_other = [remote(source.at[polar * f + core], pool_other[f].at[mine], sibling) for f in order]
    to_early = [
        remote(source.at[polar * last + 1 - core], early_mine.at[mine], sibling),
        remote(source.at[polar * last + core], early_other.at[mine], sibling),
    ]
    sent += to_pack + to_mine + to_other + to_early
    to_pack[0].start()
    raw_mine = remote(
        source.at[polar * dust + core, pl.ds(0, n_raw)],
        pool_mine[dust].at[pl.ds(raw_at + core * n_raw, n_raw)], across,
    )
    raw_other = remote(
        source.at[polar * dust + 1 - core, pl.ds(0, n_raw)],
        pool_other[dust].at[pl.ds(raw_at + core * n_raw, n_raw)], across,
    )
    for c in (raw_mine, raw_other):
        c.start()
        sent.append(c)
    lane = lax.broadcasted_iota(jnp.int32, (SUB, LANES), 1)
    sub = lax.broadcasted_iota(jnp.int32, (SUB, LANES), 0)

    def row_offsets(numbers):
        amount = jnp.full((SUB, LANES), offs[numbers[0]], jnp.int32)
        for k in range(1, len(numbers)):
            amount = jnp.where(sub == k, offs[numbers[k]], amount)
        return amount

    def block_unit(b):
        return (b >> col_bits) * units + (b & (cols - 1)) * SUB

    offs_copy.wait()
    shifts = [row_offsets([t * SUB + k for k in range(SUB)]) for t in range(tiles)]
    leads, manys, befores = [], [], []
    used = jnp.zeros((SUB, LANES), jnp.int32)
    for off in shifts:
        lead = jnp.where(off == 0, ring - 1, jnp.where(off < 2 * width, (2 * width - 1 - off) >> LANE_BITS, 0))
        many = jnp.where(off < 2 * width, ring - lead, jnp.minimum(((4 * width - off) >> LANE_BITS) + 1, ring))
        many = jnp.where(off == 0, 2, many)
        run = many
        for k in (1, 2, 4):
            run = run + jnp.where(sub >= k, pltpu.roll(run, k, 0), 0)
        leads.append(lead)
        manys.append(many)
        befores.append(run - many + used)
        used = used + jnp.broadcast_to(run[SUB - 1:], (SUB, LANES))
    top_many = jnp.broadcast_to(manys[0][:1], (SUB, LANES))
    bottom_many = jnp.broadcast_to(manys[-1][SUB - 1:], (SUB, LANES))
    bases = []
    for t in range(tiles):
        base = befores[t] + bottom_many
        if t == 0:
            base = jnp.where(sub == 0, 0, base)
        if t == tiles - 1:
            base = jnp.where(sub == SUB - 1, top_many, base)
        bases.append(base)
    top_used = befores[1]
    top_used = jnp.broadcast_to(top_used[:1], (SUB, LANES))
    dust_bases = [None] + [before - top_used for before in befores[1:]]
    for size, heads, first, at in ((dust_cap, dust_bases, 1, take_rows), (cap, bases, 0, 0)):
        for q in range(-(-size // LANES)):
            j = q * LANES + lane
            place = jnp.zeros((SUB, LANES), jnp.int32)
            ahead = jnp.zeros((SUB, LANES), jnp.int32)
            for t in range(first, tiles):
                held = (j >= heads[t]) & (j < heads[t] + manys[t])
                place = place + jnp.where(held, t * SUB * cols + sub, 0)
                ahead = ahead + jnp.where(held, leads[t] - heads[t], 0)
            for k in (4, 2, 1):
                place = place + pltpu.roll(place, k, 0)
                ahead = ahead + pltpu.roll(ahead, k, 0)
            take_v[at + q:at + q + 1, :] = (block_unit((j + ahead) & (ring - 1)) + place)[:1]
    take_copy = local(take_v, take)
    for t in range(tiles):
        b = az * cols - (shifts[t] >> LANE_BITS) - 1 + lane + 2 * ring
        near = block_unit(b & (ring - 1)) + (t * SUB * cols + sub)
        here = ((b >> (col_bits + 1)) & 1) == chip
        step = (b - leads[t]) & (ring - 1)
        far = half + jnp.minimum(bases[t] + step, cap - 1)
        look_v[t * SUB:(t + 1) * SUB, :] = jnp.where(here, near, far)
        if t == 0:
            far = raw_at + ((b & (ring - 1)) >> col_bits) * n_raw + (b & (cols - 1)) * SUB + sub
        else:
            far = half + jnp.minimum(dust_bases[t] + step, dust_cap - 1)
        look_v[rows + t * SUB:rows + (t + 1) * SUB, :] = jnp.where(here, near, far)
    look_copy = local(look_v, look)

    crossing = {f: [] for f in order}
    cuts = {f: [0, cap // 2 // SUB * SUB, cap] for f in order}
    cuts[dust] = [0, dust_cap // 4 // SUB * SUB, dust_cap * 5 // 8 // SUB * SUB, dust_cap]
    cuts[last] = [n_early, (n_early + cap) // 2 // SUB * SUB, cap]

    def pack(some, lo, hi):
        def eight(k, carry):
            for s in range(SUB):
                u = take[(k >> 4) + (take_rows if some[0] == dust else 0), (k & 15) * SUB + s]
                for f in some:
                    packed[f][pl.ds(k * SUB + s, 1), :] = gathered[f][pl.ds(u, 1), :]
            return carry

        lax.fori_loop(lo // SUB, hi // SUB, eight, 0)

    def pack_ready(f):
        own_pack[order.index(f)].wait()
        to_pack[order.index(f)].wait_recv()

    def pack_send(f):
        for lo, hi in zip(cuts[f], cuts[f][1:]):
            pack([f], lo, hi)
            c = remote(packed[f].at[pl.ds(lo, hi - lo)], pool_mine[f].at[pl.ds(half + lo, hi - lo)], across)
            c.start()
            sent.append(c)
            crossing[f].append(c)

    def shift_rows(f, numbers, shift, source_ref, slot, write):
        shown = []
        for i in range(span):
            value = None
            for s, r in enumerate(numbers):
                u = look[r + (rows if f == dust else 0), i]
                strip = jnp.broadcast_to(source_ref[pl.ds(u, 1), :], (SUB, LANES))
                value = strip if s == 0 else jnp.where(sub == s, strip, value)
            shown.append(value)
        rem = shift & (LANES - 1)
        pick = (lane - rem) & (LANES - 1)
        low = lane < rem
        turned = [
            jnp.take_along_axis(shown[i], pick, axis=1, mode="promise_in_bounds") for i in range(span)
        ]
        x = [turned[0]] + [jnp.where(low, turned[j - 1], turned[j]) for j in range(1, span)]
        write(x)

    def shift_plane(f, source_ref, p):
        def one(tile):
            r = pl.ds(tile * SUB, SUB)
            below = pl.ds(SUB + tile * SUB, SUB)

            def write(x):
                right = [pltpu.roll(v, 1, 1) for v in x[:-1]]
                left = [pltpu.roll(v, LANES - 1, 1) for v in x[1:]]
                for c in range(cols):
                    cs = pl.ds(c * LANES, LANES)
                    mid = x[c + 1]
                    prev = jnp.where(lane == 0, right[c], right[c + 1])
                    nxt = jnp.where(lane == LANES - 1, left[c + 1], left[c])
                    sh[p, below, cs] = mid
                    out[p, r, cs] = mid + AZIMUTH_COEF * (nxt + prev - 2.0 * mid)

            numbers = [tile * SUB + s for s in range(SUB)]
            shift_rows(f, numbers, row_offsets(numbers), source_ref, tile, write)

        for t in range(tiles):
            one(t)

    def send_edges(f):
        ps = pl.ds(polar * f, polar)
        got = []
        for side in range(2):
            c = remote(eo.at[side, ps], ei.at[1 - side, ps], rad_at(-1 if side == 0 else 1))
            goes, comes = (inner, outer) if side == 0 else (outer, inner)
            pl.when(goes)(c.start)
            chained.append((goes, c))
            got.append((comes, c))
        return got

    def take_edges(f, got):
        for comes, c in got:
            pl.when(comes)(c.wait_recv)
        for h in range(polar):
            p = polar * f + h
            sh[p, SUB - 1:SUB, :] = jnp.where(rad > 0, ei[0, p], 0.0)
            sh[p, SUB + rows:SUB + rows + 1, :] = jnp.where(rad < n_rad - 1, ei[1, p], 0.0)

    def smooth(f, h):
        p = polar * f + h
        for tile in range(tiles):
            top = SUB + tile * SUB
            r = pl.ds(tile * SUB, SUB)
            mid = sh[p, top:top + SUB, :]
            up = sh[p, top - 1:top + SUB - 1, :]
            down = sh[p, top + 1:top + SUB + 1, :]
            new = out[p, r, :] + visc[h, r, :] * (down + up - 2.0 * mid)
            if f == energy:
                new = new + heat[h, r, :]
            out[p, r, :] = new

    def forward(f):
        i = order.index(f)
        onward = []
        for c, lo, hi in zip(crossing[f], cuts[f], cuts[f][1:]):
            c.wait_recv()
            at = pl.ds(half + lo, hi - lo)
            c = remote(pool_mine[f].at[at], pool_other[f].at[at], sibling)
            c.start()
            sent.append(c)
            onward.append(c)
        own_mine[i].wait()
        to_mine[i].wait_recv()
        return onward

    def other_ready(f, onward):
        i = order.index(f)
        own_other[i].wait()
        to_other[i].wait_recv()
        for c in onward:
            c.wait_recv()

    def work(f):
        onward = forward(f)
        shift_plane(f, pool_mine[f], polar * f + core)
        other_ready(f, onward)
        shift_plane(f, pool_other[f], polar * f + 1 - core)
        for h in range(polar):
            p = polar * f + h
            eo[0, p] = sh[p, SUB:SUB + 1, :]
            eo[1, p] = sh[p, SUB + rows - 1:SUB + rows, :]
        return send_edges(f)

    def finish(f, got):
        take_edges(f, got)
        for h in range(polar):
            smooth(f, h)

    def flush(but=()):
        for goes, c in chained:
            pl.when(goes)(c.wait_send)
        for c in sent:
            if not any(c is b for b in but):
                c.wait_send()
        sent[:] = but
        chained.clear()

    early_at = pl.ds(half, n_early)

    def early_edges():
        crossing_early.wait_recv()
        onward = remote(early_mine.at[early_at], early_other.at[early_at], sibling)
        onward.start()
        sent.append(onward)
        numbers = [0, rows - 1]
        for c in own_early:
            c.wait()
        for c in to_early:
            c.wait_recv()
        copies = [local(early_mine.at[early_at], pool_mine[last].at[early_at])]
        for ref, hh in ((early_mine, core), (early_other, 1 - core)):
            p = polar * last + hh
            if ref is early_other:
                onward.wait_recv()
                copies.append(local(early_other.at[early_at], pool_other[last].at[early_at]))

            def write(x):
                for c in range(cols):
                    cs = pl.ds(c * LANES, LANES)
                    eo[0, p, :, cs] = x[c + 1][:1]
                    eo[1, p, :, cs] = x[c + 1][1:2]

            shift_rows(last, numbers, row_offsets(numbers), ref, 0, write)
        got = send_edges(last)
        for c in copies:
            c.wait()
        return got

    own_pack = first_pack
    take_copy.wait()
    to_pack[1].start()
    pack_ready(dust)
    pack_send(dust)
    own_pack = first_pack + [local(source.at[polar * f + core], gathered[f].at[mine]) for f in order[1:]]
    for c in to_pack[2:]:
        c.start()
    look_copy.wait()
    pack_ready(energy)
    pack_send(energy)
    raw_here = pl.ds(raw_at + core * n_raw, n_raw)
    raw_onward = []
    for c, src, dst in ((raw_mine, pool_mine, pool_other), (raw_other, pool_other, pool_mine)):
        c.wait_recv()
        c = remote(src[dust].at[raw_here], dst[dust].at[raw_here], sibling)
        c.start()
        sent.append(c)
        raw_onward.append(c)
    own_mine, own_other = [], []

    def fill_pools(i):
        f = order[i]
        to_mine[i].start()
        to_other[i].start()
        own_mine.append(local(source.at[polar * f + core], pool_mine[f].at[mine]))
        own_other.append(local(source.at[polar * f + 1 - core], pool_other[f].at[mine]))

    fill_pools(0)
    params = [local(visc_in, visc), local(absorb_in, absorb)]
    pack_ready(last)
    pack([last], 0, n_early)
    crossing_early = remote(packed[last].at[pl.ds(0, n_early)], early_mine.at[early_at], across)
    crossing_early.start()
    sent.append(crossing_early)
    for i in range(2, fields - 1):
        pack_ready(order[i])
        pack_send(order[i])
        fill_pools(i - 1)
    own_early = [
        local(source.at[polar * last + core], early_mine.at[mine]),
        local(source.at[polar * last + 1 - core], early_other.at[mine]),
    ]
    for c in to_early:
        c.start()
    pack_send(last)
    for i in range(fields - 2, fields):
        fill_pools(i)
    for c in params:
        c.wait()

    for c in raw_onward:
        c.wait_recv()
    finish(dust, work(dust))

    row = lax.broadcasted_iota(jnp.int32, (SUB, width), 0)
    for h in range(polar):
        run_last = jnp.zeros((1, width), jnp.float32)
        for t in range(tiles):
            r = pl.ds(t * SUB, SUB)
            step = 2.0 * absorb[h, r, :] * out[polar * dust + h, r, :] / total_rows
            run = step
            for k in (1, 2, 4):
                run = run + jnp.where(row >= k, pltpu.roll(run, k, 0), 0.0)
            run = run + run_last
            depth[h, r, :] = run - 0.5 * step
            run_last = run[SUB - 1:]
        tot_out[0, h] = run_last
    over = ((used > cap) | (used - top_used > dust_cap)).astype(jnp.float32)[:1]
    for c in range(cols):
        tot_out[0, polar, :, pl.ds(c * LANES, LANES)] = over

    hops = []

    def scan_send():
        i = len(hops)
        peer, upper = rad_pair(i)
        c = remote(tot_out.at[i], tot_in.at[i], peer)
        c.start()
        sent.append(c)
        hops.append((c, upper))

    def scan_take():
        i = len(hops) - 1
        hops[i][0].wait_recv()
        tot_out[i + 1] = tot_out[i] + tot_in[i]

    def irradiate():
        for h in range(polar):
            carried = jnp.where(hops[0][1] == 1, tot_in[0, h], 0.0)
            for i in range(1, n_scan):
                carried = carried + jnp.where(hops[i][1] == 1, tot_in[i, h], 0.0)
            for t in range(tiles):
                r = pl.ds(t * SUB, SUB)
                radius = (rad * rows + t * SUB + row).astype(jnp.float32) + 0.5
                flux = 1.0 / (1.0 + radius / total_rows)
                depth[h, r, :] = depth[h, r, :] + carried
                heat[h, r, :] = flux * jnp.exp(-depth[h, r, :])
        flag[0] = jnp.max(tot_out[n_scan, polar])

    scan_send()
    pending = []
    for f in order[1:-1]:
        if f == order[2]:
            last_edges = early_edges()
        pending.append((f, work(f)))
        if len(hops) < n_scan:
            scan_take()
            scan_send()
            ready = [w for w in pending[:-1] if w[0] != energy]
        else:
            if energy in [w[0] for w in pending]:
                scan_take()
                irradiate()
            ready = pending[:-1]
        for w in ready:
            finish(*w)
            pending.remove(w)
    take_edges(last, last_edges)
    flush(crossing[last])
    onward = forward(last)
    shift_plane(last, pool_mine[last], polar * last + core)
    smooth(last, core)
    other_ready(last, onward)
    shift_plane(last, pool_other[last], polar * last + 1 - core)
    smooth(last, 1 - core)
    for w in pending:
        finish(*w)
    flush()


def fast(n_rad, n_az, state, offsets, viscosity, absorb):
    fields, polar, rows, width = state.shape
    planes = fields * polar
    cols = width // LANES
    units = rows * cols
    cap = units * 2 * 11 // 16 // 16 * 16
    dust_cap = (units - SUB * cols) * 2 * 73 // 100 // SUB * SUB
    n_early = 4 * cols
    n_take = -(-(-(-cap // LANES) - (-dust_cap // LANES)) // SUB) * SUB
    n_scan = (n_rad - 1).bit_length()
    n_sems = 9 * fields + 2 + 4 + 4 + n_scan
    pools = [2 * units + cap] * (fields - 1) + [2 * units + cap + 2 * SUB * cols]
    f32, i32 = jnp.float32, jnp.int32
    vm = pl.BlockSpec(memory_space=pltpu.VMEM)
    hbm = pl.BlockSpec(memory_space=pl.ANY)
    source = state.reshape(planes, rows // SUB, SUB, cols, LANES).transpose(0, 1, 3, 2, 4).reshape(planes, units, LANES)
    moved, local, flag = pl.pallas_call(
        functools.partial(fast_kernel, n_rad, n_az, cap, dust_cap),
        out_shape=(
            pltpu.VMEM((planes, rows, width), f32),
            pltpu.VMEM((polar, rows, width), f32),
            pltpu.SMEM((1,), f32),
        ),
        in_specs=[hbm, hbm, hbm, hbm],
        out_specs=(vm, vm, pl.BlockSpec(memory_space=pltpu.SMEM)),
        scratch_shapes=[
            pltpu.VMEM((polar, rows, width), f32),
            pltpu.VMEM((polar, rows, width), f32),
            pltpu.VMEM((polar, rows, width), f32),
            [pltpu.VMEM((2 * units, LANES), f32)] * fields,
            [pltpu.VMEM((cap, LANES), f32)] * fields,
            [pltpu.VMEM((n, LANES), f32) for n in pools],
            [pltpu.VMEM((n, LANES), f32) for n in pools],
            pltpu.VMEM((2 * units + n_early, LANES), f32),
            pltpu.VMEM((2 * units + n_early, LANES), f32),
            pltpu.VMEM((rows // SUB, cols + 2, SUB, LANES), f32),
            pltpu.VMEM((planes, rows + 2 * SUB, width), f32),
            pltpu.VMEM((2, planes, 1, width), f32),
            pltpu.VMEM((2, planes, 1, width), f32),
            pltpu.VMEM((n_scan + 1, polar + 1, 1, width), f32),
            pltpu.VMEM((n_scan, polar + 1, 1, width), f32),
            pltpu.VMEM((n_take, LANES), i32),
            pltpu.VMEM((2 * rows, LANES), i32),
            pltpu.SMEM((n_take, LANES), i32),
            pltpu.SMEM((2 * rows, LANES), i32),
            pltpu.SMEM((rows,), i32),
            pltpu.SemaphoreType.DMA((n_sems,)),
            pltpu.SemaphoreType.DMA((n_sems,)),
            pltpu.SemaphoreType.DMA((3 * fields + 10,)),
        ],
        compiler_params=pltpu.CompilerParams(
            collective_id=1, has_side_effects=True, vmem_limit_bytes=61 * 2**20
        ),
    )(source, offsets, viscosity, absorb)
    return moved, local, flag[0]


def hand_out(moved, local):
    def store(a, b, x, y, sems):
        copies = [pltpu.make_async_copy(a, x, sems.at[0]), pltpu.make_async_copy(b, y, sems.at[1])]
        for c in copies:
            c.start()
        for c in copies:
            c.wait()

    hbm = pl.BlockSpec(memory_space=pl.ANY)
    vm = pl.BlockSpec(memory_space=pltpu.VMEM)
    return pl.pallas_call(
        store,
        out_shape=(pltpu.HBM(moved.shape, moved.dtype), pltpu.HBM(local.shape, local.dtype)),
        in_specs=[vm, vm],
        out_specs=(hbm, hbm),
        scratch_shapes=[pltpu.SemaphoreType.DMA((2,))],
    )(moved, local)


def body(n_rad, n_az, state, offsets, viscosity, absorb):
    args = (state, offsets, viscosity, absorb)
    if n_az != 4 or state.shape[1] != 2 or n_rad not in (2, 4, 8, 16):
        moved, local = full(n_rad, n_az, *args)
    else:
        moved, local, flag = fast(n_rad, n_az, *args)
        moved, local = lax.cond(
            flag > 0, lambda m, d: tuple(full(n_rad, n_az, *args)), lambda m, d: (m, d), moved, local
        )
    moved, local = hand_out(moved, local)
    return moved.reshape(state.shape), local


def solution(mesh):
    in_specs = (P(None, None, "rad", "az"), P("rad"), P(None, "rad", "az"), P(None, "rad", "az"))
    out_specs = (P(None, None, "rad", "az"), P(None, "rad", "az"))
    f = functools.partial(body, mesh.shape["rad"], mesh.shape["az"])
    return jax.shard_map(f, mesh=mesh, in_specs=in_specs, out_specs=out_specs, check_vma=False)
```

```python
import functools

import jax
import jax.numpy as jnp
from jax import lax
from jax.experimental import pallas as pl
from jax.experimental.pallas import tpu as pltpu
from jax.sharding import PartitionSpec as P

AZIMUTH_COEF = 0.1
LANES = 128
SUB = 8
LANE_BITS = 7
SUB_BITS = 3


def tail_planes(rest):
    cuts = [0, rest // 2, rest]
    return [(a, b - a) for a, b in zip(cuts, cuts[1:]) if b > a]


def kernel(n_rad, n_az, n_local, source, offs, visc_in, absorb_in, out, depth,
           visc, absorb, heat, state, buf, sh, eo, ei, tot_out, tot_in, ss, rs, ls):
    groups = n_az // 2
    rad = lax.axis_index("rad")
    az = lax.axis_index("az")
    core = lax.rem(az, 2)
    sibling = {"az": az + 1 - 2 * core}
    planes, rows, width = state.shape
    cols = width // LANES
    tiles = rows // SUB
    dust = planes - 2
    rest = dust
    total_rows = rows * n_rad

    def rad_at(k):
        return {"rad": lax.rem(rad + k + n_rad, n_rad)}

    def az_at(k):
        return {"az": lax.rem(az + 2 * k, n_az)}

    count = [0]

    def remote(src, dst, device):
        i = count[0]
        count[0] += 1
        return pltpu.make_async_remote_copy(
            src_ref=src, dst_ref=dst, send_sem=ss.at[i], recv_sem=rs.at[i],
            device_id=device, device_id_type=pl.DeviceIdType.MESH,
        )

    fetch = pltpu.make_async_copy(source, state, ls.at[0])
    fetches = [fetch] + [
        pltpu.make_async_copy(a, b, ls.at[n_local + i])
        for i, (a, b) in enumerate(((visc_in, visc), (absorb_in, absorb)))
    ]
    inner, outer = rad > 0, rad < n_rad - 1
    ei[...] = jnp.zeros_like(ei)
    tot_in[...] = jnp.zeros_like(tot_in)
    peers = [az_at(k) for k in range(1, groups)] + [sibling]
    barrier = pltpu.get_barrier_semaphore()
    for there, k in ((inner, -1), (outer, 1)):
        @pl.when(there)
        def _():
            pl.semaphore_signal(barrier, inc=1, device_id=rad_at(k), device_id_type=pl.DeviceIdType.MESH)
    for peer in peers:
        pl.semaphore_signal(barrier, inc=1, device_id=peer, device_id_type=pl.DeviceIdType.MESH)
    senders = len(peers)
    d = 1
    while d < n_rad:
        if d > 1:
            @pl.when(rad >= d)
            def _():
                pl.semaphore_signal(barrier, inc=1, device_id=rad_at(-d), device_id_type=pl.DeviceIdType.MESH)
            senders = senders + (rad + d < n_rad).astype(jnp.int32)
        d *= 2
    pl.semaphore_wait(barrier, senders + inner.astype(jnp.int32) + outer.astype(jnp.int32))

    pieces = [(dust, 2, 0, rows)]
    edge_tiles = [0, tiles - 1]
    for t in edge_tiles + list(range(1, tiles - 2)):
        pieces.append((0, rest, t * SUB, SUB))
    tail = tail_planes(rest)
    for p0, np_ in tail:
        pieces.append((p0, np_, (tiles - 2) * SUB, SUB))

    sent, chained = [], []
    across, beside = [], []
    for p0, np_, r0, nr in pieces:
        ps, rws = pl.ds(p0, np_), pl.ds(r0, nr)
        across.append([remote(source.at[ps, rws], buf.at[2 * k - 1, ps, rws], az_at(k)) for k in range(1, groups)])
        beside.append(remote(source.at[ps, rws], buf.at[0, ps, rws], sibling))
        for c in across[-1]:
            c.start()
            sent.append(c)
    for c in beside:
        c.start()
        sent.append(c)

    def arrive(i):
        p0, np_, r0, nr = pieces[i]
        ps, rws = pl.ds(p0, np_), pl.ds(r0, nr)
        forwards = []
        for k in range(1, groups):
            across[i][k - 1].wait_recv()
            f = remote(buf.at[2 * k - 1, ps, rws], buf.at[2 * k, ps, rws], sibling)
            f.start()
            sent.append(f)
            forwards.append(f)
        beside[i].wait_recv()
        for f in forwards:
            f.wait_recv()

    lane = lax.broadcasted_iota(jnp.int32, (SUB, LANES), 1)

    def shift_tile(tile, p0, np_):
        r = pl.ds(tile * SUB, SUB)
        sub = lax.broadcasted_iota(jnp.int32, (SUB, LANES), 0)
        amount = jnp.full((SUB, LANES), offs[tile * SUB], jnp.int32)
        for k in range(1, SUB):
            amount = jnp.where(sub == k, offs[tile * SUB + k], amount)
        block = amount // width
        within = amount - block * width
        column = within // LANES
        rem = within - column * LANES
        pick = (lane - rem) & (LANES - 1)
        low = lane < rem

        def one(p, carry):
            def load(d, c):
                cs = pl.ds(c * LANES, LANES)
                if d == 0:
                    return state[p, r, cs]
                if d % 2 == 0:
                    return buf[d - 1, p, r, cs]
                slot = jnp.where(core == 1, d, (d + 2) % n_az)
                return buf[slot - 1, p, r, cs]

            line = []
            for move, c in [(1, c) for c in range(cols)] + [(0, c) for c in range(cols)] + [(-1, 0)]:
                value = load(move % n_az, c)
                for b in range(1, n_az):
                    value = jnp.where(block == b, load((b + move) % n_az, c), value)
                line.append(value)
            step = cols // 2
            while step:
                chosen = (column & step) != 0
                line = [jnp.where(chosen, line[i - step], line[i]) for i in range(step, len(line))]
                step //= 2
            turned = [jnp.take_along_axis(v, pick, axis=1, mode="promise_in_bounds") for v in line]
            x = [turned[0]] + [jnp.where(low, turned[j - 1], turned[j]) for j in range(1, len(turned))]
            right = [pltpu.roll(v, 1, 1) for v in x[:-1]]
            left = [pltpu.roll(v, LANES - 1, 1) for v in x[1:]]
            for c in range(cols):
                cs = pl.ds(c * LANES, LANES)
                mid = x[c + 1]
                prev = jnp.where(lane == 0, right[c], right[c + 1])
                nxt = jnp.where(lane == LANES - 1, left[c + 1], left[c])
                sh[p, pl.ds(SUB + tile * SUB, SUB), cs] = mid
                out[p, r, cs] = mid + AZIMUTH_COEF * (nxt + prev - 2.0 * mid)
                if tile == 0:
                    eo[0, p, :, cs] = mid[:1]
                if tile == tiles - 1:
                    eo[1, p, :, cs] = mid[SUB - 1:]
            return carry

        lax.fori_loop(p0, p0 + np_, one, 0)

    hops = []

    def scan_send():
        i = len(hops)
        d = 1 << i
        if d < n_rad:
            c = remote(tot_out.at[i], tot_in.at[i], rad_at(d))
            goes = rad + d < n_rad
            pl.when(goes)(c.start)
            chained.append((goes, c))
            hops.append(c)

    def scan_take():
        i = len(hops) - 1
        pl.when(rad >= 1 << i)(hops[i].wait_recv)
        tot_out[i + 1] = tot_out[i] + tot_in[i]

    def send_edge(side, p0, np_):
        ps = pl.ds(p0, np_)
        c = remote(eo.at[side, ps], ei.at[1 - side, ps], rad_at(-1 if side == 0 else 1))
        goes, comes = (inner, outer) if side == 0 else (outer, inner)
        pl.when(goes)(c.start)
        chained.append((goes, c))
        return comes, c

    def edge_wait(edge):
        pl.when(edge[0])(edge[1].wait_recv)

    def place_edges(p0, np_):
        def one(p, carry):
            sh[p, SUB - 1:SUB, :] = jnp.where(rad > 0, ei[0, p], 0.0)
            sh[p, SUB + rows:SUB + rows + 1, :] = jnp.where(rad < n_rad - 1, ei[1, p], 0.0)
            return carry

        lax.fori_loop(p0, p0 + np_, one, 0)

    def smooth(tile, p0, np_):
        top = SUB + tile * SUB

        def one(p, carry):
            r = pl.ds(tile * SUB, SUB)
            mid = sh[p, top:top + SUB, :]
            up = sh[p, top - 1:top + SUB - 1, :]
            down = sh[p, top + 1:top + SUB + 1, :]
            out[p, r, :] = out[p, r, :] + visc[lax.rem(p, 2), r, :] * (down + up - 2.0 * mid)
            return carry

        lax.fori_loop(p0, p0 + np_, one, 0)

    for c in fetches:
        c.start()
    arrive(0)
    for c in fetches:
        c.wait()
    for t in range(tiles):
        shift_tile(t, dust, 2)
    edges = [send_edge(s, dust, 2) for s in (0, 1)]
    for e in edges:
        edge_wait(e)
    place_edges(dust, 2)
    for t in range(tiles):
        smooth(t, dust, 2)

    row = lax.broadcasted_iota(jnp.int32, (SUB, width), 0)
    for h in range(2):
        base = jnp.zeros((1, width), jnp.float32)
        for t in range(tiles):
            r = pl.ds(t * SUB, SUB)
            step = 2.0 * absorb[h, r, :] * out[dust + h, r, :] / total_rows
            run = step
            for k in (1, 2, 4):
                run = run + jnp.where(row >= k, pltpu.roll(run, k, 0), 0.0)
            run = run + base
            depth[h, r, :] = run - 0.5 * step
            base = run[SUB - 1:]
        tot_out[0, h] = base
    scan_send()
    arrive(1)
    shift_tile(0, 0, rest)
    edge_in = send_edge(0, 0, rest)
    scan_take()
    scan_send()
    arrive(2)
    shift_tile(tiles - 1, 0, rest)
    edge_out = send_edge(1, 0, rest)

    scan_take()
    while 1 << len(hops) < n_rad:
        scan_send()
        scan_take()
    for h in range(2):
        carried = tot_in[0, h]
        for i in range(1, len(hops)):
            carried = carried + tot_in[i, h]
        for t in range(tiles):
            r = pl.ds(t * SUB, SUB)
            radius = (rad * rows + t * SUB + row).astype(jnp.float32) + 0.5
            flux = 1.0 / (1.0 + radius / total_rows)
            depth[h, r, :] = depth[h, r, :] + carried
            heat[h, r, :] = flux * jnp.exp(-depth[h, r, :])

    def warm(tile):
        r = pl.ds(tile * SUB, SUB)
        for h in range(2):
            out[rest - 2 + h, r, :] = out[rest - 2 + h, r, :] + heat[h, r, :]

    edge_wait(edge_in)
    edge_wait(edge_out)
    place_edges(0, rest)
    i = 3
    for t in range(1, tiles - 2):
        arrive(i)
        shift_tile(t, 0, rest)
        smooth(t - 1, 0, rest)
        warm(t - 1)
        i += 1
    first = max(tiles - 3, 0)
    for p0, np_ in tail:
        arrive(i)
        shift_tile(tiles - 2, p0, np_)
        for t in range(first, tiles):
            smooth(t, p0, np_)
            if p0 + np_ == rest:
                warm(t)
        i += 1
    for goes, c in chained:
        pl.when(goes)(c.wait_send)
    for c in sent:
        c.wait_send()


def full(n_rad, n_az, state, offsets, viscosity, absorb):
    fields, polar, rows, width = state.shape
    planes = fields * polar
    groups = n_az // 2
    tiles = rows // SUB
    n_tail = len(tail_planes(planes - 2))
    n_pieces = 1 + 2 + max(tiles - 3, 0) + n_tail
    n_scan = (n_rad - 1).bit_length()
    n_local = 1
    n_sems = n_pieces * (2 * (groups - 1) + 1) + 4 + n_scan
    f32 = jnp.float32
    vm = pl.BlockSpec(memory_space=pltpu.VMEM)
    hbm = pl.BlockSpec(memory_space=pl.ANY)
    moved, local = pl.pallas_call(
        functools.partial(kernel, n_rad, n_az, n_local),
        out_shape=(
            pltpu.VMEM((planes, rows, width), f32),
            pltpu.VMEM((polar, rows, width), f32),
        ),
        in_specs=[hbm, pl.BlockSpec(memory_space=pltpu.SMEM), hbm, hbm],
        out_specs=(vm, vm),
        scratch_shapes=[
            pltpu.VMEM((polar, rows, width), f32),
            pltpu.VMEM((polar, rows, width), f32),
            pltpu.VMEM((polar, rows, width), f32),
            pltpu.VMEM((planes, rows, width), f32),
            pltpu.VMEM((n_az - 1, planes, rows, width), f32),
            pltpu.VMEM((planes, rows + 2 * SUB, width), f32),
            pltpu.VMEM((2, planes, 1, width), f32),
            pltpu.VMEM((2, planes, 1, width), f32),
            pltpu.VMEM((n_scan + 1, polar, 1, width), f32),
            pltpu.VMEM((n_scan, polar, 1, width), f32),
            pltpu.SemaphoreType.DMA((n_sems,)),
            pltpu.SemaphoreType.DMA((n_sems,)),
            pltpu.SemaphoreType.DMA((n_local + 2,)),
        ],
        compiler_params=pltpu.CompilerParams(
            collective_id=0, has_side_effects=True, vmem_limit_bytes=56 * 2**20
        ),
    )(state.reshape(planes, rows, width), offsets, viscosity, absorb)
    return moved, local


def fast_kernel(n_rad, n_az, cap, dust_cap, source, offs_in, visc_in, absorb_in, out, depth, flag,
                visc, absorb, heat, gathered, packed, pool_mine, pool_other, early_mine, early_other,
                stage, sh, eo, ei, tot_out, tot_in, take_v, look_v, take, look, offs, ss, rs, ls):
    rad = lax.axis_index("rad")
    az = lax.axis_index("az")
    core = lax.rem(az, 2)
    chip = az // 2
    sibling = {"az": az + 1 - 2 * core}
    across = {"az": lax.rem(az + 2, n_az)}
    planes, rows, width = out.shape
    polar = 2
    fields = planes // polar
    cols = width // LANES
    col_bits = cols.bit_length() - 1
    tiles = rows // SUB
    units = rows * cols
    half = 2 * units
    ring = 2 * cols
    span = cols + 2
    total_rows = rows * n_rad
    dust, energy = fields - 1, fields - 2
    order = [dust, energy] + list(range(energy))
    last = order[-1]
    n_scan = (n_rad - 1).bit_length()
    n_early = 2 * ring
    n_raw = SUB * cols
    raw_at = half + cap
    take_rows = -(-cap // LANES)

    def rad_at(k):
        return {"rad": lax.rem(rad + k + n_rad, n_rad)}

    def rad_pair(i):
        d = 1 << i
        upper = lax.rem(rad // d, 2)
        return {"rad": rad + d - 2 * d * upper}, upper

    count = [0, 0]

    def remote(src, dst, device):
        i = count[0]
        count[0] += 1
        return pltpu.make_async_remote_copy(
            src_ref=src, dst_ref=dst, send_sem=ss.at[i], recv_sem=rs.at[i],
            device_id=device, device_id_type=pl.DeviceIdType.MESH,
        )

    def local(src, dst):
        i = count[1]
        count[1] += 1
        c = pltpu.make_async_copy(src, dst, ls.at[i])
        c.start()
        return c

    offs_copy = local(offs_in, offs)
    inner, outer = rad > 0, rad < n_rad - 1
    barrier = pltpu.get_barrier_semaphore()
    for peer in [rad_pair(i)[0] for i in reversed(range(1, n_scan))]:
        pl.semaphore_signal(barrier, inc=1, device_id=peer, device_id_type=pl.DeviceIdType.MESH)
    for there, k in ((inner, -1), (outer, 1)):
        @pl.when(there)
        def _():
            pl.semaphore_signal(barrier, inc=1, device_id=rad_at(k), device_id_type=pl.DeviceIdType.MESH)
    for peer in [sibling, across]:
        pl.semaphore_signal(barrier, inc=1, device_id=peer, device_id_type=pl.DeviceIdType.MESH)
    for edge, k in ((rad == 0, 0), (rad == n_rad - 1, 1)):
        @pl.when(edge)
        def _():
            ei[k] = jnp.zeros(ei.shape[1:], jnp.float32)

    mine = pl.ds(core * units, units)
    first_pack = [local(source.at[polar * f + core], gathered[f].at[mine]) for f in order[:1]]

    pl.semaphore_wait(barrier, 2 + n_scan - 1 + inner.astype(jnp.int32) + outer.astype(jnp.int32))

    sent, chained = [], []
    to_pack = [remote(source.at[polar * f + 1 - core], gathered[f].at[mine], sibling) for f in order]
    to_mine = [remote(source.at[polar * f + 1 - core], pool_mine[f].at[mine], sibling) for f in order]
    to_other = [remote(source.at[polar * f + core], pool_other[f].at[mine], sibling) for f in order]
    to_early = [
        remote(source.at[polar * last + 1 - core], early_mine.at[mine], sibling),
        remote(source.at[polar * last + core], early_other.at[mine], sibling),
    ]
    sent += to_pack + to_mine + to_other + to_early
    to_pack[0].start()
    raw_mine = remote(
        source.at[polar * dust + core, pl.ds(0, n_raw)],
        pool_mine[dust].at[pl.ds(raw_at + core * n_raw, n_raw)], across,
    )
    raw_other = remote(
        source.at[polar * dust + 1 - core, pl.ds(0, n_raw)],
        pool_other[dust].at[pl.ds(raw_at + core * n_raw, n_raw)], across,
    )
    for c in (raw_mine, raw_other):
        c.start()
        sent.append(c)
    lane = lax.broadcasted_iota(jnp.int32, (SUB, LANES), 1)
    sub = lax.broadcasted_iota(jnp.int32, (SUB, LANES), 0)

    def row_offsets(numbers):
        amount = jnp.full((SUB, LANES), offs[numbers[0]], jnp.int32)
        for k in range(1, len(numbers)):
            amount = jnp.where(sub == k, offs[numbers[k]], amount)
        return amount

    def block_unit(b):
        return (b >> col_bits) * units + (b & (cols - 1)) * SUB

    offs_copy.wait()
    shifts = [row_offsets([t * SUB + k for k in range(SUB)]) for t in range(tiles)]
    leads, manys, befores = [], [], []
    used = jnp.zeros((SUB, LANES), jnp.int32)
    for off in shifts:
        lead = jnp.where(off == 0, ring - 1, jnp.where(off < 2 * width, (2 * width - 1 - off) >> LANE_BITS, 0))
        many = jnp.where(off < 2 * width, ring - lead, jnp.minimum(((4 * width - off) >> LANE_BITS) + 1, ring))
        many = jnp.where(off == 0, 2, many)
        run = many
        for k in (1, 2, 4):
            run = run + jnp.where(sub >= k, pltpu.roll(run, k, 0), 0)
        leads.append(lead)
        manys.append(many)
        befores.append(run - many + used)
        used = used + jnp.broadcast_to(run[SUB - 1:], (SUB, LANES))
    top_many = jnp.broadcast_to(manys[0][:1], (SUB, LANES))
    bottom_many = jnp.broadcast_to(manys[-1][SUB - 1:], (SUB, LANES))
    bases = []
    for t in range(tiles):
        base = befores[t] + bottom_many
        if t == 0:
            base = jnp.where(sub == 0, 0, base)
        if t == tiles - 1:
            base = jnp.where(sub == SUB - 1, top_many, base)
        bases.append(base)
    top_used = befores[1]
    top_used = jnp.broadcast_to(top_used[:1], (SUB, LANES))
    dust_bases = [None] + [before - top_used for before in befores[1:]]
    for size, heads, first, at in ((dust_cap, dust_bases, 1, take_rows), (cap, bases, 0, 0)):
        for q in range(-(-size // LANES)):
            j = q * LANES + lane
            place = jnp.zeros((SUB, LANES), jnp.int32)
            ahead = jnp.zeros((SUB, LANES), jnp.int32)
            for t in range(first, tiles):
                held = (j >= heads[t]) & (j < heads[t] + manys[t])
                place = place + jnp.where(held, t * SUB * cols + sub, 0)
                ahead = ahead + jnp.where(held, leads[t] - heads[t], 0)
            for k in (4, 2, 1):
                place = place + pltpu.roll(place, k, 0)
                ahead = ahead + pltpu.roll(ahead, k, 0)
            take_v[at + q:at + q + 1, :] = (block_unit((j + ahead) & (ring - 1)) + place)[:1]
    take_copy = local(take_v, take)
    for t in range(tiles):
        b = az * cols - (shifts[t] >> LANE_BITS) - 1 + lane + 2 * ring
        near = block_unit(b & (ring - 1)) + (t * SUB * cols + sub)
        here = ((b >> (col_bits + 1)) & 1) == chip
        step = (b - leads[t]) & (ring - 1)
        far = half + jnp.minimum(bases[t] + step, cap - 1)
        look_v[t * SUB:(t + 1) * SUB, :] = jnp.where(here, near, far)
        if t == 0:
            far = raw_at + ((b & (ring - 1)) >> col_bits) * n_raw + (b & (cols - 1)) * SUB + sub
        else:
            far = half + jnp.minimum(dust_bases[t] + step, dust_cap - 1)
        look_v[rows + t * SUB:rows + (t + 1) * SUB, :] = jnp.where(here, near, far)
    look_copy = local(look_v, look)

    crossing = {f: [] for f in order}
    cuts = {f: [0, cap // 2 // SUB * SUB, cap] for f in order}
    cuts[dust] = [0, dust_cap // 4 // SUB * SUB, dust_cap * 5 // 8 // SUB * SUB, dust_cap]
    cuts[last] = [n_early, (n_early + cap) // 2 // SUB * SUB, cap]

    def pack(some, lo, hi):
        def eight(k, carry):
            for s in range(SUB):
                u = take[(k >> 4) + (take_rows if some[0] == dust else 0), (k & 15) * SUB + s]
                for f in some:
                    packed[f][pl.ds(k * SUB + s, 1), :] = gathered[f][pl.ds(u, 1), :]
            return carry

        lax.fori_loop(lo // SUB, hi // SUB, eight, 0)

    def pack_ready(f):
        own_pack[order.index(f)].wait()
        to_pack[order.index(f)].wait_recv()

    def pack_send(f):
        for lo, hi in zip(cuts[f], cuts[f][1:]):
            pack([f], lo, hi)
            c = remote(packed[f].at[pl.ds(lo, hi - lo)], pool_mine[f].at[pl.ds(half + lo, hi - lo)], across)
            c.start()
            sent.append(c)
            crossing[f].append(c)

    def shift_rows(f, numbers, shift, source_ref, slot, write):
        for s, r in enumerate(numbers):
            for i in range(span):
                u = look[r + (rows if f == dust else 0), i]
                stage[slot, i, s:s + 1, :] = source_ref[pl.ds(u, 1), :]
        rem = shift & (LANES - 1)
        pick = (lane - rem) & (LANES - 1)
        low = lane < rem
        turned = [
            jnp.take_along_axis(stage[slot, i], pick, axis=1, mode="promise_in_bounds") for i in range(span)
        ]
        x = [turned[0]] + [jnp.where(low, turned[j - 1], turned[j]) for j in range(1, span)]
        write(x)

    def shift_plane(f, source_ref, p):
        def one(tile):
            r = pl.ds(tile * SUB, SUB)
            below = pl.ds(SUB + tile * SUB, SUB)

            def write(x):
                right = [pltpu.roll(v, 1, 1) for v in x[:-1]]
                left = [pltpu.roll(v, LANES - 1, 1) for v in x[1:]]
                for c in range(cols):
                    cs = pl.ds(c * LANES, LANES)
                    mid = x[c + 1]
                    prev = jnp.where(lane == 0, right[c], right[c + 1])
                    nxt = jnp.where(lane == LANES - 1, left[c + 1], left[c])
                    sh[p, below, cs] = mid
                    out[p, r, cs] = mid + AZIMUTH_COEF * (nxt + prev - 2.0 * mid)

            numbers = [tile * SUB + s for s in range(SUB)]
            shift_rows(f, numbers, row_offsets(numbers), source_ref, tile, write)

        for t in range(tiles):
            one(t)

    def send_edges(f):
        ps = pl.ds(polar * f, polar)
        got = []
        for side in range(2):
            c = remote(eo.at[side, ps], ei.at[1 - side, ps], rad_at(-1 if side == 0 else 1))
            goes, comes = (inner, outer) if side == 0 else (outer, inner)
            pl.when(goes)(c.start)
            chained.append((goes, c))
            got.append((comes, c))
        return got

    def take_edges(f, got):
        for comes, c in got:
            pl.when(comes)(c.wait_recv)
        for h in range(polar):
            p = polar * f + h
            sh[p, SUB - 1:SUB, :] = jnp.where(rad > 0, ei[0, p], 0.0)
            sh[p, SUB + rows:SUB + rows + 1, :] = jnp.where(rad < n_rad - 1, ei[1, p], 0.0)

    def smooth(f, h):
        p = polar * f + h
        for tile in range(tiles):
            top = SUB + tile * SUB
            r = pl.ds(tile * SUB, SUB)
            mid = sh[p, top:top + SUB, :]
            up = sh[p, top - 1:top + SUB - 1, :]
            down = sh[p, top + 1:top + SUB + 1, :]
            new = out[p, r, :] + visc[h, r, :] * (down + up - 2.0 * mid)
            if f == energy:
                new = new + heat[h, r, :]
            out[p, r, :] = new

    def forward(f):
        i = order.index(f)
        onward = []
        for c, lo, hi in zip(crossing[f], cuts[f], cuts[f][1:]):
            c.wait_recv()
            at = pl.ds(half + lo, hi - lo)
            c = remote(pool_mine[f].at[at], pool_other[f].at[at], sibling)
            c.start()
            sent.append(c)
            onward.append(c)
        own_mine[i].wait()
        to_mine[i].wait_recv()
        return onward

    def other_ready(f, onward):
        i = order.index(f)
        own_other[i].wait()
        to_other[i].wait_recv()
        for c in onward:
            c.wait_recv()

    def work(f):
        onward = forward(f)
        shift_plane(f, pool_mine[f], polar * f + core)
        other_ready(f, onward)
        shift_plane(f, pool_other[f], polar * f + 1 - core)
        for h in range(polar):
            p = polar * f + h
            eo[0, p] = sh[p, SUB:SUB + 1, :]
            eo[1, p] = sh[p, SUB + rows - 1:SUB + rows, :]
        return send_edges(f)

    def finish(f, got):
        take_edges(f, got)
        for h in range(polar):
            smooth(f, h)

    def flush(but=()):
        for goes, c in chained:
            pl.when(goes)(c.wait_send)
        for c in sent:
            if not any(c is b for b in but):
                c.wait_send()
        sent[:] = but
        chained.clear()

    early_at = pl.ds(half, n_early)

    def early_edges():
        crossing_early.wait_recv()
        onward = remote(early_mine.at[early_at], early_other.at[early_at], sibling)
        onward.start()
        sent.append(onward)
        numbers = [0, rows - 1]
        for c in own_early:
            c.wait()
        for c in to_early:
            c.wait_recv()
        copies = [local(early_mine.at[early_at], pool_mine[last].at[early_at])]
        for ref, hh in ((early_mine, core), (early_other, 1 - core)):
            p = polar * last + hh
            if ref is early_other:
                onward.wait_recv()
                copies.append(local(early_other.at[early_at], pool_other[last].at[early_at]))

            def write(x):
                for c in range(cols):
                    cs = pl.ds(c * LANES, LANES)
                    eo[0, p, :, cs] = x[c + 1][:1]
                    eo[1, p, :, cs] = x[c + 1][1:2]

            shift_rows(last, numbers, row_offsets(numbers), ref, 0, write)
        got = send_edges(last)
        for c in copies:
            c.wait()
        return got

    own_pack = first_pack
    take_copy.wait()
    to_pack[1].start()
    pack_ready(dust)
    pack_send(dust)
    own_pack = first_pack + [local(source.at[polar * f + core], gathered[f].at[mine]) for f in order[1:]]
    for c in to_pack[2:]:
        c.start()
    look_copy.wait()
    pack_ready(energy)
    pack_send(energy)
    raw_here = pl.ds(raw_at + core * n_raw, n_raw)
    raw_onward = []
    for c, src, dst in ((raw_mine, pool_mine, pool_other), (raw_other, pool_other, pool_mine)):
        c.wait_recv()
        c = remote(src[dust].at[raw_here], dst[dust].at[raw_here], sibling)
        c.start()
        sent.append(c)
        raw_onward.append(c)
    own_mine, own_other = [], []

    def fill_pools(i):
        f = order[i]
        to_mine[i].start()
        to_other[i].start()
        own_mine.append(local(source.at[polar * f + core], pool_mine[f].at[mine]))
        own_other.append(local(source.at[polar * f + 1 - core], pool_other[f].at[mine]))

    fill_pools(0)
    params = [local(visc_in, visc), local(absorb_in, absorb)]
    pack_ready(last)
    pack([last], 0, n_early)
    crossing_early = remote(packed[last].at[pl.ds(0, n_early)], early_mine.at[early_at], across)
    crossing_early.start()
    sent.append(crossing_early)
    for i in range(2, fields - 1):
        pack_ready(order[i])
        pack_send(order[i])
        fill_pools(i - 1)
    own_early = [
        local(source.at[polar * last + core], early_mine.at[mine]),
        local(source.at[polar * last + 1 - core], early_other.at[mine]),
    ]
    for c in to_early:
        c.start()
    pack_send(last)
    for i in range(fields - 2, fields):
        fill_pools(i)
    for c in params:
        c.wait()

    for c in raw_onward:
        c.wait_recv()
    finish(dust, work(dust))

    row = lax.broadcasted_iota(jnp.int32, (SUB, width), 0)
    for h in range(polar):
        run_last = jnp.zeros((1, width), jnp.float32)
        for t in range(tiles):
            r = pl.ds(t * SUB, SUB)
            step = 2.0 * absorb[h, r, :] * out[polar * dust + h, r, :] / total_rows
            run = step
            for k in (1, 2, 4):
                run = run + jnp.where(row >= k, pltpu.roll(run, k, 0), 0.0)
            run = run + run_last
            depth[h, r, :] = run - 0.5 * step
            run_last = run[SUB - 1:]
        tot_out[0, h] = run_last
    over = ((used > cap) | (used - top_used > dust_cap)).astype(jnp.float32)[:1]
    for c in range(cols):
        tot_out[0, polar, :, pl.ds(c * LANES, LANES)] = over

    hops = []

    def scan_send():
        i = len(hops)
        peer, upper = rad_pair(i)
        c = remote(tot_out.at[i], tot_in.at[i], peer)
        c.start()
        sent.append(c)
        hops.append((c, upper))

    def scan_take():
        i = len(hops) - 1
        hops[i][0].wait_recv()
        tot_out[i + 1] = tot_out[i] + tot_in[i]

    def irradiate():
        for h in range(polar):
            carried = jnp.where(hops[0][1] == 1, tot_in[0, h], 0.0)
            for i in range(1, n_scan):
                carried = carried + jnp.where(hops[i][1] == 1, tot_in[i, h], 0.0)
            for t in range(tiles):
                r = pl.ds(t * SUB, SUB)
                radius = (rad * rows + t * SUB + row).astype(jnp.float32) + 0.5
                flux = 1.0 / (1.0 + radius / total_rows)
                depth[h, r, :] = depth[h, r, :] + carried
                heat[h, r, :] = flux * jnp.exp(-depth[h, r, :])
        flag[0] = jnp.max(tot_out[n_scan, polar])

    scan_send()
    pending = []
    for f in order[1:-1]:
        if f == order[3]:
            last_edges = early_edges()
        pending.append((f, work(f)))
        if len(hops) < n_scan:
            scan_take()
            scan_send()
            ready = [w for w in pending[:-1] if w[0] != energy]
        else:
            if energy in [w[0] for w in pending]:
                scan_take()
                irradiate()
            ready = pending[:-1]
        for w in ready:
            finish(*w)
            pending.remove(w)
    take_edges(last, last_edges)
    flush(crossing[last])
    onward = forward(last)
    shift_plane(last, pool_mine[last], polar * last + core)
    smooth(last, core)
    other_ready(last, onward)
    shift_plane(last, pool_other[last], polar * last + 1 - core)
    smooth(last, 1 - core)
    for w in pending:
        finish(*w)
    flush()


def fast(n_rad, n_az, state, offsets, viscosity, absorb):
    fields, polar, rows, width = state.shape
    planes = fields * polar
    cols = width // LANES
    units = rows * cols
    cap = units * 2 * 11 // 16 // 16 * 16
    dust_cap = (units - SUB * cols) * 2 * 73 // 100 // SUB * SUB
    n_early = 4 * cols
    n_take = -(-(-(-cap // LANES) - (-dust_cap // LANES)) // SUB) * SUB
    n_scan = (n_rad - 1).bit_length()
    n_sems = 9 * fields + 2 + 4 + 4 + n_scan
    pools = [2 * units + cap] * (fields - 1) + [2 * units + cap + 2 * SUB * cols]
    f32, i32 = jnp.float32, jnp.int32
    vm = pl.BlockSpec(memory_space=pltpu.VMEM)
    hbm = pl.BlockSpec(memory_space=pl.ANY)
    source = state.reshape(planes, rows // SUB, SUB, cols, LANES).transpose(0, 1, 3, 2, 4).reshape(planes, units, LANES)
    moved, local, flag = pl.pallas_call(
        functools.partial(fast_kernel, n_rad, n_az, cap, dust_cap),
        out_shape=(
            pltpu.VMEM((planes, rows, width), f32),
            pltpu.VMEM((polar, rows, width), f32),
            pltpu.SMEM((1,), f32),
        ),
        in_specs=[hbm, hbm, hbm, hbm],
        out_specs=(vm, vm, pl.BlockSpec(memory_space=pltpu.SMEM)),
        scratch_shapes=[
            pltpu.VMEM((polar, rows, width), f32),
            pltpu.VMEM((polar, rows, width), f32),
            pltpu.VMEM((polar, rows, width), f32),
            [pltpu.VMEM((2 * units, LANES), f32)] * fields,
            [pltpu.VMEM((cap, LANES), f32)] * fields,
            [pltpu.VMEM((n, LANES), f32) for n in pools],
            [pltpu.VMEM((n, LANES), f32) for n in pools],
            pltpu.VMEM((2 * units + n_early, LANES), f32),
            pltpu.VMEM((2 * units + n_early, LANES), f32),
            pltpu.VMEM((rows // SUB, cols + 2, SUB, LANES), f32),
            pltpu.VMEM((planes, rows + 2 * SUB, width), f32),
            pltpu.VMEM((2, planes, 1, width), f32),
            pltpu.VMEM((2, planes, 1, width), f32),
            pltpu.VMEM((n_scan + 1, polar + 1, 1, width), f32),
            pltpu.VMEM((n_scan, polar + 1, 1, width), f32),
            pltpu.VMEM((n_take, LANES), i32),
            pltpu.VMEM((2 * rows, LANES), i32),
            pltpu.SMEM((n_take, LANES), i32),
            pltpu.SMEM((2 * rows, LANES), i32),
            pltpu.SMEM((rows,), i32),
            pltpu.SemaphoreType.DMA((n_sems,)),
            pltpu.SemaphoreType.DMA((n_sems,)),
            pltpu.SemaphoreType.DMA((3 * fields + 10,)),
        ],
        compiler_params=pltpu.CompilerParams(
            collective_id=1, has_side_effects=True, vmem_limit_bytes=61 * 2**20
        ),
    )(source, offsets, viscosity, absorb)
    return moved, local, flag[0]


def hand_out(moved, local):
    def store(a, b, x, y, sems):
        copies = [pltpu.make_async_copy(a, x, sems.at[0]), pltpu.make_async_copy(b, y, sems.at[1])]
        for c in copies:
            c.start()
        for c in copies:
            c.wait()

    hbm = pl.BlockSpec(memory_space=pl.ANY)
    vm = pl.BlockSpec(memory_space=pltpu.VMEM)
    return pl.pallas_call(
        store,
        out_shape=(pltpu.HBM(moved.shape, moved.dtype), pltpu.HBM(local.shape, local.dtype)),
        in_specs=[vm, vm],
        out_specs=(hbm, hbm),
        scratch_shapes=[pltpu.SemaphoreType.DMA((2,))],
    )(moved, local)


def body(n_rad, n_az, state, offsets, viscosity, absorb):
    args = (state, offsets, viscosity, absorb)
    if n_az != 4 or state.shape[1] != 2 or n_rad not in (2, 4, 8, 16):
        moved, local = full(n_rad, n_az, *args)
    else:
        moved, local, flag = fast(n_rad, n_az, *args)
        moved, local = lax.cond(
            flag > 0, lambda m, d: tuple(full(n_rad, n_az, *args)), lambda m, d: (m, d), moved, local
        )
    moved, local = hand_out(moved, local)
    return moved.reshape(state.shape), local


def solution(mesh):
    in_specs = (P(None, None, "rad", "az"), P("rad"), P(None, "rad", "az"), P(None, "rad", "az"))
    out_specs = (P(None, None, "rad", "az"), P(None, "rad", "az"))
    f = functools.partial(body, mesh.shape["rad"], mesh.shape["az"])
    return jax.shard_map(f, mesh=mesh, in_specs=in_specs, out_specs=out_specs, check_vma=False)
```
